32 devices in a mesh: grp: 8 (over z, core), voc: 4 (over y, x).
Axes of the slice: x: 2, y: 2, z: 4, core: 2. Of those that a mesh axis runs over, the one named last changes fastest.
Arguments:
- student_hidden: bfloat16 [192, 4096], P('grp', 'voc')
- norm_gain: float32 [4096], P('voc'), may hold values from 0.5 to 1.5
- teacher_hidden: bfloat16 [192, 5120], P('grp', 'voc')
- student_head: bfloat16 [4096, 12288], P(None, ('grp', 'voc'))
- teacher_head: bfloat16 [5120, 12288], P(None, ('grp', 'voc'))
- episode_source: int32 [96], replicated, may hold values from 0 to 95, as said below
- lengths: int32 [96], replicated, may hold values from 1 to 2, 120 in all
Outputs:
- loss: float32 [], replicated
- grad_hidden: bfloat16 [192, 4096], P('grp', 'voc')
- grad_gain: float32 [4096], P('voc')
- grad_head: bfloat16 [4096, 12288], P(None, ('grp', 'voc'))
The draws below stay inside these ranges and needn't reach their ends.
Inputs may be any that keep to these rules, and one draw needn't show every extreme that they name: `episode_source`: A permutation of the episodes. Student episodes 12 * s to 12 * s + 11 form group s, teacher episodes likewise form teacher group t; at most 2 episodes of one student group come from one teacher group, and that many in some pair.
All inputs are finite; a program needn't handle non-finite values.
Results may differ from the reference program's by a relative error of at most 0.04.
Values may be sent and summed in bfloat16 or wider, within the bound.
A program may use at most 64 MiB of HBM per device.

```python
import math
import jax
import jax.numpy as jnp
import numpy as np
from jax import lax

DS = 4096
DT = 5120
VOC_DEV = 384
EP_GRP = 12
SEQ = 2
EPISODES = 96
TOKENS = 192
VOCAB = 12288
N_GRP = 8
N_VOC = 4


def student_base(key):
    return jax.random.normal(jax.random.fold_in(key, 101), (TOKENS, DS), jnp.float32)


def teacher_base(key):
    return jax.random.normal(jax.random.fold_in(key, 202), (TOKENS, DT), jnp.float32)


def column_ramp(ratio):
    steps = jnp.arange(DS, dtype=jnp.float32) / (DS - 1)
    return jnp.exp(steps * math.log(ratio))[None, :]


def draw_student_hidden(key, part):
    base_rows = student_base(key)
    base_rows = base_rows * column_ramp(5.0)
    return base_rows.astype(jnp.bfloat16)


def draw_student_head(key, part):
    key = jax.random.fold_in(key, 5)
    weights = jax.random.normal(key, (DS, VOCAB), jnp.float32) * (3.0 / math.sqrt(DS))
    return weights.astype(jnp.bfloat16)


def draw_teacher_hidden(key, part):
    base_rows = teacher_base(key)
    return base_rows.astype(jnp.bfloat16)


def draw_teacher_head(key, part):
    key = jax.random.fold_in(key, 8)
    weights = jax.random.normal(key, (DT, VOCAB), jnp.float32) * (3.0 / math.sqrt(DT))
    return weights.astype(jnp.bfloat16)


def draw_episode_source(key, part):
    key = jax.random.fold_in(key, 7)
    ranks = jax.random.permutation(jax.random.fold_in(key, 1), N_GRP).astype(jnp.int32)
    offset_ids = jnp.arange(N_GRP, dtype=jnp.int32)
    priority = jnp.where(offset_ids == N_GRP // 2, -2 * N_GRP, jnp.where(offset_ids == N_GRP - 1, -N_GRP, 0)).astype(jnp.int32)
    first = jnp.argsort(ranks + priority).astype(jnp.int32)
    offsets = jnp.concatenate([first[:1], first, first[1:]])[:EP_GRP]
    group_keys = jax.random.split(jax.random.fold_in(key, 2), N_GRP)
    orders = jax.vmap(lambda single: jax.random.permutation(single, EP_GRP))(group_keys)
    shifted = jnp.take(offsets, orders.astype(jnp.int32), axis=0)
    group_ids = jnp.arange(N_GRP, dtype=jnp.int32)[:, None]
    target = (group_ids + shifted) % N_GRP
    ranking = jax.random.permutation(jax.random.fold_in(key, 3), EPISODES).astype(jnp.int32)
    scores = target.reshape(-1) * EPISODES + ranking
    ordering = jnp.argsort(scores)
    source = jnp.zeros((EPISODES,), jnp.int32).at[ordering].set(jnp.arange(EPISODES, dtype=jnp.int32))
    return source


def split_up(number_of, total, most, skew):
    weights = [(1 << 20) // math.isqrt(grade ** skew) + 1 for grade in range(2, number_of + 1)]
    spare, given = total - most - (number_of - 1), [1] * (number_of - 1)
    while spare > 0:
        candidates = [i for i in range(number_of - 1) if given[i] < most]
        pool, remaining = sum([weights[i] for i in candidates]), spare
        for i in candidates:
            more = min(most - given[i], max(1, remaining * weights[i] // pool), spare)
            given[i] = given[i] + more
            spare = spare - more
    return np.array([most] + given)


def ragged_sizes(own_key, number_of, total, limit, skew):
    if number_of == 2:
        one = jax.random.randint(own_key, (), max(1, total - limit), min(limit, total - 1) + 1)
        return jnp.stack([one, total - one])
    sizes = jnp.asarray(split_up(number_of, total, limit, skew), jnp.int32)
    twos = (number_of - 1) // 2
    source_of, taker = sizes[1:1 + 2 * twos:2], sizes[2:2 + 2 * twos:2]
    margin = jnp.minimum(source_of - 1, limit - taker)
    moved = jax.random.randint(jax.random.fold_in(own_key, 1), (twos,), 0, 1 << 20) % (margin + 1)
    sizes = sizes.at[1:1 + 2 * twos:2].set(source_of - moved).at[2:2 + 2 * twos:2].set(taker + moved)
    return sizes[jax.random.permutation(jax.random.fold_in(own_key, 2), number_of)]


def setup_inputs(seed: int = 0) -> dict:
    streams_of = jax.random.split(jax.random.key(seed), 8)
    student_hidden = draw_student_hidden(jax.random.fold_in(streams_of[7], 71), 0)
    norm_gain = jnp.clip(1.0 + 0.1 * jax.random.normal(streams_of[1], (DS,), jnp.float32), 0.5, 1.5)
    teacher_hidden = draw_teacher_hidden(jax.random.fold_in(streams_of[7], 71), 0)
    student_head = draw_student_head(jax.random.fold_in(streams_of[7], 71), 0)
    teacher_head = draw_teacher_head(jax.random.fold_in(streams_of[7], 71), 0)
    episode_source = draw_episode_source(jax.random.fold_in(streams_of[7], 71), 0)
    lengths = ragged_sizes(streams_of[6], EPISODES, EPISODES * SEQ * 5 // 8, SEQ, 2).astype(jnp.int32)
    return dict(student_hidden=student_hidden, norm_gain=norm_gain, teacher_hidden=teacher_hidden, student_head=student_head, teacher_head=teacher_head, episode_source=episode_source, lengths=lengths)


EPSILON = 1e-06

def reference(student_hidden, norm_gain, teacher_hidden, student_head, teacher_head, episode_source, lengths):
    hidden_f32 = student_hidden.astype(jnp.float32)
    inverse_rms = lax.rsqrt(lax.optimization_barrier(jnp.mean(hidden_f32 * hidden_f32, axis=1)) + EPSILON)
    normed = (hidden_f32 * inverse_rms[:, None] * norm_gain[None, :]).astype(jnp.bfloat16)
    positions = jnp.arange(SEQ, dtype=jnp.int32)
    token_order = (episode_source[:, None] * SEQ + positions[None, :]).reshape(-1).astype(jnp.int32)
    teacher_rows = jnp.take(teacher_hidden, token_order, axis=0)
    student_logits = jnp.dot(normed, student_head, preferred_element_type=jnp.float32)
    teacher_logits = jnp.dot(teacher_rows, teacher_head, preferred_element_type=jnp.float32)
    log_student = jax.nn.log_softmax(student_logits, axis=1)
    log_teacher = jax.nn.log_softmax(teacher_logits, axis=1)
    prob_student = jnp.exp(log_student)
    log_ratio = log_student - log_teacher
    divergence = lax.optimization_barrier(jnp.sum(prob_student * log_ratio, axis=1))
    lengths_f32 = lengths.astype(jnp.float32)
    valid = positions[None, :] < lengths[:, None]
    token_weight = jnp.where(valid, 1.0 / lengths_f32[:, None], jnp.zeros_like(lengths_f32)[:, None]).reshape(-1)
    loss = jnp.sum(token_weight * divergence)
    logit_grad = (token_weight[:, None] * prob_student * (log_ratio - divergence[:, None])).astype(jnp.bfloat16)
    blocks = N_GRP * N_VOC
    grad_blocks = logit_grad.reshape(TOKENS, blocks, VOC_DEV).transpose(1, 0, 2)
    normed_t = normed.T

    def head_block(block):
        return jnp.dot(normed_t, block, preferred_element_type=jnp.float32).astype(jnp.bfloat16)
    grad_head = lax.map(head_block, grad_blocks).transpose(1, 0, 2).reshape(DS, VOCAB)
    normed_grad = jnp.dot(logit_grad, student_head.T, preferred_element_type=jnp.float32)
    grad_gain = lax.optimization_barrier(jnp.sum(normed_grad * hidden_f32 * inverse_rms[:, None], axis=0))
    scaled = normed_grad * norm_gain[None, :]
    inner = lax.optimization_barrier(jnp.sum(scaled * hidden_f32, axis=1))
    grad_hidden = inverse_rms[:, None] * scaled - hidden_f32 * (inverse_rms ** 3)[:, None] * inner[:, None] / DS
    return (loss, grad_hidden.astype(jnp.bfloat16), grad_gain, grad_head)
```

```python
import functools

import jax
import jax.numpy as jnp
from jax import lax
from jax.experimental import pallas as pl
from jax.experimental.pallas import tpu as pltpu
from jax.sharding import PartitionSpec as P

DS = 4096
SEQ = 2
MOST = 2


EPSILON = 1e-06

F32 = jnp.float32
BF16 = jnp.bfloat16
MESH = pl.DeviceIdType.MESH


def flip(number, mask):
    low, high = number % 2, number // 2
    if mask & 1:
        low = 1 - low
    if mask & 2:
        high = 1 - high
    return high * 2 + low


def merge(parts):
    top = functools.reduce(jnp.maximum, [p[0:1] for p in parts])
    top_t = functools.reduce(jnp.maximum, [p[2:3] for p in parts])
    total = total_t = ratio = logit = both = 0.0
    for p in parts:
        shift, shift_t = p[0:1] - top, p[2:3] - top_t
        factor, factor_t = jnp.exp(shift), jnp.exp(shift_t)
        live = factor > 0.0
        shift = jnp.where(live, shift, 0.0)
        gap = shift - jnp.where(live, shift_t, 0.0)
        total = total + factor * p[1:2]
        total_t = total_t + factor_t * p[3:4]
        ratio = ratio + factor * (p[4:5] + p[1:2] * gap)
        logit = logit + factor * (p[5:6] + p[1:2] * shift)
        both = both + factor * (p[6:7] + gap * p[5:6] + shift * p[4:5] + shift * gap * p[1:2])
    return jnp.concatenate([top, total, top_t, total_t, ratio, logit, both, jnp.zeros_like(top)], axis=0)


def kernel(
    sh_ref, th_ref, gain_ref, order_ref, weight_ref, w_hbm, t_hbm,
    loss_ref, gh_ref, gg_ref, head_hbm,
    wv, tv, sx, tx, in_s, in_t, s_blk, t_blk, hg, s_acc, t_acc, sq, cols,
    st_a, st_b, g2, own, p_sib, r_sib, p_x, r_x, rb, rz, gp, gz, head,
    w_sem, t_sem, h_sem, s1s, s1r, t1s, t1r, s2s, s2r, t2s, t2r, as_, ar, bs, br,
    qs, qr, xs, xr, zs, zr, ys, yr,
):
    g = lax.axis_index("grp")
    v = lax.axis_index("voc")
    z, c = g // 2, g % 2
    k = v * 2 + c
    rows, half_s = in_s.shape[1], in_s.shape[2]
    half_t = in_t.shape[2]
    tokens = s_acc.shape[0]

    def plane(vm, cm):
        return {"grp": z * 2 + (1 - c if cm else c), "voc": flip(v, vm)}

    def column(zm, cm):
        return {"grp": flip(z, zm) * 2 + (1 - c if cm else c), "voc": v}

    def slot(vm, cm):
        return flip(v, vm) * 2 + (1 - c if cm else c)

    sends = []

    def send(src, dst, ssem, rsem, to):
        copy = pltpu.make_async_remote_copy(
            src_ref=src, dst_ref=dst, send_sem=ssem, recv_sem=rsem, device_id=to, device_id_type=MESH
        )
        copy.start()
        sends.append(copy)

    def arrived(dst, ssem, rsem, to):
        pltpu.make_async_remote_copy(
            src_ref=dst, dst_ref=dst, send_sem=ssem, recv_sem=rsem, device_id=to, device_id_type=MESH
        ).wait_recv()

    w_copy = pltpu.make_async_copy(w_hbm, wv, w_sem)
    t_copy = pltpu.make_async_copy(t_hbm, tv, t_sem)
    w_copy.start()
    t_copy.start()

    barrier = pltpu.get_barrier_semaphore()
    peers = [plane(m // 2, m % 2) for m in range(1, 8)] + [column(m // 2, m % 2) for m in range(2, 8)]
    for peer in peers:
        pl.semaphore_signal(barrier, inc=1, device_id=peer, device_id_type=MESH)
    for h in range(2):
        sx[h] = sh_ref[:, h * half_s:(h + 1) * half_s]
        tx[h] = th_ref[:, h * half_t:(h + 1) * half_t]
    pl.semaphore_wait(barrier, len(peers))

    for m in range(1, 8):
        other = 1 - c if m % 2 else c
        send(sx.at[other], in_s.at[g], s1s.at[m], s1r.at[m], column(m // 2, m % 2))
    for m in range(1, 8):
        other = 1 - c if m % 2 else c
        send(tx.at[other], in_t.at[g], t1s.at[m], t1r.at[m], column(m // 2, m % 2))
    in_s[g] = sx[c]
    in_t[g] = tx[c]
    gain = gain_ref[...]
    own_gain = jnp.where(c == 0, gain[:, :half_s], gain[:, half_s:])
    hi = own_gain.astype(BF16).astype(F32)
    mid = (own_gain - hi).astype(BF16).astype(F32)
    lo = own_gain - hi - mid
    line = lax.broadcasted_iota(jnp.int32, (16, half_s), 0)
    gain_rows = jnp.where(line == 0, hi, jnp.where(line == 1, mid, jnp.where(line == 2, lo, 0.0)))
    s_blk[k, tokens:, :] = gain_rows.astype(BF16)

    def source(m):
        return flip(z, m // 2) * 2 + (1 - c if m % 2 else c)

    for m in range(1, 8):
        arrived(in_s.at[source(m)], s1s.at[m], s1r.at[m], column(m // 2, m % 2))
    s_blk[k, :tokens, :] = jnp.concatenate([in_s[i].astype(F32) for i in range(8)], axis=0).astype(BF16)
    for vm in (1, 2, 3):
        send(s_blk.at[k], s_blk.at[k], s2s.at[vm * 2], s2r.at[vm * 2], plane(vm, 0))
    send(s_blk.at[k], s_blk.at[k], s2s.at[1], s2r.at[1], plane(0, 1))
    for m in range(1, 8):
        arrived(in_t.at[source(m)], t1s.at[m], t1r.at[m], column(m // 2, m % 2))
    t_blk[k] = jnp.concatenate([in_t[i].astype(F32) for i in range(8)], axis=0).astype(BF16)
    for vm in (1, 2, 3):
        send(t_blk.at[k], t_blk.at[k], t2s.at[vm * 2], t2r.at[vm * 2], plane(vm, 0))
    send(t_blk.at[k], t_blk.at[k], t2s.at[1], t2r.at[1], plane(0, 1))

    s_acc[...] = jnp.zeros_like(s_acc)
    t_acc[...] = jnp.zeros_like(t_acc)
    sq[...] = jnp.zeros_like(sq)
    w_copy.wait()

    def student_block(at):
        x = s_blk[at, :tokens, :].astype(F32)
        tail = s_blk[at, tokens:, :].astype(F32)
        scale = jnp.sum(tail, axis=0, keepdims=True)
        squares = x * x
        partial = squares[:, 0:128]
        for i in range(1, half_s // 128):
            partial = partial + squares[:, i * 128:(i + 1) * 128]
        sq[...] += partial
        scaled = (x * scale).astype(BF16)
        hg[at] = scaled
        s_acc[...] += jnp.dot(scaled, wv[at], preferred_element_type=F32)

    def teacher_block(at):
        t_acc[...] += jnp.dot(t_blk[at], tv[at], preferred_element_type=F32)

    def relay(blk, ssem, rsem, vm):
        at = slot(vm, 0)
        arrived(blk.at[at], ssem.at[vm * 2], rsem.at[vm * 2], plane(vm, 0))
        send(blk.at[at], blk.at[at], ssem.at[vm * 2 + 1], rsem.at[vm * 2 + 1], plane(0, 1))

    def sibling(blk, ssem, rsem, vm):
        arrived(blk.at[slot(vm, 1)], ssem.at[vm * 2 + 1], rsem.at[vm * 2 + 1], plane(0, 1))

    student_block(k)
    t_copy.wait()
    teacher_block(k)
    sibling(s_blk, s2s, s2r, 0)
    student_block(slot(0, 1))
    sibling(t_blk, t2s, t2r, 0)
    teacher_block(slot(0, 1))
    for vm in (1, 2, 3):
        relay(s_blk, s2s, s2r, vm)
        student_block(slot(vm, 0))
        sibling(s_blk, s2s, s2r, vm)
        student_block(slot(vm, 1))
    for vm in (1, 2, 3):
        relay(t_blk, t2s, t2r, vm)
        teacher_block(slot(vm, 0))
        sibling(t_blk, t2s, t2r, vm)
        teacher_block(slot(vm, 1))

    inv = lax.rsqrt(jnp.sum(sq[...], axis=1, keepdims=True) / DS + EPSILON)
    s_log = s_acc[...] * inv
    raw = t_acc[...]
    pick = (order_ref[...] == lax.broadcasted_iota(jnp.int32, (tokens, tokens), 1)).astype(F32).astype(BF16)
    part0 = raw.astype(BF16)
    rest = raw - part0.astype(F32)
    part1 = rest.astype(BF16)
    part2 = (rest - part1.astype(F32)).astype(BF16)
    t_log = (
        jnp.dot(pick, part0, preferred_element_type=F32)
        + jnp.dot(pick, part1, preferred_element_type=F32)
        + jnp.dot(pick, part2, preferred_element_type=F32)
    )
    top = jnp.max(s_log, axis=1, keepdims=True)
    top_t = jnp.max(t_log, axis=1, keepdims=True)
    a = s_log - top
    b = t_log - top_t
    e = jnp.exp(a)
    ea = e * a
    d = a - b
    figures = [
        top, jnp.sum(e, axis=1, keepdims=True), top_t, jnp.sum(jnp.exp(b), axis=1, keepdims=True),
        jnp.sum(e * d, axis=1, keepdims=True), jnp.sum(ea, axis=1, keepdims=True),
        jnp.sum(ea * d, axis=1, keepdims=True),
    ]
    lane = lax.broadcasted_iota(jnp.int32, (tokens, 128), 1)
    packed = jnp.zeros((tokens, 128), F32)
    for i, figure in enumerate(figures):
        packed = jnp.where(lane == i, figure, packed)
    packed = jnp.concatenate([packed, jnp.zeros((256 - tokens, 128), F32)], axis=0)
    st_a[k] = jnp.transpose(packed)[0:8, :]
    for m in range(1, 8):
        send(st_a.at[k], st_a.at[k], as_.at[m], ar.at[m], plane(m // 2, m % 2))
    for m in range(1, 8):
        arrived(st_a.at[slot(m // 2, m % 2)], as_.at[m], ar.at[m], plane(m // 2, m % 2))
    st_b[z] = merge([st_a[i] for i in range(8)])
    for m in range(1, 4):
        send(st_b.at[z], st_b.at[z], bs.at[m], br.at[m], column(m, 0))
    for m in range(1, 4):
        arrived(st_b.at[flip(z, m)], bs.at[m], br.at[m], column(m, 0))
    full = merge([st_b[i] for i in range(4)])
    total = full[1:2]
    lse = full[0:1] + jnp.log(total)
    lse_t = full[2:3] + jnp.log(full[3:4])
    mean_ratio, mean_logit = full[4:5] / total, full[5:6] / total
    divergence = mean_ratio - jnp.log(total) + jnp.log(full[3:4])
    offset = lse - lse_t + divergence
    cov = full[6:7] / total - mean_ratio * mean_logit
    back = jnp.concatenate([lse, offset, divergence, cov, jnp.zeros((124, 256), F32)], axis=0)
    back = jnp.transpose(back)[:tokens]
    weight = weight_ref[...]
    loss_ref[...] = jnp.sum(weight * back[:, 2:3], axis=0, keepdims=True)
    prob = jnp.exp(s_log - back[:, 0:1])
    grad = ((weight * inv) * prob * (s_log - t_log - back[:, 1:2])).astype(BF16)
    g2[...] = grad
    lane = lax.broadcasted_iota(jnp.int32, (tokens, 128), 1)
    cols[...] = jnp.where(lane == 0, weight * inv * inv * back[:, 3:4] / DS, 0.0)

    def block_grad(at):
        return lax.dot_general(g2[...], wv[at], (((1,), (1,)), ((), ())), preferred_element_type=F32)

    order = (1, 2, 3, 0)
    for vm in order:
        p_sib[vm] = block_grad(slot(vm, 1)).astype(BF16)
        send(p_sib.at[vm], r_sib.at[vm], qs.at[vm], qr.at[vm], plane(0, 1))
    for vm in order:
        mine = block_grad(slot(vm, 0))
        arrived(r_sib.at[vm], qs.at[vm], qr.at[vm], plane(0, 1))
        mine = mine + r_sib[vm].astype(F32)
        if vm:
            p_x[vm] = mine.astype(BF16)
            send(p_x.at[vm], r_x.at[vm], xs.at[vm], xr.at[vm], plane(vm, 0))
        else:
            own[...] = mine

    head_copies = []
    for i in range(8):
        head[i] = lax.dot_general(
            hg[i], g2[...], (((0,), (0,)), ((), ())), preferred_element_type=F32
        ).astype(BF16)
        copy = pltpu.make_async_copy(head.at[i], head_hbm.at[i], h_sem.at[i])
        copy.start()
        head_copies.append(copy)

    for vm in (1, 2, 3):
        arrived(r_x.at[vm], xs.at[vm], xr.at[vm], plane(vm, 0))
    total = own[...]
    for vm in (1, 2, 3):
        total = total + r_x[vm].astype(F32)
    for i in range(8):
        rb[i] = total[i * rows:(i + 1) * rows].astype(BF16)
    for m in range(1, 8):
        send(rb.at[source(m)], rz.at[g], zs.at[m], zr.at[m], column(m // 2, m % 2))
    rz[g] = rb[g]
    prod = total * s_blk[k, :tokens, :].astype(F32)
    part = prod[0:8]
    for i in range(1, tokens // 8):
        part = part + prod[i * 8:(i + 1) * 8]
    gp[...] = part
    for m in range(1, 8):
        send(gp, gz.at[g], ys.at[m], yr.at[m], column(m // 2, m % 2))
    gz[g] = part
    for m in range(1, 8):
        arrived(rz.at[source(m)], zs.at[m], zr.at[m], column(m // 2, m % 2))
    own_cols = cols[pl.ds(pl.multiple_of(g * rows, 8), rows), :][:, 0:1]
    for h in range(2):
        at = slice(h * half_s, (h + 1) * half_s)
        ng = rz[h].astype(F32)
        for i in range(1, 4):
            ng = ng + rz[2 * i + h].astype(F32)
        hid = sh_ref[:, at].astype(F32)
        gh_ref[:, at] = (gain_ref[:, at] * ng - hid * own_cols).astype(BF16)
    for m in range(1, 8):
        arrived(gz.at[source(m)], ys.at[m], yr.at[m], column(m // 2, m % 2))
    for h in range(2):
        at = slice(h * half_s, (h + 1) * half_s)
        ng = gz[h]
        for i in range(1, 4):
            ng = ng + gz[2 * i + h]
        gg_ref[:, at] = jnp.sum(ng, axis=0, keepdims=True)
    for copy in head_copies:
        copy.wait()
    for copy in sends:
        copy.wait_send()


def fused(
    student_hidden, norm_gain, teacher_hidden, student_head, teacher_head, episode_source, lengths
):
    rows, wide_s = student_hidden.shape
    wide_t = teacher_hidden.shape[1]
    tokens = rows * lax.axis_size("grp")
    voc = student_head.shape[1]
    half_s, half_t = wide_s // 2, wide_t // 2
    positions = jnp.arange(SEQ, dtype=jnp.int32)
    order = (episode_source[:, None] * SEQ + positions[None, :]).reshape(-1, 1)
    valid = positions[None, :] < lengths[:, None]
    weight = jnp.where(valid, 1.0 / lengths.astype(F32)[:, None], 0.0).reshape(-1, 1)
    vmem = pl.BlockSpec(memory_space=pltpu.VMEM)
    hbm = pl.BlockSpec(memory_space=pl.ANY)
    dma = pltpu.SemaphoreType.DMA
    loss, grad_hidden, grad_gain, grad_head = pl.pallas_call(
        kernel,
        out_shape=(
            jax.ShapeDtypeStruct((1, 1), F32),
            jax.ShapeDtypeStruct((rows, wide_s), BF16),
            jax.ShapeDtypeStruct((1, wide_s), F32),
            jax.ShapeDtypeStruct((8, half_s, voc), BF16),
        ),
        in_specs=[vmem] * 5 + [hbm] * 2,
        out_specs=(vmem, vmem, vmem, hbm),
        scratch_shapes=[
            pltpu.VMEM((8, half_s, voc), BF16),
            pltpu.VMEM((8, half_t, voc), BF16),
            pltpu.VMEM((2, rows, half_s), BF16),
            pltpu.VMEM((2, rows, half_t), BF16),
            pltpu.VMEM((8, rows, half_s), BF16),
            pltpu.VMEM((8, rows, half_t), BF16),
            pltpu.VMEM((8, tokens + 16, half_s), BF16),
            pltpu.VMEM((8, tokens, half_t), BF16),
            pltpu.VMEM((8, tokens, half_s), BF16),
            pltpu.VMEM((tokens, voc), F32),
            pltpu.VMEM((tokens, voc), F32),
            pltpu.VMEM((tokens, 128), F32),
            pltpu.VMEM((tokens, 128), F32),
            pltpu.VMEM((8, 8, 256), F32),
            pltpu.VMEM((4, 8, 256), F32),
            pltpu.VMEM((tokens, voc), BF16),
            pltpu.VMEM((tokens, half_s), F32),
            pltpu.VMEM((4, tokens, half_s), BF16),
            pltpu.VMEM((4, tokens, half_s), BF16),
            pltpu.VMEM((4, tokens, half_s), BF16),
            pltpu.VMEM((4, tokens, half_s), BF16),
            pltpu.VMEM((8, rows, half_s), BF16),
            pltpu.VMEM((8, rows, half_s), BF16),
            pltpu.VMEM((8, half_s), F32),
            pltpu.VMEM((8, 8, half_s), F32),
            pltpu.VMEM((8, half_s, voc), BF16),
            dma(()), dma(()), dma((8,)),
        ] + [dma((8,))] * 20,
        compiler_params=pltpu.CompilerParams(
            collective_id=0, has_side_effects=True, vmem_limit_bytes=52 * 1024 * 1024
        ),
        cost_estimate=pl.CostEstimate(flops=2600000000, bytes_accessed=11000000, transcendentals=400000),
    )(
        student_hidden, teacher_hidden, norm_gain.reshape(1, -1), order, weight,
        student_head.reshape(8, half_s, voc), teacher_head.reshape(8, half_t, voc),
    )
    return (loss[0, 0], grad_hidden, grad_gain.reshape(-1), grad_head.reshape(student_head.shape))


def realign(teacher_hidden, table, group_index, per_group):
    groups = table.shape[0]
    source_group = table // per_group
    source_local = table % per_group
    mine = (source_group == group_index).astype(jnp.int32)
    earlier = jnp.cumsum(mine, axis=1) - mine
    slot_ids = jnp.arange(MOST, dtype=jnp.int32)
    matches = mine[:, :, None] * (earlier[:, :, None] == slot_ids[None, None, :]).astype(jnp.int32)
    send_index = jnp.sum(matches * source_local[:, :, None], axis=1)
    features = teacher_hidden.shape[1]
    episodes = teacher_hidden.reshape(per_group, SEQ, features)
    outgoing = jnp.take(episodes, send_index, axis=0)
    incoming = lax.all_to_all(outgoing, "grp", split_axis=0, concat_axis=0, tiled=True)
    own_groups = lax.dynamic_index_in_dim(source_group, group_index, 0, keepdims=False)
    matching = (own_groups[:, None] == own_groups[None, :]).astype(jnp.int32)
    position = jnp.sum(jnp.tril(matching, -1), axis=1)
    flat_index = own_groups * MOST + position
    received = incoming.reshape(groups * MOST, SEQ, features)
    return jnp.take(received, flat_index, axis=0).reshape(per_group * SEQ, features)


def local(
    student_hidden, norm_gain, teacher_hidden, student_head, teacher_head, episode_source, lengths
):
    groups = lax.axis_size("grp")
    group_index = lax.axis_index("grp")
    rows_group = student_hidden.shape[0]
    per_group = rows_group // SEQ
    hidden_f32 = student_hidden.astype(jnp.float32)
    squares = lax.psum(jnp.sum(hidden_f32 * hidden_f32, axis=1), "voc")
    inverse_rms = lax.rsqrt(squares / DS + EPSILON)
    normed = (hidden_f32 * inverse_rms[:, None] * norm_gain[None, :]).astype(jnp.bfloat16)
    table = episode_source.reshape(groups, per_group)
    aligned = realign(teacher_hidden, table, group_index, per_group)
    teacher_rows, student_rows = (
        lax.all_gather(aligned, "voc", axis=1, tiled=True),
        lax.all_gather(normed, "voc", axis=1, tiled=True),
    )
    teacher_logits = jnp.dot(
        lax.all_gather(teacher_rows, "grp", axis=0, tiled=True),
        teacher_head,
        preferred_element_type=jnp.float32,
    )
    positions = jnp.arange(SEQ, dtype=jnp.int32)
    all_rows = lax.all_gather(student_rows, "grp", axis=0, tiled=True)
    student_logits = jnp.dot(all_rows, student_head, preferred_element_type=jnp.float32)
    lengths_f32 = lengths.astype(jnp.float32)
    valid = positions[None, :] < lengths[:, None]
    token_weight = jnp.where(
        valid, 1.0 / lengths_f32[:, None], jnp.zeros_like(lengths_f32)[:, None]
    ).reshape(-1)
    top_student, top_teacher = lax.pmax(
        (jnp.max(student_logits, axis=1), jnp.max(teacher_logits, axis=1)), ("grp", "voc")
    )
    exp_student = jnp.exp(student_logits - top_student[:, None])
    exp_teacher = jnp.exp(teacher_logits - top_teacher[:, None])
    total_student, total_teacher = lax.psum(
        (jnp.sum(exp_student, axis=1), jnp.sum(exp_teacher, axis=1)), ("grp", "voc")
    )
    log_student = student_logits - (top_student + jnp.log(total_student))[:, None]
    log_teacher = teacher_logits - (top_teacher + jnp.log(total_teacher))[:, None]
    prob_student = jnp.exp(log_student)
    log_ratio = log_student - log_teacher
    divergence = lax.psum(jnp.sum(prob_student * log_ratio, axis=1), ("grp", "voc"))
    loss = jnp.sum(token_weight * divergence)
    logit_grad = (token_weight[:, None] * prob_student * (log_ratio - divergence[:, None])).astype(
        jnp.bfloat16
    )
    grad_head = lax.dot_general(
        all_rows, logit_grad, (((0,), (0,)), ((), ())), preferred_element_type=jnp.float32
    ).astype(jnp.bfloat16)
    full_term = lax.dot_general(
        logit_grad, student_head, (((1,), (1,)), ((), ())), preferred_element_type=jnp.float32
    )
    feature_part = lax.psum_scatter(
        full_term.astype(jnp.bfloat16), "voc", scatter_dimension=1, tiled=True
    )
    normed_grad = lax.psum_scatter(feature_part, "grp", scatter_dimension=0, tiled=True).astype(
        jnp.float32
    )
    scaled = normed_grad * norm_gain[None, :]
    inner = lax.psum(jnp.sum(scaled * hidden_f32, axis=1), "voc")
    grad_hidden = (
        inverse_rms[:, None] * scaled - hidden_f32 * (inverse_rms**3)[:, None] * inner[:, None] / DS
    )
    grad_gain = lax.psum(jnp.sum(normed_grad * hidden_f32 * inverse_rms[:, None], axis=0), "grp")
    return (loss, grad_hidden.astype(jnp.bfloat16), grad_gain, grad_head)


def solution(mesh):
    placed = (
        P("grp", "voc"),
        P("voc"),
        P("grp", "voc"),
        P(None, ("grp", "voc")),
        P(None, ("grp", "voc")),
        P(),
        P(),
    )
    body = fused if tuple(mesh.shape.values()) == (8, 4) else local
    return jax.shard_map(
        body,
        mesh=mesh,
        in_specs=placed,
        out_specs=(P(), P("grp", "voc"), P("voc"), P(None, ("grp", "voc"))),
        check_vma=False,
    )
```

```python
import functools

import jax
import jax.numpy as jnp
from jax import lax
from jax.experimental import pallas as pl
from jax.experimental.pallas import tpu as pltpu
from jax.sharding import PartitionSpec as P

DS = 4096
SEQ = 2
MOST = 2


EPSILON = 1e-06

F32 = jnp.float32
BF16 = jnp.bfloat16
LIMIT = 65472
MESH = pl.DeviceIdType.MESH


def flip(number, mask):
    low, high = number % 2, number // 2
    if mask & 1:
        low = 1 - low
    if mask & 2:
        high = 1 - high
    return high * 2 + low


def merge(parts):
    top = functools.reduce(jnp.maximum, [p[0:1] for p in parts])
    top_t = functools.reduce(jnp.maximum, [p[2:3] for p in parts])
    total = total_t = ratio = logit = both = 0.0
    for p in parts:
        shift, shift_t = p[0:1] - top, p[2:3] - top_t
        factor, factor_t = jnp.exp(shift), jnp.exp(shift_t)
        live = factor > 0.0
        shift = jnp.where(live, shift, 0.0)
        gap = shift - jnp.where(live, shift_t, 0.0)
        total = total + factor * p[1:2]
        total_t = total_t + factor_t * p[3:4]
        ratio = ratio + factor * (p[4:5] + p[1:2] * gap)
        logit = logit + factor * (p[5:6] + p[1:2] * shift)
        both = both + factor * (p[6:7] + gap * p[5:6] + shift * p[4:5] + shift * gap * p[1:2])
    return jnp.concatenate([top, total, top_t, total_t, ratio, logit, both, jnp.zeros_like(top)], axis=0)


def kernel(
    sh_hbm, th_hbm, gain_hbm, source_hbm, lengths_hbm, w_hbm, t_hbm,
    loss_ref, gh_ref, gg_ref, hg, g2,
    wv, tv, sh_ref, gain_ref, source_ref, lengths_ref, pick_ref, in_s, in_t, s_blk, t_blk, s_acc, t_acc, sq, cols,
    st_a, st_b, own, p_sib, r_sib, p_x, r_x, rb, rz, gp, gz,
    w_sem, t_sem, l_sem, s1s, s1r, t1s, t1r, s2s, s2r, t2s, t2r, as_, ar, bs, br,
    qs, qr, xs, xr, zs, zr, ys, yr,
):
    g = lax.axis_index("grp")
    v = lax.axis_index("voc")
    z, c = g // 2, g % 2
    k = v * 2 + c
    rows, half_s = in_s.shape[1], in_s.shape[2]
    half_t = in_t.shape[2]
    tokens = in_s.shape[0] * rows
    valid = tokens * 5 // 8
    slots = s_acc.shape[0]

    def plane(vm, cm):
        return {"grp": z * 2 + (1 - c if cm else c), "voc": flip(v, vm)}

    def column(zm, cm):
        return {"grp": flip(z, zm) * 2 + (1 - c if cm else c), "voc": v}

    def slot(vm, cm):
        return flip(v, vm) * 2 + (1 - c if cm else c)

    sends = []

    def send(src, dst, ssem, rsem, to):
        copy = pltpu.make_async_remote_copy(
            src_ref=src, dst_ref=dst, send_sem=ssem, recv_sem=rsem, device_id=to, device_id_type=MESH
        )
        copy.start()
        sends.append(copy)

    def arrived(dst, ssem, rsem, to):
        pltpu.make_async_remote_copy(
            src_ref=dst, dst_ref=dst, send_sem=ssem, recv_sem=rsem, device_id=to, device_id_type=MESH
        ).wait_recv()

    def half(ref, number, width):
        return ref.at[:, pl.ds(pl.multiple_of(number * width, 128), width)]

    local_copies = [
        pltpu.make_async_copy(src, dst, l_sem.at[i])
        for i, (src, dst) in enumerate((
            (source_hbm, source_ref), (lengths_hbm, lengths_ref), (gain_hbm, gain_ref),
            (half(sh_hbm, c, half_s), in_s.at[g]), (half(th_hbm, c, half_t), in_t.at[g]), (sh_hbm, sh_ref),
        ))
    ]
    for copy in local_copies:
        copy.start()
    w_copy = pltpu.make_async_copy(w_hbm, wv, w_sem)
    t_copy = pltpu.make_async_copy(t_hbm, tv, t_sem)
    w_copy.start()
    t_copy.start()

    barrier = pltpu.get_barrier_semaphore()
    peers = [plane(m // 2, m % 2) for m in range(1, 8)] + [column(m // 2, m % 2) for m in range(2, 8)]
    for peer in peers:
        pl.semaphore_signal(barrier, inc=1, device_id=peer, device_id_type=MESH)
    pl.semaphore_wait(barrier, len(peers))

    for m in range(1, 8):
        other = 1 - c if m % 2 else c
        send(half(sh_hbm, other, half_s), in_s.at[g], s1s.at[m], s1r.at[m], column(m // 2, m % 2))
    for m in range(1, 8):
        other = 1 - c if m % 2 else c
        send(half(th_hbm, other, half_t), in_t.at[g], t1s.at[m], t1r.at[m], column(m // 2, m % 2))

    for copy in local_copies[:3]:
        copy.wait()
    episodes = source_ref.shape[1]
    line = lax.broadcasted_iota(jnp.int32, (8, episodes), 0)
    table = jnp.where(line == 0, source_ref[...], jnp.where(line == 1, lengths_ref[...], 0)).astype(F32).astype(BF16)
    spread = lax.broadcasted_iota(jnp.int32, (episodes, tokens), 1) // SEQ == lax.broadcasted_iota(
        jnp.int32, (episodes, tokens), 0
    )
    table = jnp.dot(table, spread.astype(F32).astype(BF16), preferred_element_type=F32)
    position = (lax.broadcasted_iota(jnp.int32, (1, tokens), 1) % SEQ).astype(F32)
    row_source = table[0:1] * SEQ + position
    row_length = table[1:2]
    row_valid = (position < row_length).astype(F32)
    before = lax.broadcasted_iota(jnp.int32, (tokens, tokens), 0) < lax.broadcasted_iota(jnp.int32, (tokens, tokens), 1)
    rank = jnp.dot(
        jnp.broadcast_to(row_valid, (8, tokens)).astype(BF16), before.astype(F32).astype(BF16),
        preferred_element_type=F32,
    )[0:1]
    slot_line = lax.broadcasted_iota(jnp.int32, (slots, tokens), 0).astype(F32)
    pick = jnp.where(slot_line == rank, row_valid, 0.0).astype(BF16)
    pick_ref[...] = pick
    line = lax.broadcasted_iota(jnp.int32, (8, tokens), 0)
    both = jnp.where(line == 0, row_source, jnp.where(line == 1, row_length, 0.0)).astype(BF16)
    slot_table = lax.dot_general(pick, both, (((1,), (1,)), ((), ())), preferred_element_type=F32)
    slot_source, slot_length = slot_table[:, 0:1], slot_table[:, 1:2]
    weight = jnp.where(slot_length > 0.0, 1.0 / jnp.maximum(slot_length, 1.0), 0.0)
    teacher_lane = lax.broadcasted_iota(jnp.int32, (slots, tokens), 1).astype(F32)
    pick_t = jnp.where((slot_source == teacher_lane) & (slot_length > 0.0), 1.0, 0.0).astype(BF16)

    gain = gain_ref[...]
    own_gain = jnp.where(c == 0, gain[:, :half_s], gain[:, half_s:])
    hi = own_gain.astype(BF16).astype(F32)
    mid = (own_gain - hi).astype(BF16).astype(F32)
    lo = own_gain - hi - mid
    slot_id = lax.broadcasted_iota(jnp.int32, (slots, half_s), 0)
    gain_rows = jnp.where(
        slot_id == valid, hi, jnp.where(slot_id == valid + 1, mid, jnp.where(slot_id == valid + 2, lo, 0.0))
    )

    def source(m):
        return flip(z, m // 2) * 2 + (1 - c if m % 2 else c)

    for m in range(1, 8):
        arrived(in_s.at[source(m)], s1s.at[m], s1r.at[m], column(m // 2, m % 2))
    for copy in local_copies[3:]:
        copy.wait()
    block = jnp.concatenate([in_s[i].astype(F32) for i in range(8)], axis=0).astype(BF16)
    block = jnp.dot(pick, block, preferred_element_type=F32)
    s_blk[k] = jnp.where(slot_id < valid, block, gain_rows).astype(BF16)
    for vm in (1, 2, 3):
        send(s_blk.at[k], s_blk.at[k], s2s.at[vm * 2], s2r.at[vm * 2], plane(vm, 0))
    send(s_blk.at[k], s_blk.at[k], s2s.at[1], s2r.at[1], plane(0, 1))
    for m in range(1, 8):
        arrived(in_t.at[source(m)], t1s.at[m], t1r.at[m], column(m // 2, m % 2))
    block = jnp.concatenate([in_t[i].astype(F32) for i in range(8)], axis=0).astype(BF16)
    t_blk[k] = jnp.dot(pick_t, block, preferred_element_type=F32).astype(BF16)
    for vm in (1, 2, 3):
        send(t_blk.at[k], t_blk.at[k], t2s.at[vm * 2], t2r.at[vm * 2], plane(vm, 0))
    send(t_blk.at[k], t_blk.at[k], t2s.at[1], t2r.at[1], plane(0, 1))

    s_acc[...] = jnp.zeros_like(s_acc)
    t_acc[...] = jnp.zeros_like(t_acc)
    sq[...] = jnp.zeros_like(sq)
    w_copy.wait()

    def student_block(at):
        x = s_blk[at].astype(F32)
        scale = jnp.sum(x[valid:], axis=0, keepdims=True)
        x = jnp.where(slot_id < valid, x, 0.0)
        squares = x * x
        partial = squares[:, 0:128]
        for i in range(1, half_s // 128):
            partial = partial + squares[:, i * 128:(i + 1) * 128]
        sq[...] += partial
        scaled = (x * scale).astype(BF16)
        hg[at] = scaled
        s_acc[...] += jnp.dot(scaled, wv[at], preferred_element_type=F32)

    def teacher_block(at):
        t_acc[...] += jnp.dot(t_blk[at], tv[at], preferred_element_type=F32)

    def relay(blk, ssem, rsem, vm):
        at = slot(vm, 0)
        arrived(blk.at[at], ssem.at[vm * 2], rsem.at[vm * 2], plane(vm, 0))
        send(blk.at[at], blk.at[at], ssem.at[vm * 2 + 1], rsem.at[vm * 2 + 1], plane(0, 1))

    def sibling(blk, ssem, rsem, vm):
        arrived(blk.at[slot(vm, 1)], ssem.at[vm * 2 + 1], rsem.at[vm * 2 + 1], plane(0, 1))

    student_block(k)
    t_copy.wait()
    teacher_block(k)
    sibling(s_blk, s2s, s2r, 0)
    student_block(slot(0, 1))
    sibling(t_blk, t2s, t2r, 0)
    teacher_block(slot(0, 1))
    for vm in (1, 2, 3):
        relay(s_blk, s2s, s2r, vm)
        student_block(slot(vm, 0))
        sibling(s_blk, s2s, s2r, vm)
        student_block(slot(vm, 1))
    for vm in (1, 2, 3):
        relay(t_blk, t2s, t2r, vm)
        teacher_block(slot(vm, 0))
        sibling(t_blk, t2s, t2r, vm)
        teacher_block(slot(vm, 1))

    inv = lax.rsqrt(jnp.sum(sq[...], axis=1, keepdims=True) / DS + EPSILON)
    s_log = s_acc[...] * inv
    t_log = t_acc[...]
    top = jnp.max(s_log, axis=1, keepdims=True)
    top_t = jnp.max(t_log, axis=1, keepdims=True)
    a = s_log - top
    b = t_log - top_t
    e = jnp.exp(a)
    ea = e * a
    d = a - b
    figures = [
        top, jnp.sum(e, axis=1, keepdims=True), top_t, jnp.sum(jnp.exp(b), axis=1, keepdims=True),
        jnp.sum(e * d, axis=1, keepdims=True), jnp.sum(ea, axis=1, keepdims=True),
        jnp.sum(ea * d, axis=1, keepdims=True),
    ]
    lane = lax.broadcasted_iota(jnp.int32, (slots, 128), 1)
    packed = jnp.zeros((slots, 128), F32)
    for i, figure in enumerate(figures):
        packed = jnp.where(lane == i, figure, packed)
    st_a[k] = jnp.transpose(packed)[0:8, :]
    for m in range(1, 8):
        send(st_a.at[k], st_a.at[k], as_.at[m], ar.at[m], plane(m // 2, m % 2))
    for m in range(1, 8):
        arrived(st_a.at[slot(m // 2, m % 2)], as_.at[m], ar.at[m], plane(m // 2, m % 2))
    st_b[z] = merge([st_a[i] for i in range(8)])
    for m in range(1, 4):
        send(st_b.at[z], st_b.at[z], bs.at[m], br.at[m], column(m, 0))
    for m in range(1, 4):
        arrived(st_b.at[flip(z, m)], bs.at[m], br.at[m], column(m, 0))
    full = merge([st_b[i] for i in range(4)])
    total = full[1:2]
    lse = full[0:1] + jnp.log(total)
    lse_t = full[2:3] + jnp.log(full[3:4])
    mean_ratio, mean_logit = full[4:5] / total, full[5:6] / total
    divergence = mean_ratio - jnp.log(total) + jnp.log(full[3:4])
    offset = lse - lse_t + divergence
    cov = full[6:7] / total - mean_ratio * mean_logit
    back = jnp.concatenate([lse, offset, divergence, cov, jnp.zeros((slots - 4, slots), F32)], axis=0)
    back = jnp.transpose(back)
    loss_ref[...] = jnp.sum(weight * back[:, 2:3], axis=0, keepdims=True)
    prob = jnp.exp(s_log - back[:, 0:1])
    grad = ((weight * inv) * prob * (s_log - t_log - back[:, 1:2])).astype(BF16)
    g2[...] = grad
    lane = lax.broadcasted_iota(jnp.int32, (slots, 128), 1)
    figure = weight * inv * inv * back[:, 3:4] / DS
    hi = figure.astype(BF16).astype(F32)
    mid = (figure - hi).astype(BF16).astype(F32)
    lo = figure - hi - mid
    packed = jnp.where(lane == 0, hi, jnp.where(lane == 1, mid, jnp.where(lane == 2, lo, 0.0))).astype(BF16)
    packed = lax.dot_general(pick_ref[...], packed, (((0,), (0,)), ((), ())), preferred_element_type=F32)
    cols[...] = jnp.broadcast_to(jnp.sum(packed, axis=1, keepdims=True), cols.shape)

    def block_grad(at):
        return lax.dot_general(g2[...], wv[at], (((1,), (1,)), ((), ())), preferred_element_type=F32)

    order = (1, 2, 3, 0)
    for vm in order:
        p_sib[vm] = block_grad(slot(vm, 1)).astype(BF16)
        send(p_sib.at[vm], r_sib.at[vm], qs.at[vm], qr.at[vm], plane(0, 1))
    for vm in order:
        mine = block_grad(slot(vm, 0))
        arrived(r_sib.at[vm], qs.at[vm], qr.at[vm], plane(0, 1))
        mine = mine + r_sib[vm].astype(F32)
        if vm:
            p_x[vm] = mine.astype(BF16)
            send(p_x.at[vm], r_x.at[vm], xs.at[vm], xr.at[vm], plane(vm, 0))
        else:
            own[...] = mine

    for vm in (1, 2, 3):
        arrived(r_x.at[vm], xs.at[vm], xr.at[vm], plane(vm, 0))
    total = own[...]
    for vm in (1, 2, 3):
        total = total + r_x[vm].astype(F32)
    spread_out = lax.dot_general(
        pick_ref[...], total.astype(BF16), (((0,), (0,)), ((), ())), preferred_element_type=F32
    )
    for i in range(8):
        rb[i] = spread_out[i * rows:(i + 1) * rows].astype(BF16)
    for m in range(1, 8):
        send(rb.at[source(m)], rz.at[g], zs.at[m], zr.at[m], column(m // 2, m % 2))
    rz[g] = rb[g]
    part = jnp.sum(total * jnp.where(slot_id < valid, s_blk[k].astype(F32), 0.0), axis=0, keepdims=True)
    gp[...] = part
    for m in range(1, 8):
        send(gp, gz.at[g], ys.at[m], yr.at[m], column(m // 2, m % 2))
    gz[g] = part
    for m in range(1, 8):
        arrived(rz.at[source(m)], zs.at[m], zr.at[m], column(m // 2, m % 2))
    own_cols = cols[pl.ds(pl.multiple_of(g * rows, 8), rows), :][:, 0:1]
    for h in range(2):
        at = slice(h * half_s, (h + 1) * half_s)
        ng = rz[h].astype(F32)
        for i in range(1, 4):
            ng = ng + rz[2 * i + h].astype(F32)
        hid = sh_ref[:, at].astype(F32)
        gh_ref[:, at] = (gain_ref[:, at] * ng - hid * own_cols).astype(BF16)
    for m in range(1, 8):
        arrived(gz.at[source(m)], ys.at[m], yr.at[m], column(m // 2, m % 2))
    for h in range(2):
        at = slice(h * half_s, (h + 1) * half_s)
        ng = gz[h]
        for i in range(1, 4):
            ng = ng + gz[2 * i + h]
        gg_ref[:, at] = ng
    for copy in sends:
        copy.wait_send()


def head_kernel(
    rows_hbm, grad_hbm, loss_hbm, hidden_hbm, gain_hbm, head_hbm, loss_out, hidden_out, gain_out,
    rows_ref, grad_ref, head, in_sem, out_sem, pass_sem, grad_sem,
):
    copies = [pltpu.make_async_copy(grad_hbm, grad_ref, grad_sem)]
    copies += [pltpu.make_async_copy(rows_hbm.at[i], rows_ref.at[i], in_sem.at[i]) for i in range(8)]
    passed = [
        pltpu.make_async_copy(src, dst, pass_sem.at[i])
        for i, (src, dst) in enumerate(((hidden_hbm, hidden_out), (gain_hbm, gain_out), (loss_hbm, loss_out)))
    ]
    for copy in copies + passed:
        copy.start()
    copies[0].wait()
    for i in range(8):
        copies[i + 1].wait()
        head[i] = lax.dot_general(
            rows_ref[i], grad_ref[...], (((0,), (0,)), ((), ())), preferred_element_type=F32
        ).astype(BF16)
        copy = pltpu.make_async_copy(head.at[i], head_hbm.at[i], out_sem.at[i])
        copy.start()
        passed.append(copy)
    for copy in passed:
        copy.wait()


def fused(
    student_hidden, norm_gain, teacher_hidden, student_head, teacher_head, episode_source, lengths
):
    rows, wide_s = student_hidden.shape
    wide_t = teacher_hidden.shape[1]
    tokens = rows * lax.axis_size("grp")
    voc = student_head.shape[1]
    half_s, half_t = wide_s // 2, wide_t // 2
    slots = -(-(tokens * 5 // 8 + 3) // 128) * 128
    vmem = pl.BlockSpec(memory_space=pltpu.VMEM)
    hbm = pl.BlockSpec(memory_space=pltpu.HBM)
    dma = pltpu.SemaphoreType.DMA
    loss, grad_hidden, grad_gain, scaled_rows, logit_grad = pl.pallas_call(
        kernel,
        out_shape=(
            jax.ShapeDtypeStruct((1, 1), F32),
            jax.ShapeDtypeStruct((rows, wide_s), BF16),
            jax.ShapeDtypeStruct((1, wide_s), F32),
            jax.ShapeDtypeStruct((8, slots, half_s), BF16),
            jax.ShapeDtypeStruct((slots, voc), BF16),
        ),
        in_specs=[hbm] * 7,
        out_specs=(vmem,) * 5,
        scratch_shapes=[
            pltpu.VMEM((8, half_s, voc), BF16),
            pltpu.VMEM((8, half_t, voc), BF16),
            pltpu.VMEM((rows, wide_s), BF16),
            pltpu.VMEM((1, wide_s), F32),
            pltpu.VMEM((1, episode_source.shape[0]), jnp.int32),
            pltpu.VMEM((1, episode_source.shape[0]), jnp.int32),
            pltpu.VMEM((slots, tokens), BF16),
            pltpu.VMEM((8, rows, half_s), BF16),
            pltpu.VMEM((8, rows, half_t), BF16),
            pltpu.VMEM((8, slots, half_s), BF16),
            pltpu.VMEM((8, slots, half_t), BF16),
            pltpu.VMEM((slots, voc), F32),
            pltpu.VMEM((slots, voc), F32),
            pltpu.VMEM((slots, 128), F32),
            pltpu.VMEM((tokens, 128), F32),
            pltpu.VMEM((8, 8, slots), F32),
            pltpu.VMEM((4, 8, slots), F32),
            pltpu.VMEM((slots, half_s), F32),
            pltpu.VMEM((4, slots, half_s), BF16),
            pltpu.VMEM((4, slots, half_s), BF16),
            pltpu.VMEM((4, slots, half_s), BF16),
            pltpu.VMEM((4, slots, half_s), BF16),
            pltpu.VMEM((8, rows, half_s), BF16),
            pltpu.VMEM((8, rows, half_s), BF16),
            pltpu.VMEM((1, half_s), F32),
            pltpu.VMEM((8, 1, half_s), F32),
            dma(()), dma(()), dma((8,)),
        ] + [dma((8,))] * 20,
        compiler_params=pltpu.CompilerParams(
            collective_id=0, has_side_effects=True, vmem_limit_bytes=LIMIT * 1024
        ),
        cost_estimate=pl.CostEstimate(flops=2600000000, bytes_accessed=11000000, transcendentals=400000),
    )(
        student_hidden, teacher_hidden, norm_gain.reshape(1, -1),
        episode_source.reshape(1, -1), lengths.reshape(1, -1),
        student_head.reshape(8, half_s, voc), teacher_head.reshape(8, half_t, voc),
    )
    grad_head, loss, grad_hidden, grad_gain = pl.pallas_call(
        head_kernel,
        out_shape=(
            jax.ShapeDtypeStruct((8, half_s, voc), BF16),
            jax.ShapeDtypeStruct((1, 1), F32),
            jax.ShapeDtypeStruct((rows, wide_s), BF16),
            jax.ShapeDtypeStruct((1, wide_s), F32),
        ),
        in_specs=[hbm] * 5,
        out_specs=(hbm,) * 4,
        scratch_shapes=[
            pltpu.VMEM((8, slots, half_s), BF16),
            pltpu.VMEM((slots, voc), BF16),
            pltpu.VMEM((8, half_s, voc), BF16),
            dma((8,)), dma((8,)), dma((3,)), dma(()),
        ],
        compiler_params=pltpu.CompilerParams(vmem_limit_bytes=LIMIT * 1024),
        cost_estimate=pl.CostEstimate(flops=402653184, bytes_accessed=4300000, transcendentals=0),
    )(scaled_rows, logit_grad, loss, grad_hidden, grad_gain)
    return (loss[0, 0], grad_hidden, grad_gain.reshape(-1), grad_head.reshape(student_head.shape))


def realign(teacher_hidden, table, group_index, per_group):
    groups = table.shape[0]
    source_group = table // per_group
    source_local = table % per_group
    mine = (source_group == group_index).astype(jnp.int32)
    earlier = jnp.cumsum(mine, axis=1) - mine
    slot_ids = jnp.arange(MOST, dtype=jnp.int32)
    matches = mine[:, :, None] * (earlier[:, :, None] == slot_ids[None, None, :]).astype(jnp.int32)
    send_index = jnp.sum(matches * source_local[:, :, None], axis=1)
    features = teacher_hidden.shape[1]
    episodes = teacher_hidden.reshape(per_group, SEQ, features)
    outgoing = jnp.take(episodes, send_index, axis=0)
    incoming = lax.all_to_all(outgoing, "grp", split_axis=0, concat_axis=0, tiled=True)
    own_groups = lax.dynamic_index_in_dim(source_group, group_index, 0, keepdims=False)
    matching = (own_groups[:, None] == own_groups[None, :]).astype(jnp.int32)
    position = jnp.sum(jnp.tril(matching, -1), axis=1)
    flat_index = own_groups * MOST + position
    received = incoming.reshape(groups * MOST, SEQ, features)
    return jnp.take(received, flat_index, axis=0).reshape(per_group * SEQ, features)


def local(
    student_hidden, norm_gain, teacher_hidden, student_head, teacher_head, episode_source, lengths
):
    groups = lax.axis_size("grp")
    group_index = lax.axis_index("grp")
    rows_group = student_hidden.shape[0]
    per_group = rows_group // SEQ
    hidden_f32 = student_hidden.astype(jnp.float32)
    squares = lax.psum(jnp.sum(hidden_f32 * hidden_f32, axis=1), "voc")
    inverse_rms = lax.rsqrt(squares / DS + EPSILON)
    normed = (hidden_f32 * inverse_rms[:, None] * norm_gain[None, :]).astype(jnp.bfloat16)
    table = episode_source.reshape(groups, per_group)
    aligned = realign(teacher_hidden, table, group_index, per_group)
    teacher_rows, student_rows = (
        lax.all_gather(aligned, "voc", axis=1, tiled=True),
        lax.all_gather(normed, "voc", axis=1, tiled=True),
    )
    teacher_logits = jnp.dot(
        lax.all_gather(teacher_rows, "grp", axis=0, tiled=True),
        teacher_head,
        preferred_element_type=jnp.float32,
    )
    positions = jnp.arange(SEQ, dtype=jnp.int32)
    all_rows = lax.all_gather(student_rows, "grp", axis=0, tiled=True)
    student_logits = jnp.dot(all_rows, student_head, preferred_element_type=jnp.float32)
    lengths_f32 = lengths.astype(jnp.float32)
    valid = positions[None, :] < lengths[:, None]
    token_weight = jnp.where(
        valid, 1.0 / lengths_f32[:, None], jnp.zeros_like(lengths_f32)[:, None]
    ).reshape(-1)
    top_student, top_teacher = lax.pmax(
        (jnp.max(student_logits, axis=1), jnp.max(teacher_logits, axis=1)), ("grp", "voc")
    )
    exp_student = jnp.exp(student_logits - top_student[:, None])
    exp_teacher = jnp.exp(teacher_logits - top_teacher[:, None])
    total_student, total_teacher = lax.psum(
        (jnp.sum(exp_student, axis=1), jnp.sum(exp_teacher, axis=1)), ("grp", "voc")
    )
    log_student = student_logits - (top_student + jnp.log(total_student))[:, None]
    log_teacher = teacher_logits - (top_teacher + jnp.log(total_teacher))[:, None]
    prob_student = jnp.exp(log_student)
    log_ratio = log_student - log_teacher
    divergence = lax.psum(jnp.sum(prob_student * log_ratio, axis=1), ("grp", "voc"))
    loss = jnp.sum(token_weight * divergence)
    logit_grad = (token_weight[:, None] * prob_student * (log_ratio - divergence[:, None])).astype(
        jnp.bfloat16
    )
    grad_head = lax.dot_general(
        all_rows, logit_grad, (((0,), (0,)), ((), ())), preferred_element_type=jnp.float32
    ).astype(jnp.bfloat16)
    full_term = lax.dot_general(
        logit_grad, student_head, (((1,), (1,)), ((), ())), preferred_element_type=jnp.float32
    )
    feature_part = lax.psum_scatter(
        full_term.astype(jnp.bfloat16), "voc", scatter_dimension=1, tiled=True
    )
    normed_grad = lax.psum_scatter(feature_part, "grp", scatter_dimension=0, tiled=True).astype(
        jnp.float32
    )
    scaled = normed_grad * norm_gain[None, :]
    inner = lax.psum(jnp.sum(scaled * hidden_f32, axis=1), "voc")
    grad_hidden = (
        inverse_rms[:, None] * scaled - hidden_f32 * (inverse_rms**3)[:, None] * inner[:, None] / DS
    )
    grad_gain = lax.psum(jnp.sum(normed_grad * hidden_f32 * inverse_rms[:, None], axis=0), "grp")
    return (loss, grad_hidden.astype(jnp.bfloat16), grad_gain, grad_head)


def solution(mesh):
    placed = (
        P("grp", "voc"),
        P("voc"),
        P("grp", "voc"),
        P(None, ("grp", "voc")),
        P(None, ("grp", "voc")),
        P(),
        P(),
    )
    body = fused if tuple(mesh.shape.values()) == (8, 4) else local
    return jax.shard_map(
        body,
        mesh=mesh,
        in_specs=placed,
        out_specs=(P(), P("grp", "voc"), P("voc"), P(None, ("grp", "voc"))),
        check_vma=False,
    )
```

```python
import functools

import jax
import jax.numpy as jnp
from jax import lax
from jax.experimental import pallas as pl
from jax.experimental.pallas import tpu as pltpu
from jax.sharding import PartitionSpec as P

DS = 4096
SEQ = 2
MOST = 2


EPSILON = 1e-06

F32 = jnp.float32
BF16 = jnp.bfloat16
LIMIT = 65472
MESH = pl.DeviceIdType.MESH


def flip(number, mask):
    low, high = number % 2, number // 2
    if mask & 1:
        low = 1 - low
    if mask & 2:
        high = 1 - high
    return high * 2 + low


def merge(parts):
    top = functools.reduce(jnp.maximum, [p[0:1] for p in parts])
    top_t = functools.reduce(jnp.maximum, [p[2:3] for p in parts])
    total = total_t = ratio = logit = both = 0.0
    for p in parts:
        shift, shift_t = p[0:1] - top, p[2:3] - top_t
        factor, factor_t = jnp.exp(shift), jnp.exp(shift_t)
        live = factor > 0.0
        shift = jnp.where(live, shift, 0.0)
        gap = shift - jnp.where(live, shift_t, 0.0)
        total = total + factor * p[1:2]
        total_t = total_t + factor_t * p[3:4]
        ratio = ratio + factor * (p[4:5] + p[1:2] * gap)
        logit = logit + factor * (p[5:6] + p[1:2] * shift)
        both = both + factor * (p[6:7] + gap * p[5:6] + shift * p[4:5] + shift * gap * p[1:2])
    return jnp.concatenate([top, total, top_t, total_t, ratio, logit, both, jnp.zeros_like(top)], axis=0)


def kernel(
    sh_hbm, th_hbm, gain_hbm, source_hbm, lengths_hbm, w_hbm, t_hbm,
    loss_ref, gh_ref, gg_ref, head_hbm,
    wv, tv, sh_ref, gain_ref, source_ref, lengths_ref, pick_ref, in_s, in_t, s_blk, t_blk, hg, s_acc, t_acc, sq, cols,
    st_a, st_b, g2, own, p_sib, r_sib, p_x, r_x, rb, rz, gp, gz, head,
    w_sem, t_sem, h_sem, l_sem, s1s, s1r, t1s, t1r, s2s, s2r, t2s, t2r, as_, ar, bs, br,
    qs, qr, xs, xr, zs, zr, ys, yr,
):
    g = lax.axis_index("grp")
    v = lax.axis_index("voc")
    z, c = g // 2, g % 2
    k = v * 2 + c
    rows, half_s = in_s.shape[1], in_s.shape[2]
    half_t = in_t.shape[2]
    tokens = in_s.shape[0] * rows
    valid = tokens * 5 // 8
    slots = s_acc.shape[0]

    def plane(vm, cm):
        return {"grp": z * 2 + (1 - c if cm else c), "voc": flip(v, vm)}

    def column(zm, cm):
        return {"grp": flip(z, zm) * 2 + (1 - c if cm else c), "voc": v}

    def slot(vm, cm):
        return flip(v, vm) * 2 + (1 - c if cm else c)

    sends = []

    def send(src, dst, ssem, rsem, to):
        copy = pltpu.make_async_remote_copy(
            src_ref=src, dst_ref=dst, send_sem=ssem, recv_sem=rsem, device_id=to, device_id_type=MESH
        )
        copy.start()
        sends.append(copy)

    def arrived(dst, ssem, rsem, to):
        pltpu.make_async_remote_copy(
            src_ref=dst, dst_ref=dst, send_sem=ssem, recv_sem=rsem, device_id=to, device_id_type=MESH
        ).wait_recv()

    def half(ref, number, width):
        return ref.at[:, pl.ds(pl.multiple_of(number * width, 128), width)]

    local_copies = [
        pltpu.make_async_copy(src, dst, l_sem.at[i])
        for i, (src, dst) in enumerate((
            (source_hbm, source_ref), (lengths_hbm, lengths_ref), (gain_hbm, gain_ref),
            (half(sh_hbm, c, half_s), in_s.at[g]), (half(th_hbm, c, half_t), in_t.at[g]), (sh_hbm, sh_ref),
        ))
    ]
    for copy in local_copies:
        copy.start()
    w_copy = pltpu.make_async_copy(w_hbm, wv, w_sem)
    t_copy = pltpu.make_async_copy(t_hbm, tv, t_sem)
    w_copy.start()
    t_copy.start()

    barrier = pltpu.get_barrier_semaphore()
    peers = [plane(m // 2, m % 2) for m in range(1, 8)] + [column(m // 2, m % 2) for m in range(2, 8)]
    for peer in peers:
        pl.semaphore_signal(barrier, inc=1, device_id=peer, device_id_type=MESH)
    pl.semaphore_wait(barrier, len(peers))

    for m in range(1, 8):
        other = 1 - c if m % 2 else c
        send(half(sh_hbm, other, half_s), in_s.at[g], s1s.at[m], s1r.at[m], column(m // 2, m % 2))
    for m in range(1, 8):
        other = 1 - c if m % 2 else c
        send(half(th_hbm, other, half_t), in_t.at[g], t1s.at[m], t1r.at[m], column(m // 2, m % 2))

    for copy in local_copies[:3]:
        copy.wait()
    episodes = source_ref.shape[1]
    line = lax.broadcasted_iota(jnp.int32, (8, episodes), 0)
    table = jnp.where(line == 0, source_ref[...], jnp.where(line == 1, lengths_ref[...], 0)).astype(F32).astype(BF16)
    spread = lax.broadcasted_iota(jnp.int32, (episodes, tokens), 1) // SEQ == lax.broadcasted_iota(
        jnp.int32, (episodes, tokens), 0
    )
    table = jnp.dot(table, spread.astype(F32).astype(BF16), preferred_element_type=F32)
    position = (lax.broadcasted_iota(jnp.int32, (1, tokens), 1) % SEQ).astype(F32)
    row_source = table[0:1] * SEQ + position
    row_length = table[1:2]
    row_valid = (position < row_length).astype(F32)
    before = lax.broadcasted_iota(jnp.int32, (tokens, tokens), 0) < lax.broadcasted_iota(jnp.int32, (tokens, tokens), 1)
    rank = jnp.dot(
        jnp.broadcast_to(row_valid, (8, tokens)).astype(BF16), before.astype(F32).astype(BF16),
        preferred_element_type=F32,
    )[0:1]
    slot_line = lax.broadcasted_iota(jnp.int32, (slots, tokens), 0).astype(F32)
    pick = jnp.where(slot_line == rank, row_valid, 0.0).astype(BF16)
    pick_ref[...] = pick
    line = lax.broadcasted_iota(jnp.int32, (8, tokens), 0)
    both = jnp.where(line == 0, row_source, jnp.where(line == 1, row_length, 0.0)).astype(BF16)
    slot_table = lax.dot_general(pick, both, (((1,), (1,)), ((), ())), preferred_element_type=F32)
    slot_source, slot_length = slot_table[:, 0:1], slot_table[:, 1:2]
    weight = jnp.where(slot_length > 0.0, 1.0 / jnp.maximum(slot_length, 1.0), 0.0)
    teacher_lane = lax.broadcasted_iota(jnp.int32, (slots, tokens), 1).astype(F32)
    pick_t = jnp.where((slot_source == teacher_lane) & (slot_length > 0.0), 1.0, 0.0).astype(BF16)

    gain = gain_ref[...]
    own_gain = jnp.where(c == 0, gain[:, :half_s], gain[:, half_s:])
    hi = own_gain.astype(BF16).astype(F32)
    mid = (own_gain - hi).astype(BF16).astype(F32)
    lo = own_gain - hi - mid
    slot_id = lax.broadcasted_iota(jnp.int32, (slots, half_s), 0)
    gain_rows = jnp.where(
        slot_id == valid, hi, jnp.where(slot_id == valid + 1, mid, jnp.where(slot_id == valid + 2, lo, 0.0))
    )

    def source(m):
        return flip(z, m // 2) * 2 + (1 - c if m % 2 else c)

    for m in range(1, 8):
        arrived(in_s.at[source(m)], s1s.at[m], s1r.at[m], column(m // 2, m % 2))
    for copy in local_copies[3:]:
        copy.wait()
    block = jnp.concatenate([in_s[i].astype(F32) for i in range(8)], axis=0).astype(BF16)
    block = jnp.dot(pick, block, preferred_element_type=F32)
    s_blk[k] = jnp.where(slot_id < valid, block, gain_rows).astype(BF16)
    for vm in (1, 2, 3):
        send(s_blk.at[k], s_blk.at[k], s2s.at[vm * 2], s2r.at[vm * 2], plane(vm, 0))
    send(s_blk.at[k], s_blk.at[k], s2s.at[1], s2r.at[1], plane(0, 1))
    for m in range(1, 8):
        arrived(in_t.at[source(m)], t1s.at[m], t1r.at[m], column(m // 2, m % 2))
    block = jnp.concatenate([in_t[i].astype(F32) for i in range(8)], axis=0).astype(BF16)
    t_blk[k] = jnp.dot(pick_t, block, preferred_element_type=F32).astype(BF16)
    for vm in (1, 2, 3):
        send(t_blk.at[k], t_blk.at[k], t2s.at[vm * 2], t2r.at[vm * 2], plane(vm, 0))
    send(t_blk.at[k], t_blk.at[k], t2s.at[1], t2r.at[1], plane(0, 1))

    s_acc[...] = jnp.zeros_like(s_acc)
    t_acc[...] = jnp.zeros_like(t_acc)
    sq[...] = jnp.zeros_like(sq)
    w_copy.wait()

    def student_block(at):
        x = s_blk[at].astype(F32)
        scale = jnp.sum(x[valid:], axis=0, keepdims=True)
        x = jnp.where(slot_id < valid, x, 0.0)
        squares = x * x
        partial = squares[:, 0:128]
        for i in range(1, half_s // 128):
            partial = partial + squares[:, i * 128:(i + 1) * 128]
        sq[...] += partial
        scaled = x * scale
        hg[at] = jnp.transpose(scaled).astype(BF16)
        s_acc[...] += jnp.dot(scaled.astype(BF16), wv[at], preferred_element_type=F32)

    def teacher_block(at):
        t_acc[...] += jnp.dot(t_blk[at], tv[at], preferred_element_type=F32)

    def relay(blk, ssem, rsem, vm):
        at = slot(vm, 0)
        arrived(blk.at[at], ssem.at[vm * 2], rsem.at[vm * 2], plane(vm, 0))
        send(blk.at[at], blk.at[at], ssem.at[vm * 2 + 1], rsem.at[vm * 2 + 1], plane(0, 1))

    def sibling(blk, ssem, rsem, vm):
        arrived(blk.at[slot(vm, 1)], ssem.at[vm * 2 + 1], rsem.at[vm * 2 + 1], plane(0, 1))

    student_block(k)
    t_copy.wait()
    teacher_block(k)
    sibling(s_blk, s2s, s2r, 0)
    student_block(slot(0, 1))
    sibling(t_blk, t2s, t2r, 0)
    teacher_block(slot(0, 1))
    for vm in (1, 2, 3):
        relay(s_blk, s2s, s2r, vm)
        student_block(slot(vm, 0))
        sibling(s_blk, s2s, s2r, vm)
        student_block(slot(vm, 1))
    for vm in (1, 2, 3):
        relay(t_blk, t2s, t2r, vm)
        teacher_block(slot(vm, 0))
        sibling(t_blk, t2s, t2r, vm)
        teacher_block(slot(vm, 1))

    inv = lax.rsqrt(jnp.sum(sq[...], axis=1, keepdims=True) / DS + EPSILON)
    s_log = s_acc[...] * inv
    t_log = t_acc[...]
    top = jnp.max(s_log, axis=1, keepdims=True)
    top_t = jnp.max(t_log, axis=1, keepdims=True)
    a = s_log - top
    b = t_log - top_t
    e = jnp.exp(a)
    ea = e * a
    d = a - b
    figures = [
        top, jnp.sum(e, axis=1, keepdims=True), top_t, jnp.sum(jnp.exp(b), axis=1, keepdims=True),
        jnp.sum(e * d, axis=1, keepdims=True), jnp.sum(ea, axis=1, keepdims=True),
        jnp.sum(ea * d, axis=1, keepdims=True),
    ]
    lane = lax.broadcasted_iota(jnp.int32, (slots, 128), 1)
    packed = jnp.zeros((slots, 128), F32)
    for i, figure in enumerate(figures):
        packed = jnp.where(lane == i, figure, packed)
    st_a[k] = jnp.transpose(packed)[0:8, :]
    for m in range(1, 8):
        send(st_a.at[k], st_a.at[k], as_.at[m], ar.at[m], plane(m // 2, m % 2))
    for m in range(1, 8):
        arrived(st_a.at[slot(m // 2, m % 2)], as_.at[m], ar.at[m], plane(m // 2, m % 2))
    st_b[z] = merge([st_a[i] for i in range(8)])
    for m in range(1, 4):
        send(st_b.at[z], st_b.at[z], bs.at[m], br.at[m], column(m, 0))
    for m in range(1, 4):
        arrived(st_b.at[flip(z, m)], bs.at[m], br.at[m], column(m, 0))
    full = merge([st_b[i] for i in range(4)])
    total = full[1:2]
    lse = full[0:1] + jnp.log(total)
    lse_t = full[2:3] + jnp.log(full[3:4])
    mean_ratio, mean_logit = full[4:5] / total, full[5:6] / total
    divergence = mean_ratio - jnp.log(total) + jnp.log(full[3:4])
    offset = lse - lse_t + divergence
    cov = full[6:7] / total - mean_ratio * mean_logit
    back = jnp.concatenate([lse, offset, divergence, cov, jnp.zeros((slots - 4, slots), F32)], axis=0)
    back = jnp.transpose(back)
    loss_ref[...] = jnp.sum(weight * back[:, 2:3], axis=0, keepdims=True)
    prob = jnp.exp(s_log - back[:, 0:1])
    grad = ((weight * inv) * prob * (s_log - t_log - back[:, 1:2])).astype(BF16)
    g2[...] = grad
    lane = lax.broadcasted_iota(jnp.int32, (slots, 128), 1)
    figure = weight * inv * inv * back[:, 3:4] / DS
    hi = figure.astype(BF16).astype(F32)
    mid = (figure - hi).astype(BF16).astype(F32)
    lo = figure - hi - mid
    packed = jnp.where(lane == 0, hi, jnp.where(lane == 1, mid, jnp.where(lane == 2, lo, 0.0))).astype(BF16)
    packed = lax.dot_general(pick_ref[...], packed, (((0,), (0,)), ((), ())), preferred_element_type=F32)
    cols[...] = jnp.broadcast_to(jnp.sum(packed, axis=1, keepdims=True), cols.shape)

    def block_grad(at):
        return lax.dot_general(g2[...], wv[at], (((1,), (1,)), ((), ())), preferred_element_type=F32)

    order = (1, 2, 3, 0)
    part = half_s // 2
    for vm in order:
        p_sib[vm] = block_grad(slot(vm, 1)).astype(BF16)
        send(p_sib.at[vm], r_sib.at[vm], qs.at[vm], qr.at[vm], plane(0, 1))
    for vm in order:
        mine = block_grad(slot(vm, 0))
        arrived(r_sib.at[vm], qs.at[vm], qr.at[vm], plane(0, 1))
        mine = mine + r_sib[vm].astype(F32)
        if vm:
            p_x[vm] = mine.astype(BF16)
            send(p_x.at[vm, :, 0:part], r_x.at[vm, :, 0:part], xs.at[vm], xr.at[vm], plane(vm, 0))
        else:
            own[...] = mine
    for vm in (1, 2, 3):
        send(p_x.at[vm, :, part:], r_x.at[vm, :, part:], xs.at[vm + 4], xr.at[vm + 4], plane(vm, 0))

    def head_block(i):
        head[i] = jnp.dot(hg[i], g2[...], preferred_element_type=F32).astype(BF16)
        copy = pltpu.make_async_copy(head.at[i], head_hbm.at[i], h_sem.at[i])
        copy.start()
        head_copies.append(copy)

    head_copies = []
    for i in range(4):
        head_block(i)
    for h in range(2):
        at = slice(h * part, (h + 1) * part)
        for vm in (1, 2, 3):
            arrived(r_x.at[vm, :, at], xs.at[vm + 4 * h], xr.at[vm + 4 * h], plane(vm, 0))
        total = own[:, at]
        for vm in (1, 2, 3):
            total = total + r_x[vm, :, at].astype(F32)
        spread_out = lax.dot_general(
            pick_ref[...], total.astype(BF16), (((0,), (0,)), ((), ())), preferred_element_type=F32
        )
        for i in range(8):
            rb[i, :, at] = spread_out[i * rows:(i + 1) * rows].astype(BF16)
        for m in range(1, 8):
            send(
                rb.at[source(m), :, at], rz.at[g, :, at], zs.at[m + 8 * h], zr.at[m + 8 * h],
                column(m // 2, m % 2),
            )
        gp[:, at] = jnp.sum(
            total * jnp.where(slot_id < valid, s_blk[k].astype(F32), 0.0)[:, at], axis=0, keepdims=True
        )
        if h:
            for m in range(1, 8):
                send(gp, gz.at[g], ys.at[m], yr.at[m], column(m // 2, m % 2))
        for i in range(4 + 2 * h, 6 + 2 * h):
            head_block(i)
    rz[g] = rb[g]
    gz[g] = gp[...]
    for h in range(2):
        at = slice(h * part, (h + 1) * part)
        for m in range(1, 8):
            arrived(rz.at[source(m), :, at], zs.at[m + 8 * h], zr.at[m + 8 * h], column(m // 2, m % 2))
    own_cols = cols[pl.ds(pl.multiple_of(g * rows, 8), rows), :][:, 0:1]
    for h in range(2):
        at = slice(h * half_s, (h + 1) * half_s)
        ng = rz[h].astype(F32)
        for i in range(1, 4):
            ng = ng + rz[2 * i + h].astype(F32)
        hid = sh_ref[:, at].astype(F32)
        gh_ref[:, at] = (gain_ref[:, at] * ng - hid * own_cols).astype(BF16)
    for m in range(1, 8):
        arrived(gz.at[source(m)], ys.at[m], yr.at[m], column(m // 2, m % 2))
    for h in range(2):
        at = slice(h * half_s, (h + 1) * half_s)
        ng = gz[h]
        for i in range(1, 4):
            ng = ng + gz[2 * i + h]
        gg_ref[:, at] = ng
    for copy in head_copies:
        copy.wait()
    for copy in sends:
        copy.wait_send()


def finish(
    head_in, loss_in, hidden_in, gain_in, head_out, loss_out, hidden_out, gain_out,
    head, hidden, gain, loss, in_sem, out_sem,
):
    moves = [(head_in.at[i], head.at[i], head_out.at[i]) for i in range(8)]
    moves += [(hidden_in, hidden, hidden_out), (gain_in, gain, gain_out), (loss_in, loss, loss_out)]
    inward = [pltpu.make_async_copy(a, b, in_sem.at[i]) for i, (a, b, _) in enumerate(moves)]
    outward = [pltpu.make_async_copy(b, c, out_sem.at[i]) for i, (_, b, c) in enumerate(moves)]
    for copy in inward:
        copy.start()
    for first, second in zip(inward, outward):
        first.wait()
        second.start()
    for copy in outward:
        copy.wait()


def fused(
    student_hidden, norm_gain, teacher_hidden, student_head, teacher_head, episode_source, lengths
):
    rows, wide_s = student_hidden.shape
    wide_t = teacher_hidden.shape[1]
    tokens = rows * lax.axis_size("grp")
    voc = student_head.shape[1]
    half_s, half_t = wide_s // 2, wide_t // 2
    slots = -(-(tokens * 5 // 8 + 3) // 128) * 128
    vmem = pl.BlockSpec(memory_space=pltpu.VMEM)
    hbm = pl.BlockSpec(memory_space=pltpu.HBM)
    dma = pltpu.SemaphoreType.DMA
    loss, grad_hidden, grad_gain, grad_head = pl.pallas_call(
        kernel,
        out_shape=(
            jax.ShapeDtypeStruct((1, 1), F32),
            jax.ShapeDtypeStruct((rows, wide_s), BF16),
            jax.ShapeDtypeStruct((1, wide_s), F32),
            jax.ShapeDtypeStruct((8, half_s, voc), BF16),
        ),
        in_specs=[hbm] * 7,
        out_specs=(vmem, vmem, vmem, hbm),
        scratch_shapes=[
            pltpu.VMEM((8, half_s, voc), BF16),
            pltpu.VMEM((8, half_t, voc), BF16),
            pltpu.VMEM((rows, wide_s), BF16),
            pltpu.VMEM((1, wide_s), F32),
            pltpu.VMEM((1, episode_source.shape[0]), jnp.int32),
            pltpu.VMEM((1, episode_source.shape[0]), jnp.int32),
            pltpu.VMEM((slots, tokens), BF16),
            pltpu.VMEM((8, rows, half_s), BF16),
            pltpu.VMEM((8, rows, half_t), BF16),
            pltpu.VMEM((8, slots, half_s), BF16),
            pltpu.VMEM((8, slots, half_t), BF16),
            pltpu.VMEM((8, half_s, slots), BF16),
            pltpu.VMEM((slots, voc), F32),
            pltpu.VMEM((slots, voc), F32),
            pltpu.VMEM((slots, 128), F32),
            pltpu.VMEM((tokens, 128), F32),
            pltpu.VMEM((8, 8, slots), F32),
            pltpu.VMEM((4, 8, slots), F32),
            pltpu.VMEM((slots, voc), BF16),
            pltpu.VMEM((slots, half_s), F32),
            pltpu.VMEM((4, slots, half_s), BF16),
            pltpu.VMEM((4, slots, half_s), BF16),
            pltpu.VMEM((4, slots, half_s), BF16),
            pltpu.VMEM((4, slots, half_s), BF16),
            pltpu.VMEM((8, rows, half_s), BF16),
            pltpu.VMEM((8, rows, half_s), BF16),
            pltpu.VMEM((1, half_s), F32),
            pltpu.VMEM((8, 1, half_s), F32),
            pltpu.VMEM((8, half_s, voc), BF16),
            dma(()), dma(()), dma((8,)), dma((8,)),
        ] + [dma((8,))] * 16 + [dma((16,))] * 2 + [dma((8,))] * 2,
        compiler_params=pltpu.CompilerParams(
            collective_id=0, has_side_effects=True, vmem_limit_bytes=LIMIT * 1024
        ),
        cost_estimate=pl.CostEstimate(flops=2600000000, bytes_accessed=11000000, transcendentals=400000),
    )(
        student_hidden, teacher_hidden, norm_gain.reshape(1, -1),
        episode_source.reshape(1, -1), lengths.reshape(1, -1),
        student_head.reshape(8, half_s, voc), teacher_head.reshape(8, half_t, voc),
    )
    results = (grad_head, loss, grad_hidden, grad_gain)
    grad_head, loss, grad_hidden, grad_gain = pl.pallas_call(
        finish,
        out_shape=tuple(jax.ShapeDtypeStruct(r.shape, r.dtype) for r in results),
        in_specs=[hbm] * 4,
        out_specs=(hbm,) * 4,
        scratch_shapes=[
            pltpu.VMEM((8, half_s, voc), BF16),
            pltpu.VMEM((rows, wide_s), BF16),
            pltpu.VMEM((1, wide_s), F32),
            pltpu.VMEM((1, 1), F32),
            dma((11,)), dma((11,)),
        ],
        compiler_params=pltpu.CompilerParams(vmem_limit_bytes=LIMIT * 1024),
        cost_estimate=pl.CostEstimate(flops=0, bytes_accessed=6400000, transcendentals=0),
    )(*results)
    return (loss[0, 0], grad_hidden, grad_gain.reshape(-1), grad_head.reshape(student_head.shape))


def realign(teacher_hidden, table, group_index, per_group):
    groups = table.shape[0]
    source_group = table // per_group
    source_local = table % per_group
    mine = (source_group == group_index).astype(jnp.int32)
    earlier = jnp.cumsum(mine, axis=1) - mine
    slot_ids = jnp.arange(MOST, dtype=jnp.int32)
    matches = mine[:, :, None] * (earlier[:, :, None] == slot_ids[None, None, :]).astype(jnp.int32)
    send_index = jnp.sum(matches * source_local[:, :, None], axis=1)
    features = teacher_hidden.shape[1]
    episodes = teacher_hidden.reshape(per_group, SEQ, features)
    outgoing = jnp.take(episodes, send_index, axis=0)
    incoming = lax.all_to_all(outgoing, "grp", split_axis=0, concat_axis=0, tiled=True)
    own_groups = lax.dynamic_index_in_dim(source_group, group_index, 0, keepdims=False)
    matching = (own_groups[:, None] == own_groups[None, :]).astype(jnp.int32)
    position = jnp.sum(jnp.tril(matching, -1), axis=1)
    flat_index = own_groups * MOST + position
    received = incoming.reshape(groups * MOST, SEQ, features)
    return jnp.take(received, flat_index, axis=0).reshape(per_group * SEQ, features)


def local(
    student_hidden, norm_gain, teacher_hidden, student_head, teacher_head, episode_source, lengths
):
    groups = lax.axis_size("grp")
    group_index = lax.axis_index("grp")
    rows_group = student_hidden.shape[0]
    per_group = rows_group // SEQ
    hidden_f32 = student_hidden.astype(jnp.float32)
    squares = lax.psum(jnp.sum(hidden_f32 * hidden_f32, axis=1), "voc")
    inverse_rms = lax.rsqrt(squares / DS + EPSILON)
    normed = (hidden_f32 * inverse_rms[:, None] * norm_gain[None, :]).astype(jnp.bfloat16)
    table = episode_source.reshape(groups, per_group)
    aligned = realign(teacher_hidden, table, group_index, per_group)
    teacher_rows, student_rows = (
        lax.all_gather(aligned, "voc", axis=1, tiled=True),
        lax.all_gather(normed, "voc", axis=1, tiled=True),
    )
    teacher_logits = jnp.dot(
        lax.all_gather(teacher_rows, "grp", axis=0, tiled=True),
        teacher_head,
        preferred_element_type=jnp.float32,
    )
    positions = jnp.arange(SEQ, dtype=jnp.int32)
    all_rows = lax.all_gather(student_rows, "grp", axis=0, tiled=True)
    student_logits = jnp.dot(all_rows, student_head, preferred_element_type=jnp.float32)
    lengths_f32 = lengths.astype(jnp.float32)
    valid = positions[None, :] < lengths[:, None]
    token_weight = jnp.where(
        valid, 1.0 / lengths_f32[:, None], jnp.zeros_like(lengths_f32)[:, None]
    ).reshape(-1)
    top_student, top_teacher = lax.pmax(
        (jnp.max(student_logits, axis=1), jnp.max(teacher_logits, axis=1)), ("grp", "voc")
    )
    exp_student = jnp.exp(student_logits - top_student[:, None])
    exp_teacher = jnp.exp(teacher_logits - top_teacher[:, None])
    total_student, total_teacher = lax.psum(
        (jnp.sum(exp_student, axis=1), jnp.sum(exp_teacher, axis=1)), ("grp", "voc")
    )
    log_student = student_logits - (top_student + jnp.log(total_student))[:, None]
    log_teacher = teacher_logits - (top_teacher + jnp.log(total_teacher))[:, None]
    prob_student = jnp.exp(log_student)
    log_ratio = log_student - log_teacher
    divergence = lax.psum(jnp.sum(prob_student * log_ratio, axis=1), ("grp", "voc"))
    loss = jnp.sum(token_weight * divergence)
    logit_grad = (token_weight[:, None] * prob_student * (log_ratio - divergence[:, None])).astype(
        jnp.bfloat16
    )
    grad_head = lax.dot_general(
        all_rows, logit_grad, (((0,), (0,)), ((), ())), preferred_element_type=jnp.float32
    ).astype(jnp.bfloat16)
    full_term = lax.dot_general(
        logit_grad, student_head, (((1,), (1,)), ((), ())), preferred_element_type=jnp.float32
    )
    feature_part = lax.psum_scatter(
        full_term.astype(jnp.bfloat16), "voc", scatter_dimension=1, tiled=True
    )
    normed_grad = lax.psum_scatter(feature_part, "grp", scatter_dimension=0, tiled=True).astype(
        jnp.float32
    )
    scaled = normed_grad * norm_gain[None, :]
    inner = lax.psum(jnp.sum(scaled * hidden_f32, axis=1), "voc")
    grad_hidden = (
        inverse_rms[:, None] * scaled - hidden_f32 * (inverse_rms**3)[:, None] * inner[:, None] / DS
    )
    grad_gain = lax.psum(jnp.sum(normed_grad * hidden_f32 * inverse_rms[:, None], axis=0), "grp")
    return (loss, grad_hidden.astype(jnp.bfloat16), grad_gain, grad_head)


def solution(mesh):
    placed = (
        P("grp", "voc"),
        P("voc"),
        P("grp", "voc"),
        P(None, ("grp", "voc")),
        P(None, ("grp", "voc")),
        P(),
        P(),
    )
    body = fused if tuple(mesh.shape.values()) == (8, 4) else local
    return jax.shard_map(
        body,
        mesh=mesh,
        in_specs=placed,
        out_specs=(P(), P("grp", "voc"), P("voc"), P(None, ("grp", "voc"))),
        check_vma=False,
    )
```

```python
import functools

import jax
import jax.numpy as jnp
from jax import lax
from jax.experimental import pallas as pl
from jax.experimental.pallas import tpu as pltpu
from jax.sharding import PartitionSpec as P

DS = 4096
SEQ = 2
MOST = 2


EPSILON = 1e-06

F32 = jnp.float32
BF16 = jnp.bfloat16
LIMIT = 65472
MESH = pl.DeviceIdType.MESH


def flip(number, mask):
    low, high = number % 2, number // 2
    if mask & 1:
        low = 1 - low
    if mask & 2:
        high = 1 - high
    return high * 2 + low


def merge(parts):
    top = functools.reduce(jnp.maximum, [p[0:1] for p in parts])
    top_t = functools.reduce(jnp.maximum, [p[2:3] for p in parts])
    total = total_t = ratio = logit = both = 0.0
    for p in parts:
        shift, shift_t = p[0:1] - top, p[2:3] - top_t
        factor, factor_t = jnp.exp(shift), jnp.exp(shift_t)
        live = factor > 0.0
        shift = jnp.where(live, shift, 0.0)
        gap = shift - jnp.where(live, shift_t, 0.0)
        total = total + factor * p[1:2]
        total_t = total_t + factor_t * p[3:4]
        ratio = ratio + factor * (p[4:5] + p[1:2] * gap)
        logit = logit + factor * (p[5:6] + p[1:2] * shift)
        both = both + factor * (p[6:7] + gap * p[5:6] + shift * p[4:5] + shift * gap * p[1:2])
    return jnp.concatenate([top, total, top_t, total_t, ratio, logit, both, jnp.zeros_like(top)], axis=0)


def kernel(
    sh_hbm, th_hbm, gain_hbm, source_hbm, lengths_hbm, w_hbm, t_hbm,
    loss_ref, gh_ref, gg_ref, head_hbm,
    wv, tv, sh_ref, gain_ref, source_ref, lengths_ref, pick_ref, in_s, in_t, s_blk, t_blk, hg, s_acc, t_acc, sq, cols,
    st_a, st_b, g2, own, p_sib, r_sib, p_x, r_x, rb, rz, gp, gz, head,
    w_sem, t_sem, h_sem, l_sem, s1s, s1r, t1s, t1r, s2s, s2r, t2s, t2r, as_, ar, bs, br,
    qs, qr, xs, xr, zs, zr, ys, yr,
):
    g = lax.axis_index("grp")
    v = lax.axis_index("voc")
    z, c = g // 2, g % 2
    k = v * 2 + c
    rows, half_s = in_s.shape[1], in_s.shape[2]
    half_t = in_t.shape[2]
    tokens = in_s.shape[0] * rows
    valid = tokens * 5 // 8
    slots = s_acc.shape[0]

    def plane(vm, cm):
        return {"grp": z * 2 + (1 - c if cm else c), "voc": flip(v, vm)}

    def column(zm, cm):
        return {"grp": flip(z, zm) * 2 + (1 - c if cm else c), "voc": v}

    def slot(vm, cm):
        return flip(v, vm) * 2 + (1 - c if cm else c)

    sends = []

    def send(src, dst, ssem, rsem, to):
        copy = pltpu.make_async_remote_copy(
            src_ref=src, dst_ref=dst, send_sem=ssem, recv_sem=rsem, device_id=to, device_id_type=MESH
        )
        copy.start()
        sends.append(copy)

    def arrived(dst, ssem, rsem, to):
        pltpu.make_async_remote_copy(
            src_ref=dst, dst_ref=dst, send_sem=ssem, recv_sem=rsem, device_id=to, device_id_type=MESH
        ).wait_recv()

    def half(ref, number, width):
        return ref.at[:, pl.ds(pl.multiple_of(number * width, 128), width)]

    local_copies = [
        pltpu.make_async_copy(src, dst, l_sem.at[i])
        for i, (src, dst) in enumerate((
            (source_hbm, source_ref), (lengths_hbm, lengths_ref), (gain_hbm, gain_ref),
            (half(sh_hbm, c, half_s), in_s.at[g]), (half(th_hbm, c, half_t), in_t.at[g]), (sh_hbm, sh_ref),
        ))
    ]
    for copy in local_copies:
        copy.start()
    w_copy = pltpu.make_async_copy(w_hbm, wv, w_sem)
    t_copy = pltpu.make_async_copy(t_hbm, tv, t_sem)
    w_copy.start()
    t_copy.start()

    barrier = pltpu.get_barrier_semaphore()
    peers = [plane(m // 2, m % 2) for m in range(1, 8)] + [column(m // 2, m % 2) for m in range(2, 8)]
    for peer in peers:
        pl.semaphore_signal(barrier, inc=1, device_id=peer, device_id_type=MESH)
    pl.semaphore_wait(barrier, len(peers))

    for m in range(1, 8):
        other = 1 - c if m % 2 else c
        send(half(sh_hbm, other, half_s), in_s.at[g], s1s.at[m], s1r.at[m], column(m // 2, m % 2))
    for m in range(1, 8):
        other = 1 - c if m % 2 else c
        send(half(th_hbm, other, half_t), in_t.at[g], t1s.at[m], t1r.at[m], column(m // 2, m % 2))

    for copy in local_copies[:3]:
        copy.wait()
    episodes = source_ref.shape[1]
    line = lax.broadcasted_iota(jnp.int32, (8, episodes), 0)
    table = jnp.where(line == 0, source_ref[...], jnp.where(line == 1, lengths_ref[...], 0)).astype(F32).astype(BF16)
    spread = lax.broadcasted_iota(jnp.int32, (episodes, tokens), 1) // SEQ == lax.broadcasted_iota(
        jnp.int32, (episodes, tokens), 0
    )
    table = jnp.dot(table, spread.astype(F32).astype(BF16), preferred_element_type=F32)
    position = (lax.broadcasted_iota(jnp.int32, (1, tokens), 1) % SEQ).astype(F32)
    row_source = table[0:1] * SEQ + position
    row_length = table[1:2]
    row_valid = (position < row_length).astype(F32)
    before = lax.broadcasted_iota(jnp.int32, (tokens, tokens), 0) < lax.broadcasted_iota(jnp.int32, (tokens, tokens), 1)
    rank = jnp.dot(
        jnp.broadcast_to(row_valid, (8, tokens)).astype(BF16), before.astype(F32).astype(BF16),
        preferred_element_type=F32,
    )[0:1]
    slot_line = lax.broadcasted_iota(jnp.int32, (slots, tokens), 0).astype(F32)
    pick = jnp.where(slot_line == rank, row_valid, 0.0).astype(BF16)
    pick_ref[...] = pick
    line = lax.broadcasted_iota(jnp.int32, (8, tokens), 0)
    both = jnp.where(line == 0, row_source, jnp.where(line == 1, row_length, 0.0)).astype(BF16)
    slot_table = lax.dot_general(pick, both, (((1,), (1,)), ((), ())), preferred_element_type=F32)
    slot_source, slot_length = slot_table[:, 0:1], slot_table[:, 1:2]
    weight = jnp.where(slot_length > 0.0, 1.0 / jnp.maximum(slot_length, 1.0), 0.0)
    teacher_lane = lax.broadcasted_iota(jnp.int32, (slots, tokens), 1).astype(F32)
    pick_t = jnp.where((slot_source == teacher_lane) & (slot_length > 0.0), 1.0, 0.0).astype(BF16)

    gain = gain_ref[...]
    own_gain = jnp.where(c == 0, gain[:, :half_s], gain[:, half_s:])
    hi = own_gain.astype(BF16).astype(F32)
    mid = (own_gain - hi).astype(BF16).astype(F32)
    lo = own_gain - hi - mid
    slot_id = lax.broadcasted_iota(jnp.int32, (slots, half_s), 0)
    gain_rows = jnp.where(
        slot_id == valid, hi, jnp.where(slot_id == valid + 1, mid, jnp.where(slot_id == valid + 2, lo, 0.0))
    )

    def source(m):
        return flip(z, m // 2) * 2 + (1 - c if m % 2 else c)

    halves = (slice(0, slots // 2), slice(slots // 2, slots))

    def share(blk, ssem, rsem):
        for vm, half_id in ((1, 0), (2, 1), (1, 1), (2, 0)):
            piece = blk.at[k, halves[half_id]]
            send(piece, piece, ssem.at[vm * 4 + half_id], rsem.at[vm * 4 + half_id], plane(vm, 0))
        send(blk.at[k], blk.at[k], ssem.at[2], rsem.at[2], plane(0, 1))

    def landed(blk, ssem, rsem, vm, half_id):
        piece = blk.at[slot(vm, 0), halves[half_id]]
        arrived(piece, ssem.at[vm * 4 + half_id], rsem.at[vm * 4 + half_id], plane(vm, 0))
        return piece

    def relay(blk, ssem, rsem):
        for vm, half_id in ((1, 0), (2, 1)):
            piece = landed(blk, ssem, rsem, vm, half_id)
            send(piece, piece, ssem.at[12 + half_id], rsem.at[12 + half_id], plane(3 - vm, 0))

    def to_sibling(blk, ssem, rsem, vm):
        for half_id in {1: (1,), 2: (0,), 3: (0, 1)}[vm]:
            landed(blk, ssem, rsem, vm, half_id)
        at = slot(vm, 0)
        send(blk.at[at], blk.at[at], ssem.at[vm * 4 + 2], rsem.at[vm * 4 + 2], plane(0, 1))

    def sibling(blk, ssem, rsem, vm):
        arrived(blk.at[slot(vm, 1)], ssem.at[vm * 4 + 2], rsem.at[vm * 4 + 2], plane(0, 1))

    for m in range(1, 8):
        arrived(in_s.at[source(m)], s1s.at[m], s1r.at[m], column(m // 2, m % 2))
    for copy in local_copies[3:]:
        copy.wait()
    block = jnp.concatenate([in_s[i].astype(F32) for i in range(8)], axis=0).astype(BF16)
    block = jnp.dot(pick, block, preferred_element_type=F32)
    s_blk[k] = jnp.where(slot_id < valid, block, gain_rows).astype(BF16)
    share(s_blk, s2s, s2r)
    s_acc[...] = jnp.zeros_like(s_acc)
    t_acc[...] = jnp.zeros_like(t_acc)
    sq[...] = jnp.zeros_like(sq)

    def student_block(at):
        x = s_blk[at].astype(F32)
        scale = jnp.sum(x[valid:], axis=0, keepdims=True)
        x = jnp.where(slot_id < valid, x, 0.0)
        squares = x * x
        partial = squares[:, 0:128]
        for i in range(1, half_s // 128):
            partial = partial + squares[:, i * 128:(i + 1) * 128]
        sq[...] += partial
        scaled = x * scale
        hg[at] = jnp.transpose(scaled).astype(BF16)
        s_acc[...] += jnp.dot(scaled.astype(BF16), wv[at], preferred_element_type=F32)

    def teacher_block(at):
        t_acc[...] += jnp.dot(t_blk[at], tv[at], preferred_element_type=F32)

    w_copy.wait()
    student_block(k)
    sibling(s_blk, s2s, s2r, 0)
    student_block(slot(0, 1))
    relay(s_blk, s2s, s2r)
    for m in range(1, 8):
        arrived(in_t.at[source(m)], t1s.at[m], t1r.at[m], column(m // 2, m % 2))
    block = jnp.concatenate([in_t[i].astype(F32) for i in range(8)], axis=0).astype(BF16)
    t_blk[k] = jnp.dot(pick_t, block, preferred_element_type=F32).astype(BF16)
    share(t_blk, t2s, t2r)

    to_sibling(s_blk, s2s, s2r, 1)
    to_sibling(s_blk, s2s, s2r, 2)
    t_copy.wait()
    teacher_block(k)
    student_block(slot(1, 0))
    student_block(slot(2, 0))
    relay(t_blk, t2s, t2r)
    sibling(s_blk, s2s, s2r, 1)
    student_block(slot(1, 1))
    sibling(s_blk, s2s, s2r, 2)
    student_block(slot(2, 1))
    to_sibling(s_blk, s2s, s2r, 3)
    student_block(slot(3, 0))
    sibling(t_blk, t2s, t2r, 0)
    teacher_block(slot(0, 1))
    to_sibling(t_blk, t2s, t2r, 1)
    to_sibling(t_blk, t2s, t2r, 2)
    sibling(s_blk, s2s, s2r, 3)
    student_block(slot(3, 1))
    teacher_block(slot(1, 0))
    teacher_block(slot(2, 0))
    for vm in (1, 2):
        sibling(t_blk, t2s, t2r, vm)
        teacher_block(slot(vm, 1))
    to_sibling(t_blk, t2s, t2r, 3)
    teacher_block(slot(3, 0))
    sibling(t_blk, t2s, t2r, 3)
    teacher_block(slot(3, 1))

    inv = lax.rsqrt(jnp.sum(sq[...], axis=1, keepdims=True) / DS + EPSILON)
    s_log = s_acc[...] * inv
    t_log = t_acc[...]
    top = jnp.max(s_log, axis=1, keepdims=True)
    top_t = jnp.max(t_log, axis=1, keepdims=True)
    a = s_log - top
    b = t_log - top_t
    e = jnp.exp(a)
    ea = e * a
    d = a - b
    figures = [
        top, jnp.sum(e, axis=1, keepdims=True), top_t, jnp.sum(jnp.exp(b), axis=1, keepdims=True),
        jnp.sum(e * d, axis=1, keepdims=True), jnp.sum(ea, axis=1, keepdims=True),
        jnp.sum(ea * d, axis=1, keepdims=True),
    ]
    lane = lax.broadcasted_iota(jnp.int32, (slots, 128), 1)
    packed = jnp.zeros((slots, 128), F32)
    for i, figure in enumerate(figures):
        packed = jnp.where(lane == i, figure, packed)
    st_a[k] = jnp.transpose(packed)[0:8, :]
    for m in range(1, 8):
        send(st_a.at[k], st_a.at[k], as_.at[m], ar.at[m], plane(m // 2, m % 2))
    for m in range(1, 8):
        arrived(st_a.at[slot(m // 2, m % 2)], as_.at[m], ar.at[m], plane(m // 2, m % 2))
    st_b[z] = merge([st_a[i] for i in range(8)])
    for m in range(1, 4):
        send(st_b.at[z], st_b.at[z], bs.at[m], br.at[m], column(m, 0))
    for m in range(1, 4):
        arrived(st_b.at[flip(z, m)], bs.at[m], br.at[m], column(m, 0))
    full = merge([st_b[i] for i in range(4)])
    total = full[1:2]
    lse = full[0:1] + jnp.log(total)
    lse_t = full[2:3] + jnp.log(full[3:4])
    mean_ratio, mean_logit = full[4:5] / total, full[5:6] / total
    divergence = mean_ratio - jnp.log(total) + jnp.log(full[3:4])
    offset = lse - lse_t + divergence
    cov = full[6:7] / total - mean_ratio * mean_logit
    back = jnp.concatenate([lse, offset, divergence, cov, jnp.zeros((slots - 4, slots), F32)], axis=0)
    back = jnp.transpose(back)
    prob = jnp.exp(s_log - back[:, 0:1])
    grad = ((weight * inv) * prob * (s_log - t_log - back[:, 1:2])).astype(BF16)
    g2[...] = grad

    def block_grad(at):
        return lax.dot_general(g2[...], wv[at], (((1,), (1,)), ((), ())), preferred_element_type=F32)

    order = (1, 2, 3, 0)
    part = half_s // 2
    for vm in order:
        p_sib[vm] = block_grad(slot(vm, 1)).astype(BF16)
        send(p_sib.at[vm], r_sib.at[vm], qs.at[vm], qr.at[vm], plane(0, 1))
    for vm in order:
        mine = block_grad(slot(vm, 0))
        arrived(r_sib.at[vm], qs.at[vm], qr.at[vm], plane(0, 1))
        mine = mine + r_sib[vm].astype(F32)
        if vm:
            p_x[vm] = mine.astype(BF16)
            send(p_x.at[vm, :, 0:part], r_x.at[vm, :, 0:part], xs.at[vm], xr.at[vm], plane(vm, 0))
        else:
            own[...] = mine
    for vm in (1, 2, 3):
        send(p_x.at[vm, :, part:], r_x.at[vm, :, part:], xs.at[vm + 4], xr.at[vm + 4], plane(vm, 0))

    loss_ref[...] = jnp.sum(weight * back[:, 2:3], axis=0, keepdims=True)
    lane = lax.broadcasted_iota(jnp.int32, (slots, 128), 1)
    figure = weight * inv * inv * back[:, 3:4] / DS
    hi = figure.astype(BF16).astype(F32)
    mid = (figure - hi).astype(BF16).astype(F32)
    lo = figure - hi - mid
    packed = jnp.where(lane == 0, hi, jnp.where(lane == 1, mid, jnp.where(lane == 2, lo, 0.0))).astype(BF16)
    packed = lax.dot_general(pick_ref[...], packed, (((0,), (0,)), ((), ())), preferred_element_type=F32)
    cols[...] = jnp.broadcast_to(jnp.sum(packed, axis=1, keepdims=True), cols.shape)

    def head_block(i):
        head[i] = jnp.dot(hg[i], g2[...], preferred_element_type=F32).astype(BF16)
        copy = pltpu.make_async_copy(head.at[i], head_hbm.at[i], h_sem.at[i])
        copy.start()
        head_copies.append(copy)

    head_copies = []
    for i in range(4):
        head_block(i)
    for h in range(2):
        at = slice(h * part, (h + 1) * part)
        for vm in (1, 2, 3):
            arrived(r_x.at[vm, :, at], xs.at[vm + 4 * h], xr.at[vm + 4 * h], plane(vm, 0))
        total = own[:, at]
        for vm in (1, 2, 3):
            total = total + r_x[vm, :, at].astype(F32)
        spread_out = lax.dot_general(
            pick_ref[...], total.astype(BF16), (((0,), (0,)), ((), ())), preferred_element_type=F32
        )
        for i in range(8):
            rb[i, :, at] = spread_out[i * rows:(i + 1) * rows].astype(BF16)
        for m in range(1, 8):
            send(
                rb.at[source(m), :, at], rz.at[g, :, at], zs.at[m + 8 * h], zr.at[m + 8 * h],
                column(m // 2, m % 2),
            )
        gp[:, at] = jnp.sum(
            total * jnp.where(slot_id < valid, s_blk[k].astype(F32), 0.0)[:, at], axis=0, keepdims=True
        )
        if h:
            for m in range(1, 8):
                send(gp, gz.at[g], ys.at[m], yr.at[m], column(m // 2, m % 2))
        for i in range(4 + 2 * h, 6 + 2 * h):
            head_block(i)
    rz[g] = rb[g]
    gz[g] = gp[...]
    for h in range(2):
        at = slice(h * part, (h + 1) * part)
        for m in range(1, 8):
            arrived(rz.at[source(m), :, at], zs.at[m + 8 * h], zr.at[m + 8 * h], column(m // 2, m % 2))
    own_cols = cols[pl.ds(pl.multiple_of(g * rows, 8), rows), :][:, 0:1]
    for h in range(2):
        at = slice(h * half_s, (h + 1) * half_s)
        ng = rz[h].astype(F32)
        for i in range(1, 4):
            ng = ng + rz[2 * i + h].astype(F32)
        hid = sh_ref[:, at].astype(F32)
        gh_ref[:, at] = (gain_ref[:, at] * ng - hid * own_cols).astype(BF16)
    for m in range(1, 8):
        arrived(gz.at[source(m)], ys.at[m], yr.at[m], column(m // 2, m % 2))
    for h in range(2):
        at = slice(h * half_s, (h + 1) * half_s)
        ng = gz[h]
        for i in range(1, 4):
            ng = ng + gz[2 * i + h]
        gg_ref[:, at] = ng
    for copy in head_copies:
        copy.wait()
    for copy in sends:
        copy.wait_send()


def finish(
    head_in, loss_in, hidden_in, gain_in, head_out, loss_out, hidden_out, gain_out,
    head, hidden, gain, loss, in_sem, out_sem,
):
    moves = [(head_in.at[i], head.at[i], head_out.at[i]) for i in range(8)]
    moves += [(hidden_in, hidden, hidden_out), (gain_in, gain, gain_out), (loss_in, loss, loss_out)]
    inward = [pltpu.make_async_copy(a, b, in_sem.at[i]) for i, (a, b, _) in enumerate(moves)]
    outward = [pltpu.make_async_copy(b, c, out_sem.at[i]) for i, (_, b, c) in enumerate(moves)]
    for copy in inward:
        copy.start()
    for first, second in zip(inward, outward):
        first.wait()
        second.start()
    for copy in outward:
        copy.wait()


def fused(
    student_hidden, norm_gain, teacher_hidden, student_head, teacher_head, episode_source, lengths
):
    rows, wide_s = student_hidden.shape
    wide_t = teacher_hidden.shape[1]
    tokens = rows * lax.axis_size("grp")
    voc = student_head.shape[1]
    half_s, half_t = wide_s // 2, wide_t // 2
    slots = -(-(tokens * 5 // 8 + 3) // 128) * 128
    vmem = pl.BlockSpec(memory_space=pltpu.VMEM)
    hbm = pl.BlockSpec(memory_space=pltpu.HBM)
    dma = pltpu.SemaphoreType.DMA
    loss, grad_hidden, grad_gain, grad_head = pl.pallas_call(
        kernel,
        out_shape=(
            jax.ShapeDtypeStruct((1, 1), F32),
            jax.ShapeDtypeStruct((rows, wide_s), BF16),
            jax.ShapeDtypeStruct((1, wide_s), F32),
            jax.ShapeDtypeStruct((8, half_s, voc), BF16),
        ),
        in_specs=[hbm] * 7,
        out_specs=(vmem, vmem, vmem, hbm),
        scratch_shapes=[
            pltpu.VMEM((8, half_s, voc), BF16),
            pltpu.VMEM((8, half_t, voc), BF16),
            pltpu.VMEM((rows, wide_s), BF16),
            pltpu.VMEM((1, wide_s), F32),
            pltpu.VMEM((1, episode_source.shape[0]), jnp.int32),
            pltpu.VMEM((1, episode_source.shape[0]), jnp.int32),
            pltpu.VMEM((slots, tokens), BF16),
            pltpu.VMEM((8, rows, half_s), BF16),
            pltpu.VMEM((8, rows, half_t), BF16),
            pltpu.VMEM((8, slots, half_s), BF16),
            pltpu.VMEM((8, slots, half_t), BF16),
            pltpu.VMEM((8, half_s, slots), BF16),
            pltpu.VMEM((slots, voc), F32),
            pltpu.VMEM((slots, voc), F32),
            pltpu.VMEM((slots, 128), F32),
            pltpu.VMEM((tokens, 128), F32),
            pltpu.VMEM((8, 8, slots), F32),
            pltpu.VMEM((4, 8, slots), F32),
            pltpu.VMEM((slots, voc), BF16),
            pltpu.VMEM((slots, half_s), F32),
            pltpu.VMEM((4, slots, half_s), BF16),
            pltpu.VMEM((4, slots, half_s), BF16),
            pltpu.VMEM((4, slots, half_s), BF16),
            pltpu.VMEM((4, slots, half_s), BF16),
            pltpu.VMEM((8, rows, half_s), BF16),
            pltpu.VMEM((8, rows, half_s), BF16),
            pltpu.VMEM((1, half_s), F32),
            pltpu.VMEM((8, 1, half_s), F32),
            pltpu.VMEM((8, half_s, voc), BF16),
            dma(()), dma(()), dma((8,)), dma((8,)),
        ] + [dma((8,))] * 4 + [dma((16,))] * 4 + [dma((8,))] * 8 + [dma((16,))] * 2 + [dma((8,))] * 2,
        compiler_params=pltpu.CompilerParams(
            collective_id=0, has_side_effects=True, vmem_limit_bytes=LIMIT * 1024
        ),
        cost_estimate=pl.CostEstimate(flops=2600000000, bytes_accessed=11000000, transcendentals=400000),
    )(
        student_hidden, teacher_hidden, norm_gain.reshape(1, -1),
        episode_source.reshape(1, -1), lengths.reshape(1, -1),
        student_head.reshape(8, half_s, voc), teacher_head.reshape(8, half_t, voc),
    )
    results = (grad_head, loss, grad_hidden, grad_gain)
    grad_head, loss, grad_hidden, grad_gain = pl.pallas_call(
        finish,
        out_shape=tuple(jax.ShapeDtypeStruct(r.shape, r.dtype) for r in results),
        in_specs=[hbm] * 4,
        out_specs=(hbm,) * 4,
        scratch_shapes=[
            pltpu.VMEM((8, half_s, voc), BF16),
            pltpu.VMEM((rows, wide_s), BF16),
            pltpu.VMEM((1, wide_s), F32),
            pltpu.VMEM((1, 1), F32),
            dma((11,)), dma((11,)),
        ],
        compiler_params=pltpu.CompilerParams(vmem_limit_bytes=LIMIT * 1024),
        cost_estimate=pl.CostEstimate(flops=0, bytes_accessed=6400000, transcendentals=0),
    )(*results)
    return (loss[0, 0], grad_hidden, grad_gain.reshape(-1), grad_head.reshape(student_head.shape))


def realign(teacher_hidden, table, group_index, per_group):
    groups = table.shape[0]
    source_group = table // per_group
    source_local = table % per_group
    mine = (source_group == group_index).astype(jnp.int32)
    earlier = jnp.cumsum(mine, axis=1) - mine
    slot_ids = jnp.arange(MOST, dtype=jnp.int32)
    matches = mine[:, :, None] * (earlier[:, :, None] == slot_ids[None, None, :]).astype(jnp.int32)
    send_index = jnp.sum(matches * source_local[:, :, None], axis=1)
    features = teacher_hidden.shape[1]
    episodes = teacher_hidden.reshape(per_group, SEQ, features)
    outgoing = jnp.take(episodes, send_index, axis=0)
    incoming = lax.all_to_all(outgoing, "grp", split_axis=0, concat_axis=0, tiled=True)
    own_groups = lax.dynamic_index_in_dim(source_group, group_index, 0, keepdims=False)
    matching = (own_groups[:, None] == own_groups[None, :]).astype(jnp.int32)
    position = jnp.sum(jnp.tril(matching, -1), axis=1)
    flat_index = own_groups * MOST + position
    received = incoming.reshape(groups * MOST, SEQ, features)
    return jnp.take(received, flat_index, axis=0).reshape(per_group * SEQ, features)


def local(
    student_hidden, norm_gain, teacher_hidden, student_head, teacher_head, episode_source, lengths
):
    groups = lax.axis_size("grp")
    group_index = lax.axis_index("grp")
    rows_group = student_hidden.shape[0]
    per_group = rows_group // SEQ
    hidden_f32 = student_hidden.astype(jnp.float32)
    squares = lax.psum(jnp.sum(hidden_f32 * hidden_f32, axis=1), "voc")
    inverse_rms = lax.rsqrt(squares / DS + EPSILON)
    normed = (hidden_f32 * inverse_rms[:, None] * norm_gain[None, :]).astype(jnp.bfloat16)
    table = episode_source.reshape(groups, per_group)
    aligned = realign(teacher_hidden, table, group_index, per_group)
    teacher_rows, student_rows = (
        lax.all_gather(aligned, "voc", axis=1, tiled=True),
        lax.all_gather(normed, "voc", axis=1, tiled=True),
    )
    teacher_logits = jnp.dot(
        lax.all_gather(teacher_rows, "grp", axis=0, tiled=True),
        teacher_head,
        preferred_element_type=jnp.float32,
    )
    positions = jnp.arange(SEQ, dtype=jnp.int32)
    all_rows = lax.all_gather(student_rows, "grp", axis=0, tiled=True)
    student_logits = jnp.dot(all_rows, student_head, preferred_element_type=jnp.float32)
    lengths_f32 = lengths.astype(jnp.float32)
    valid = positions[None, :] < lengths[:, None]
    token_weight = jnp.where(
        valid, 1.0 / lengths_f32[:, None], jnp.zeros_like(lengths_f32)[:, None]
    ).reshape(-1)
    top_student, top_teacher = lax.pmax(
        (jnp.max(student_logits, axis=1), jnp.max(teacher_logits, axis=1)), ("grp", "voc")
    )
    exp_student = jnp.exp(student_logits - top_student[:, None])
    exp_teacher = jnp.exp(teacher_logits - top_teacher[:, None])
    total_student, total_teacher = lax.psum(
        (jnp.sum(exp_student, axis=1), jnp.sum(exp_teacher, axis=1)), ("grp", "voc")
    )
    log_student = student_logits - (top_student + jnp.log(total_student))[:, None]
    log_teacher = teacher_logits - (top_teacher + jnp.log(total_teacher))[:, None]
    prob_student = jnp.exp(log_student)
    log_ratio = log_student - log_teacher
    divergence = lax.psum(jnp.sum(prob_student * log_ratio, axis=1), ("grp", "voc"))
    loss = jnp.sum(token_weight * divergence)
    logit_grad = (token_weight[:, None] * prob_student * (log_ratio - divergence[:, None])).astype(
        jnp.bfloat16
    )
    grad_head = lax.dot_general(
        all_rows, logit_grad, (((0,), (0,)), ((), ())), preferred_element_type=jnp.float32
    ).astype(jnp.bfloat16)
    full_term = lax.dot_general(
        logit_grad, student_head, (((1,), (1,)), ((), ())), preferred_element_type=jnp.float32
    )
    feature_part = lax.psum_scatter(
        full_term.astype(jnp.bfloat16), "voc", scatter_dimension=1, tiled=True
    )
    normed_grad = lax.psum_scatter(feature_part, "grp", scatter_dimension=0, tiled=True).astype(
        jnp.float32
    )
    scaled = normed_grad * norm_gain[None, :]
    inner = lax.psum(jnp.sum(scaled * hidden_f32, axis=1), "voc")
    grad_hidden = (
        inverse_rms[:, None] * scaled - hidden_f32 * (inverse_rms**3)[:, None] * inner[:, None] / DS
    )
    grad_gain = lax.psum(jnp.sum(normed_grad * hidden_f32 * inverse_rms[:, None], axis=0), "grp")
    return (loss, grad_hidden.astype(jnp.bfloat16), grad_gain, grad_head)


def solution(mesh):
    placed = (
        P("grp", "voc"),
        P("voc"),
        P("grp", "voc"),
        P(None, ("grp", "voc")),
        P(None, ("grp", "voc")),
        P(),
        P(),
    )
    body = fused if tuple(mesh.shape.values()) == (8, 4) else local
    return jax.shard_map(
        body,
        mesh=mesh,
        in_specs=placed,
        out_specs=(P(), P("grp", "voc"), P("voc"), P(None, ("grp", "voc"))),
        check_vma=False,
    )
```

```python
import functools

import jax
import jax.numpy as jnp
from jax import lax
from jax.experimental import pallas as pl
from jax.experimental.pallas import tpu as pltpu
from jax.sharding import PartitionSpec as P

DS = 4096
SEQ = 2
MOST = 2


EPSILON = 1e-06

F32 = jnp.float32
BF16 = jnp.bfloat16
LIMIT = 65472
MESH = pl.DeviceIdType.MESH


def flip(number, mask):
    low, high = number % 2, number // 2
    if mask & 1:
        low = 1 - low
    if mask & 2:
        high = 1 - high
    return high * 2 + low


def merge(parts):
    top = functools.reduce(jnp.maximum, [p[0:1] for p in parts])
    top_t = functools.reduce(jnp.maximum, [p[2:3] for p in parts])
    total = total_t = ratio = logit = both = 0.0
    for p in parts:
        shift, shift_t = p[0:1] - top, p[2:3] - top_t
        factor, factor_t = jnp.exp(shift), jnp.exp(shift_t)
        live = factor > 0.0
        shift = jnp.where(live, shift, 0.0)
        gap = shift - jnp.where(live, shift_t, 0.0)
        total = total + factor * p[1:2]
        total_t = total_t + factor_t * p[3:4]
        ratio = ratio + factor * (p[4:5] + p[1:2] * gap)
        logit = logit + factor * (p[5:6] + p[1:2] * shift)
        both = both + factor * (p[6:7] + gap * p[5:6] + shift * p[4:5] + shift * gap * p[1:2])
    return jnp.concatenate([top, total, top_t, total_t, ratio, logit, both, jnp.zeros_like(top)], axis=0)


def kernel(
    sh_hbm, th_hbm, gain_hbm, source_hbm, lengths_hbm, w_hbm, t_hbm,
    loss_ref, gh_ref, gg_ref, head_hbm,
    wv, tv, sh_ref, gain_ref, source_ref, lengths_ref, pick_ref, in_s, in_t, s_blk, t_blk, hg, s_acc, t_acc, raw, cols,
    st_a, st_b, g2, own, p_sib, r_sib, p_x, r_x, rb, rz, gp, gz, head,
    w_sem, t_sem, h_sem, l_sem, s1s, s1r, t1s, t1r, s2s, s2r, t2s, t2r, as_, ar, bs, br,
    qs, qr, xs, xr, zs, zr, ys, yr,
):
    g = lax.axis_index("grp")
    v = lax.axis_index("voc")
    z, c = g // 2, g % 2
    k = v * 2 + c
    rows, half_s = in_s.shape[1], in_s.shape[2]
    half_t = in_t.shape[2]
    tokens = in_s.shape[0] * rows
    valid = tokens * 5 // 8
    slots = s_acc.shape[0]

    def plane(vm, cm):
        return {"grp": z * 2 + (1 - c if cm else c), "voc": flip(v, vm)}

    def column(zm, cm):
        return {"grp": flip(z, zm) * 2 + (1 - c if cm else c), "voc": v}

    def slot(vm, cm):
        return flip(v, vm) * 2 + (1 - c if cm else c)

    sends = []

    def send(src, dst, ssem, rsem, to):
        copy = pltpu.make_async_remote_copy(
            src_ref=src, dst_ref=dst, send_sem=ssem, recv_sem=rsem, device_id=to, device_id_type=MESH
        )
        copy.start()
        sends.append(copy)

    def arrived(dst, ssem, rsem, to):
        pltpu.make_async_remote_copy(
            src_ref=dst, dst_ref=dst, send_sem=ssem, recv_sem=rsem, device_id=to, device_id_type=MESH
        ).wait_recv()

    def half(ref, number, width):
        return ref.at[:, pl.ds(pl.multiple_of(number * width, 128), width)]

    local_copies = [
        pltpu.make_async_copy(src, dst, l_sem.at[i])
        for i, (src, dst) in enumerate((
            (source_hbm, source_ref), (lengths_hbm, lengths_ref), (gain_hbm, gain_ref),
            (half(sh_hbm, c, half_s), in_s.at[g]), (half(th_hbm, c, half_t), in_t.at[g]), (sh_hbm, sh_ref),
        ))
    ]
    for copy in local_copies:
        copy.start()
    w_copy = pltpu.make_async_copy(w_hbm, wv, w_sem)
    t_copy = pltpu.make_async_copy(t_hbm, tv, t_sem)
    w_copy.start()
    t_copy.start()

    barrier = pltpu.get_barrier_semaphore()
    peers = [plane(m // 2, m % 2) for m in range(1, 8)] + [column(m // 2, m % 2) for m in range(2, 8)]
    for peer in peers:
        pl.semaphore_signal(barrier, inc=1, device_id=peer, device_id_type=MESH)
    pl.semaphore_wait(barrier, len(peers))

    for m in range(1, 8):
        other = 1 - c if m % 2 else c
        send(half(sh_hbm, other, half_s), in_s.at[g], s1s.at[m], s1r.at[m], column(m // 2, m % 2))
    for m in range(1, 8):
        other = 1 - c if m % 2 else c
        send(half(th_hbm, other, half_t), in_t.at[g], t1s.at[m], t1r.at[m], column(m // 2, m % 2))

    for copy in local_copies[:3]:
        copy.wait()
    episodes = source_ref.shape[1]
    line = lax.broadcasted_iota(jnp.int32, (8, episodes), 0)
    table = jnp.where(line == 0, source_ref[...], jnp.where(line == 1, lengths_ref[...], 0)).astype(F32).astype(BF16)
    spread = lax.broadcasted_iota(jnp.int32, (episodes, tokens), 1) // SEQ == lax.broadcasted_iota(
        jnp.int32, (episodes, tokens), 0
    )
    table = jnp.dot(table, spread.astype(F32).astype(BF16), preferred_element_type=F32)
    position = (lax.broadcasted_iota(jnp.int32, (1, tokens), 1) % SEQ).astype(F32)
    row_source = table[0:1] * SEQ + position
    row_length = table[1:2]
    row_valid = (position < row_length).astype(F32)
    before = lax.broadcasted_iota(jnp.int32, (tokens, tokens), 0) < lax.broadcasted_iota(jnp.int32, (tokens, tokens), 1)
    rank = jnp.dot(
        jnp.broadcast_to(row_valid, (8, tokens)).astype(BF16), before.astype(F32).astype(BF16),
        preferred_element_type=F32,
    )[0:1]
    slot_line = lax.broadcasted_iota(jnp.int32, (slots, tokens), 0).astype(F32)
    pick = jnp.where(slot_line == rank, row_valid, 0.0).astype(BF16)
    pick_ref[...] = pick
    line = lax.broadcasted_iota(jnp.int32, (8, tokens), 0)
    both = jnp.where(line == 0, row_source, jnp.where(line == 1, row_length, 0.0)).astype(BF16)
    slot_table = lax.dot_general(pick, both, (((1,), (1,)), ((), ())), preferred_element_type=F32)
    slot_source, slot_length = slot_table[:, 0:1], slot_table[:, 1:2]
    weight = jnp.where(slot_length > 0.0, 1.0 / jnp.maximum(slot_length, 1.0), 0.0)
    teacher_lane = lax.broadcasted_iota(jnp.int32, (slots, tokens), 1).astype(F32)
    pick_t = jnp.where((slot_source == teacher_lane) & (slot_length > 0.0), 1.0, 0.0).astype(BF16)

    gain = gain_ref[...]
    own_gain = jnp.where(c == 0, gain[:, :half_s], gain[:, half_s:])
    slot_id = lax.broadcasted_iota(jnp.int32, (slots, half_s), 0)

    def source(m):
        return flip(z, m // 2) * 2 + (1 - c if m % 2 else c)

    halves = (slice(0, slots // 2), slice(slots // 2, slots))

    def share(blk, ssem, rsem):
        for vm, half_id in ((1, 0), (2, 1), (1, 1), (2, 0)):
            piece = blk.at[k, halves[half_id]]
            send(piece, piece, ssem.at[vm * 4 + half_id], rsem.at[vm * 4 + half_id], plane(vm, 0))
        send(blk.at[k], blk.at[k], ssem.at[2], rsem.at[2], plane(0, 1))

    def landed(blk, ssem, rsem, vm, half_id):
        piece = blk.at[slot(vm, 0), halves[half_id]]
        arrived(piece, ssem.at[vm * 4 + half_id], rsem.at[vm * 4 + half_id], plane(vm, 0))
        return piece

    def relay(blk, ssem, rsem):
        for vm, half_id in ((1, 0), (2, 1)):
            piece = landed(blk, ssem, rsem, vm, half_id)
            send(piece, piece, ssem.at[12 + half_id], rsem.at[12 + half_id], plane(3 - vm, 0))

    def to_sibling(blk, ssem, rsem, vm):
        for half_id in {1: (1,), 2: (0,), 3: (0, 1)}[vm]:
            landed(blk, ssem, rsem, vm, half_id)
        at = slot(vm, 0)
        send(blk.at[at], blk.at[at], ssem.at[vm * 4 + 2], rsem.at[vm * 4 + 2], plane(0, 1))

    def sibling(blk, ssem, rsem, vm):
        arrived(blk.at[slot(vm, 1)], ssem.at[vm * 4 + 2], rsem.at[vm * 4 + 2], plane(0, 1))

    for m in range(1, 8):
        arrived(in_s.at[source(m)], s1s.at[m], s1r.at[m], column(m // 2, m % 2))
    for copy in local_copies[3:]:
        copy.wait()
    block = jnp.concatenate([in_s[i].astype(F32) for i in range(8)], axis=0).astype(BF16)
    block = jnp.dot(pick, block, preferred_element_type=F32)
    raw[...] = block
    squares = block * block
    partial = squares[:, 0:128]
    for i in range(1, half_s // 128):
        partial = partial + squares[:, i * 128:(i + 1) * 128]
    sums = jnp.sum(jnp.transpose(partial), axis=0, keepdims=True)
    sums = jnp.concatenate([sums, jnp.zeros((1, half_s - slots), F32)], axis=1)
    hi = sums.astype(BF16).astype(F32)
    mid = (sums - hi).astype(BF16).astype(F32)
    lo = sums - hi - mid
    sum_rows = jnp.where(
        slot_id == valid, hi, jnp.where(slot_id == valid + 1, mid, jnp.where(slot_id == valid + 2, lo, 0.0))
    )
    s_blk[k] = jnp.where(slot_id < valid, block * own_gain, sum_rows).astype(BF16)
    share(s_blk, s2s, s2r)
    s_acc[...] = jnp.zeros_like(s_acc)
    t_acc[...] = jnp.zeros_like(t_acc)

    def student_block(at):
        s_acc[...] += jnp.dot(s_blk[at], wv[at], preferred_element_type=F32)

    def teacher_block(at):
        t_acc[...] += jnp.dot(t_blk[at], tv[at], preferred_element_type=F32)

    w_copy.wait()
    student_block(k)
    sibling(s_blk, s2s, s2r, 0)
    student_block(slot(0, 1))
    relay(s_blk, s2s, s2r)
    for m in range(1, 8):
        arrived(in_t.at[source(m)], t1s.at[m], t1r.at[m], column(m // 2, m % 2))
    block = jnp.concatenate([in_t[i].astype(F32) for i in range(8)], axis=0).astype(BF16)
    t_blk[k] = jnp.dot(pick_t, block, preferred_element_type=F32).astype(BF16)
    share(t_blk, t2s, t2r)

    to_sibling(s_blk, s2s, s2r, 1)
    to_sibling(s_blk, s2s, s2r, 2)
    t_copy.wait()
    teacher_block(k)
    student_block(slot(1, 0))
    student_block(slot(2, 0))
    relay(t_blk, t2s, t2r)
    sibling(s_blk, s2s, s2r, 1)
    student_block(slot(1, 1))
    sibling(s_blk, s2s, s2r, 2)
    student_block(slot(2, 1))
    to_sibling(s_blk, s2s, s2r, 3)
    student_block(slot(3, 0))
    sibling(t_blk, t2s, t2r, 0)
    teacher_block(slot(0, 1))
    to_sibling(t_blk, t2s, t2r, 1)
    to_sibling(t_blk, t2s, t2r, 2)
    sibling(s_blk, s2s, s2r, 3)
    student_block(slot(3, 1))
    sums = s_blk[0][:, 0:slots].astype(F32)[valid:]
    for i in range(1, 8):
        sums = sums + s_blk[i][:, 0:slots].astype(F32)[valid:]
    sums = lax.rsqrt(jnp.sum(sums, axis=0, keepdims=True) / DS + EPSILON)
    inv = jnp.transpose(jnp.broadcast_to(sums, (slots, slots)))[:, 0:1]
    live = weight > 0.0
    teacher_block(slot(1, 0))
    teacher_block(slot(2, 0))
    for vm in (1, 2):
        sibling(t_blk, t2s, t2r, vm)
        teacher_block(slot(vm, 1))
    to_sibling(t_blk, t2s, t2r, 3)
    teacher_block(slot(3, 0))
    sibling(t_blk, t2s, t2r, 3)
    teacher_block(slot(3, 1))

    s_log = s_acc[...] * inv
    t_log = t_acc[...]
    top = jnp.max(s_log, axis=1, keepdims=True)
    top_t = jnp.max(t_log, axis=1, keepdims=True)
    a = s_log - top
    b = t_log - top_t
    e = jnp.exp(a)
    ea = e * a
    d = a - b
    figures = [
        top, jnp.sum(e, axis=1, keepdims=True), top_t, jnp.sum(jnp.exp(b), axis=1, keepdims=True),
        jnp.sum(e * d, axis=1, keepdims=True), jnp.sum(ea, axis=1, keepdims=True),
        jnp.sum(ea * d, axis=1, keepdims=True),
    ]
    lane = lax.broadcasted_iota(jnp.int32, (slots, 128), 1)
    packed = jnp.zeros((slots, 128), F32)
    for i, figure in enumerate(figures):
        packed = jnp.where(lane == i, figure, packed)
    st_a[k] = jnp.transpose(packed)[0:8, :]
    for m in range(1, 8):
        send(st_a.at[k], st_a.at[k], as_.at[m], ar.at[m], plane(m // 2, m % 2))
    for i in range(4):
        hg[i] = jnp.transpose(s_blk[i].astype(F32)).astype(BF16)
    for m in range(1, 8):
        arrived(st_a.at[slot(m // 2, m % 2)], as_.at[m], ar.at[m], plane(m // 2, m % 2))
    st_b[z] = merge([st_a[i] for i in range(8)])
    for m in range(1, 4):
        send(st_b.at[z], st_b.at[z], bs.at[m], br.at[m], column(m, 0))
    for i in range(4, 8):
        hg[i] = jnp.transpose(s_blk[i].astype(F32)).astype(BF16)
    for m in range(1, 4):
        arrived(st_b.at[flip(z, m)], bs.at[m], br.at[m], column(m, 0))
    full = merge([st_b[i] for i in range(4)])
    total = full[1:2]
    lse = full[0:1] + jnp.log(total)
    lse_t = full[2:3] + jnp.log(full[3:4])
    mean_ratio, mean_logit = full[4:5] / total, full[5:6] / total
    divergence = mean_ratio - jnp.log(total) + jnp.log(full[3:4])
    offset = lse - lse_t + divergence
    cov = full[6:7] / total - mean_ratio * mean_logit
    back = jnp.concatenate([lse, offset, divergence, cov, jnp.zeros((slots - 4, slots), F32)], axis=0)
    back = jnp.transpose(back)
    prob = jnp.exp(s_log - back[:, 0:1])
    grad = (weight * inv) * prob * (s_log - t_log - back[:, 1:2])
    g2[...] = jnp.where(live, grad, 0.0).astype(BF16)

    def block_grad(at):
        return lax.dot_general(g2[...], wv[at], (((1,), (1,)), ((), ())), preferred_element_type=F32)

    order = (1, 2, 3, 0)
    part = half_s // 2
    for vm in order:
        p_sib[vm] = block_grad(slot(vm, 1)).astype(BF16)
        send(p_sib.at[vm], r_sib.at[vm], qs.at[vm], qr.at[vm], plane(0, 1))
    for vm in order:
        mine = block_grad(slot(vm, 0))
        arrived(r_sib.at[vm], qs.at[vm], qr.at[vm], plane(0, 1))
        mine = mine + r_sib[vm].astype(F32)
        if vm:
            p_x[vm] = mine.astype(BF16)
            send(p_x.at[vm, :, 0:part], r_x.at[vm, :, 0:part], xs.at[vm], xr.at[vm], plane(vm, 0))
        else:
            own[...] = mine
    for vm in (1, 2, 3):
        send(p_x.at[vm, :, part:], r_x.at[vm, :, part:], xs.at[vm + 4], xr.at[vm + 4], plane(vm, 0))

    loss_ref[...] = jnp.sum(jnp.where(live, weight * back[:, 2:3], 0.0), axis=0, keepdims=True)
    lane = lax.broadcasted_iota(jnp.int32, (slots, 128), 1)
    figure = jnp.where(live, weight * inv * inv * back[:, 3:4] / DS, 0.0)
    hi = figure.astype(BF16).astype(F32)
    mid = (figure - hi).astype(BF16).astype(F32)
    lo = figure - hi - mid
    packed = jnp.where(lane == 0, hi, jnp.where(lane == 1, mid, jnp.where(lane == 2, lo, 0.0))).astype(BF16)
    packed = lax.dot_general(pick_ref[...], packed, (((0,), (0,)), ((), ())), preferred_element_type=F32)
    cols[...] = jnp.broadcast_to(jnp.sum(packed, axis=1, keepdims=True), cols.shape)

    def head_block(i):
        head[i] = jnp.dot(hg[i], g2[...], preferred_element_type=F32).astype(BF16)
        copy = pltpu.make_async_copy(head.at[i], head_hbm.at[i], h_sem.at[i])
        copy.start()
        head_copies.append(copy)

    head_copies = []
    for i in range(4):
        head_block(i)
    for h in range(2):
        at = slice(h * part, (h + 1) * part)
        for vm in (1, 2, 3):
            arrived(r_x.at[vm, :, at], xs.at[vm + 4 * h], xr.at[vm + 4 * h], plane(vm, 0))
        total = own[:, at]
        for vm in (1, 2, 3):
            total = total + r_x[vm, :, at].astype(F32)
        spread_out = lax.dot_general(
            pick_ref[...], total.astype(BF16), (((0,), (0,)), ((), ())), preferred_element_type=F32
        )
        for i in range(8):
            rb[i, :, at] = spread_out[i * rows:(i + 1) * rows].astype(BF16)
        for m in range(1, 8):
            send(
                rb.at[source(m), :, at], rz.at[g, :, at], zs.at[m + 8 * h], zr.at[m + 8 * h],
                column(m // 2, m % 2),
            )
        gp[:, at] = jnp.sum(
            total * raw[:, at], axis=0, keepdims=True
        )
        if h:
            for m in range(1, 8):
                send(gp, gz.at[g], ys.at[m], yr.at[m], column(m // 2, m % 2))
        for i in range(4 + 2 * h, 6 + 2 * h):
            head_block(i)
    rz[g] = rb[g]
    gz[g] = gp[...]
    for h in range(2):
        at = slice(h * part, (h + 1) * part)
        for m in range(1, 8):
            arrived(rz.at[source(m), :, at], zs.at[m + 8 * h], zr.at[m + 8 * h], column(m // 2, m % 2))
    own_cols = cols[pl.ds(pl.multiple_of(g * rows, 8), rows), :][:, 0:1]
    for h in range(2):
        at = slice(h * half_s, (h + 1) * half_s)
        ng = rz[h].astype(F32)
        for i in range(1, 4):
            ng = ng + rz[2 * i + h].astype(F32)
        hid = sh_ref[:, at].astype(F32)
        gh_ref[:, at] = (gain_ref[:, at] * ng - hid * own_cols).astype(BF16)
    for m in range(1, 8):
        arrived(gz.at[source(m)], ys.at[m], yr.at[m], column(m // 2, m % 2))
    for h in range(2):
        at = slice(h * half_s, (h + 1) * half_s)
        ng = gz[h]
        for i in range(1, 4):
            ng = ng + gz[2 * i + h]
        gg_ref[:, at] = ng
    for copy in head_copies:
        copy.wait()
    for copy in sends:
        copy.wait_send()


def finish(head_in, loss_in, hidden_in, gain_in, head_out, loss_out, hidden_out, gain_out, sems):
    moves = [(head_in.at[i], head_out.at[i]) for i in range(8)]
    moves += [(hidden_in, hidden_out), (gain_in, gain_out), (loss_in, loss_out)]
    copies = [pltpu.make_async_copy(src, dst, sems.at[i]) for i, (src, dst) in enumerate(moves)]
    for copy in copies:
        copy.start()
    for copy in copies:
        copy.wait()


def fused(
    student_hidden, norm_gain, teacher_hidden, student_head, teacher_head, episode_source, lengths
):
    rows, wide_s = student_hidden.shape
    wide_t = teacher_hidden.shape[1]
    tokens = rows * lax.axis_size("grp")
    voc = student_head.shape[1]
    half_s, half_t = wide_s // 2, wide_t // 2
    slots = -(-(tokens * 5 // 8 + 3) // 128) * 128
    vmem = pl.BlockSpec(memory_space=pltpu.VMEM)
    hbm = pl.BlockSpec(memory_space=pltpu.HBM)
    dma = pltpu.SemaphoreType.DMA
    loss, grad_hidden, grad_gain, grad_head = pl.pallas_call(
        kernel,
        out_shape=(
            jax.ShapeDtypeStruct((1, 1), F32),
            jax.ShapeDtypeStruct((rows, wide_s), BF16),
            jax.ShapeDtypeStruct((1, wide_s), F32),
            jax.ShapeDtypeStruct((8, half_s, voc), BF16),
        ),
        in_specs=[hbm] * 7,
        out_specs=(vmem, vmem, vmem, hbm),
        scratch_shapes=[
            pltpu.VMEM((8, half_s, voc), BF16),
            pltpu.VMEM((8, half_t, voc), BF16),
            pltpu.VMEM((rows, wide_s), BF16),
            pltpu.VMEM((1, wide_s), F32),
            pltpu.VMEM((1, episode_source.shape[0]), jnp.int32),
            pltpu.VMEM((1, episode_source.shape[0]), jnp.int32),
            pltpu.VMEM((slots, tokens), BF16),
            pltpu.VMEM((8, rows, half_s), BF16),
            pltpu.VMEM((8, rows, half_t), BF16),
            pltpu.VMEM((8, slots, half_s), BF16),
            pltpu.VMEM((8, slots, half_t), BF16),
            pltpu.VMEM((8, half_s, slots), BF16),
            pltpu.VMEM((slots, voc), F32),
            pltpu.VMEM((slots, voc), F32),
            pltpu.VMEM((slots, half_s), F32),
            pltpu.VMEM((tokens, 128), F32),
            pltpu.VMEM((8, 8, slots), F32),
            pltpu.VMEM((4, 8, slots), F32),
            pltpu.VMEM((slots, voc), BF16),
            pltpu.VMEM((slots, half_s), F32),
            pltpu.VMEM((4, slots, half_s), BF16),
            pltpu.VMEM((4, slots, half_s), BF16),
            pltpu.VMEM((4, slots, half_s), BF16),
            pltpu.VMEM((4, slots, half_s), BF16),
            pltpu.VMEM((8, rows, half_s), BF16),
            pltpu.VMEM((8, rows, half_s), BF16),
            pltpu.VMEM((1, half_s), F32),
            pltpu.VMEM((8, 1, half_s), F32),
            pltpu.VMEM((8, half_s, voc), BF16),
            dma(()), dma(()), dma((8,)), dma((8,)),
        ] + [dma((8,))] * 4 + [dma((16,))] * 4 + [dma((8,))] * 8 + [dma((16,))] * 2 + [dma((8,))] * 2,
        compiler_params=pltpu.CompilerParams(
            collective_id=0, has_side_effects=True, vmem_limit_bytes=LIMIT * 1024
        ),
        cost_estimate=pl.CostEstimate(flops=2600000000, bytes_accessed=11000000, transcendentals=400000),
    )(
        student_hidden, teacher_hidden, norm_gain.reshape(1, -1),
        episode_source.reshape(1, -1), lengths.reshape(1, -1),
        student_head.reshape(8, half_s, voc), teacher_head.reshape(8, half_t, voc),
    )
    results = (grad_head, loss, grad_hidden, grad_gain)
    grad_head, loss, grad_hidden, grad_gain = pl.pallas_call(
        finish,
        out_shape=tuple(jax.ShapeDtypeStruct(r.shape, r.dtype) for r in results),
        in_specs=[hbm] * 4,
        out_specs=(hbm,) * 4,
        scratch_shapes=[dma((11,))],
        compiler_params=pltpu.CompilerParams(vmem_limit_bytes=LIMIT * 1024),
        cost_estimate=pl.CostEstimate(flops=0, bytes_accessed=6400000, transcendentals=0),
    )(*results)
    return (loss[0, 0], grad_hidden, grad_gain.reshape(-1), grad_head.reshape(student_head.shape))


def realign(teacher_hidden, table, group_index, per_group):
    groups = table.shape[0]
    source_group = table // per_group
    source_local = table % per_group
    mine = (source_group == group_index).astype(jnp.int32)
    earlier = jnp.cumsum(mine, axis=1) - mine
    slot_ids = jnp.arange(MOST, dtype=jnp.int32)
    matches = mine[:, :, None] * (earlier[:, :, None] == slot_ids[None, None, :]).astype(jnp.int32)
    send_index = jnp.sum(matches * source_local[:, :, None], axis=1)
    features = teacher_hidden.shape[1]
    episodes = teacher_hidden.reshape(per_group, SEQ, features)
    outgoing = jnp.take(episodes, send_index, axis=0)
    incoming = lax.all_to_all(outgoing, "grp", split_axis=0, concat_axis=0, tiled=True)
    own_groups = lax.dynamic_index_in_dim(source_group, group_index, 0, keepdims=False)
    matching = (own_groups[:, None] == own_groups[None, :]).astype(jnp.int32)
    position = jnp.sum(jnp.tril(matching, -1), axis=1)
    flat_index = own_groups * MOST + position
    received = incoming.reshape(groups * MOST, SEQ, features)
    return jnp.take(received, flat_index, axis=0).reshape(per_group * SEQ, features)


def local(
    student_hidden, norm_gain, teacher_hidden, student_head, teacher_head, episode_source, lengths
):
    groups = lax.axis_size("grp")
    group_index = lax.axis_index("grp")
    rows_group = student_hidden.shape[0]
    per_group = rows_group // SEQ
    hidden_f32 = student_hidden.astype(jnp.float32)
    squares = lax.psum(jnp.sum(hidden_f32 * hidden_f32, axis=1), "voc")
    inverse_rms = lax.rsqrt(squares / DS + EPSILON)
    normed = (hidden_f32 * inverse_rms[:, None] * norm_gain[None, :]).astype(jnp.bfloat16)
    table = episode_source.reshape(groups, per_group)
    aligned = realign(teacher_hidden, table, group_index, per_group)
    teacher_rows, student_rows = (
        lax.all_gather(aligned, "voc", axis=1, tiled=True),
        lax.all_gather(normed, "voc", axis=1, tiled=True),
    )
    teacher_logits = jnp.dot(
        lax.all_gather(teacher_rows, "grp", axis=0, tiled=True),
        teacher_head,
        preferred_element_type=jnp.float32,
    )
    positions = jnp.arange(SEQ, dtype=jnp.int32)
    all_rows = lax.all_gather(student_rows, "grp", axis=0, tiled=True)
    student_logits = jnp.dot(all_rows, student_head, preferred_element_type=jnp.float32)
    lengths_f32 = lengths.astype(jnp.float32)
    valid = positions[None, :] < lengths[:, None]
    token_weight = jnp.where(
        valid, 1.0 / lengths_f32[:, None], jnp.zeros_like(lengths_f32)[:, None]
    ).reshape(-1)
    top_student, top_teacher = lax.pmax(
        (jnp.max(student_logits, axis=1), jnp.max(teacher_logits, axis=1)), ("grp", "voc")
    )
    exp_student = jnp.exp(student_logits - top_student[:, None])
    exp_teacher = jnp.exp(teacher_logits - top_teacher[:, None])
    total_student, total_teacher = lax.psum(
        (jnp.sum(exp_student, axis=1), jnp.sum(exp_teacher, axis=1)), ("grp", "voc")
    )
    log_student = student_logits - (top_student + jnp.log(total_student))[:, None]
    log_teacher = teacher_logits - (top_teacher + jnp.log(total_teacher))[:, None]
    prob_student = jnp.exp(log_student)
    log_ratio = log_student - log_teacher
    divergence = lax.psum(jnp.sum(prob_student * log_ratio, axis=1), ("grp", "voc"))
    loss = jnp.sum(token_weight * divergence)
    logit_grad = (token_weight[:, None] * prob_student * (log_ratio - divergence[:, None])).astype(
        jnp.bfloat16
    )
    grad_head = lax.dot_general(
        all_rows, logit_grad, (((0,), (0,)), ((), ())), preferred_element_type=jnp.float32
    ).astype(jnp.bfloat16)
    full_term = lax.dot_general(
        logit_grad, student_head, (((1,), (1,)), ((), ())), preferred_element_type=jnp.float32
    )
    feature_part = lax.psum_scatter(
        full_term.astype(jnp.bfloat16), "voc", scatter_dimension=1, tiled=True
    )
    normed_grad = lax.psum_scatter(feature_part, "grp", scatter_dimension=0, tiled=True).astype(
        jnp.float32
    )
    scaled = normed_grad * norm_gain[None, :]
    inner = lax.psum(jnp.sum(scaled * hidden_f32, axis=1), "voc")
    grad_hidden = (
        inverse_rms[:, None] * scaled - hidden_f32 * (inverse_rms**3)[:, None] * inner[:, None] / DS
    )
    grad_gain = lax.psum(jnp.sum(normed_grad * hidden_f32 * inverse_rms[:, None], axis=0), "grp")
    return (loss, grad_hidden.astype(jnp.bfloat16), grad_gain, grad_head)


def solution(mesh):
    placed = (
        P("grp", "voc"),
        P("voc"),
        P("grp", "voc"),
        P(None, ("grp", "voc")),
        P(None, ("grp", "voc")),
        P(),
        P(),
    )
    body = fused if tuple(mesh.shape.values()) == (8, 4) else local
    return jax.shard_map(
        body,
        mesh=mesh,
        in_specs=placed,
        out_specs=(P(), P("grp", "voc"), P("voc"), P(None, ("grp", "voc"))),
        check_vma=False,
    )
```

```python
import functools

import jax
import jax.numpy as jnp
from jax import lax
from jax.experimental import pallas as pl
from jax.experimental.pallas import tpu as pltpu
from jax.sharding import PartitionSpec as P

DS = 4096
SEQ = 2
MOST = 2


EPSILON = 1e-06

F32 = jnp.float32
BF16 = jnp.bfloat16
LIMIT = 65472
MESH = pl.DeviceIdType.MESH


def flip(number, mask):
    low, high = number % 2, number // 2
    if mask & 1:
        low = 1 - low
    if mask & 2:
        high = 1 - high
    return high * 2 + low


def merge(parts):
    top = functools.reduce(jnp.maximum, [p[0:1] for p in parts])
    top_t = functools.reduce(jnp.maximum, [p[2:3] for p in parts])
    total = total_t = ratio = logit = both = 0.0
    for p in parts:
        shift, shift_t = p[0:1] - top, p[2:3] - top_t
        factor, factor_t = jnp.exp(shift), jnp.exp(shift_t)
        live = factor > 0.0
        shift = jnp.where(live, shift, 0.0)
        gap = shift - jnp.where(live, shift_t, 0.0)
        total = total + factor * p[1:2]
        total_t = total_t + factor_t * p[3:4]
        ratio = ratio + factor * (p[4:5] + p[1:2] * gap)
        logit = logit + factor * (p[5:6] + p[1:2] * shift)
        both = both + factor * (p[6:7] + gap * p[5:6] + shift * p[4:5] + shift * gap * p[1:2])
    return jnp.concatenate([top, total, top_t, total_t, ratio, logit, both, jnp.zeros_like(top)], axis=0)


def kernel(
    sh_hbm, th_hbm, gain_hbm, source_hbm, lengths_hbm, w_hbm, t_hbm,
    loss_ref, gh_ref, gg_ref, head_hbm,
    wv, tv, sh_ref, gain_ref, source_ref, lengths_ref, pick_ref, in_s, in_t, s_blk, t_blk, hg, s_acc, t_acc, raw, sq, cols,
    st_a, st_b, g2, own, p_sib, r_sib, p_x, r_x, rb, rz, gp, gz, head,
    w_sem, t_sem, h_sem, l_sem, s1s, s1r, t1s, t1r, s2s, s2r, t2s, t2r, as_, ar, bs, br,
    qs, qr, xs, xr, zs, zr, ys, yr, us, ur,
):
    g = lax.axis_index("grp")
    v = lax.axis_index("voc")
    z, c = g // 2, g % 2
    k = v * 2 + c
    rows, half_s = in_s.shape[1], in_s.shape[2]
    half_t = in_t.shape[2]
    tokens = in_s.shape[0] * rows
    slots = s_acc.shape[0]

    def plane(vm, cm):
        return {"grp": z * 2 + (1 - c if cm else c), "voc": flip(v, vm)}

    def column(zm, cm):
        return {"grp": flip(z, zm) * 2 + (1 - c if cm else c), "voc": v}

    def slot(vm, cm):
        return flip(v, vm) * 2 + (1 - c if cm else c)

    sends = []

    def send(src, dst, ssem, rsem, to):
        copy = pltpu.make_async_remote_copy(
            src_ref=src, dst_ref=dst, send_sem=ssem, recv_sem=rsem, device_id=to, device_id_type=MESH
        )
        copy.start()
        sends.append(copy)

    def arrived(dst, ssem, rsem, to):
        pltpu.make_async_remote_copy(
            src_ref=dst, dst_ref=dst, send_sem=ssem, recv_sem=rsem, device_id=to, device_id_type=MESH
        ).wait_recv()

    def half(ref, number, width):
        return ref.at[:, pl.ds(pl.multiple_of(number * width, 128), width)]

    local_copies = [
        pltpu.make_async_copy(src, dst, l_sem.at[i])
        for i, (src, dst) in enumerate((
            (source_hbm, source_ref), (lengths_hbm, lengths_ref), (gain_hbm, gain_ref),
            (half(sh_hbm, c, half_s), in_s.at[g]), (half(th_hbm, c, half_t), in_t.at[g]), (sh_hbm, sh_ref),
        ))
    ]
    for copy in local_copies:
        copy.start()
    w_copy = pltpu.make_async_copy(w_hbm, wv, w_sem)
    t_copy = pltpu.make_async_copy(t_hbm, tv, t_sem)
    w_copy.start()
    t_copy.start()

    barrier = pltpu.get_barrier_semaphore()
    peers = [plane(m // 2, m % 2) for m in range(1, 8)] + [column(m // 2, m % 2) for m in range(2, 8)]
    for peer in peers:
        pl.semaphore_signal(barrier, inc=1, device_id=peer, device_id_type=MESH)
    pl.semaphore_wait(barrier, len(peers))

    def source(m):
        return flip(z, m // 2) * 2 + (1 - c if m % 2 else c)

    middle = (z == 1) | (z == 2)
    middle_sends = []

    def spread_rows(ref, width, dst, ssem, rsem):
        for m in (4, 5, 6, 7, 2, 3, 1):
            other = 1 - c if m % 2 else c
            if m < 6:
                send(half(ref, other, width), dst.at[g], ssem.at[m], rsem.at[m], column(m // 2, m % 2))
            else:
                middle_sends.append(pltpu.make_async_remote_copy(
                    src_ref=half(ref, other, width), dst_ref=dst.at[g], send_sem=ssem.at[m], recv_sem=rsem.at[m],
                    device_id=column(m // 2, m % 2), device_id_type=MESH,
                ))
                pl.when(middle)(middle_sends[-1].start)

    def hand_on(dst, ssem, rsem):
        for m in (4, 5):
            piece = dst.at[source(m)]
            arrived(piece, ssem.at[m], rsem.at[m], column(2, m % 2))
            middle_sends.append(pltpu.make_async_remote_copy(
                src_ref=piece, dst_ref=piece, send_sem=ssem.at[m + 4], recv_sem=rsem.at[m + 2],
                device_id=column(1, 0), device_id_type=MESH,
            ))
            pl.when(middle)(middle_sends[-1].start)

    def rows_in(dst, ssem, rsem):
        for m in (1, 2, 3, 6, 7):
            arrived(dst.at[source(m)], ssem.at[m], rsem.at[m], column(m // 2, m % 2))

    spread_rows(sh_hbm, half_s, in_s, s1s, s1r)
    spread_rows(th_hbm, half_t, in_t, t1s, t1r)

    for copy in local_copies[:3]:
        copy.wait()
    episodes = source_ref.shape[1]
    line = lax.broadcasted_iota(jnp.int32, (8, episodes), 0)
    table = jnp.where(line == 0, source_ref[...], jnp.where(line == 1, lengths_ref[...], 0)).astype(F32).astype(BF16)
    spread = lax.broadcasted_iota(jnp.int32, (episodes, tokens), 1) // SEQ == lax.broadcasted_iota(
        jnp.int32, (episodes, tokens), 0
    )
    table = jnp.dot(table, spread.astype(F32).astype(BF16), preferred_element_type=F32)
    position = (lax.broadcasted_iota(jnp.int32, (1, tokens), 1) % SEQ).astype(F32)
    row_source = table[0:1] * SEQ + position
    row_length = table[1:2]
    row_valid = (position < row_length).astype(F32)
    before = lax.broadcasted_iota(jnp.int32, (tokens, tokens), 0) < lax.broadcasted_iota(jnp.int32, (tokens, tokens), 1)
    rank = jnp.dot(
        jnp.broadcast_to(row_valid, (8, tokens)).astype(BF16), before.astype(F32).astype(BF16),
        preferred_element_type=F32,
    )[0:1]
    slot_line = lax.broadcasted_iota(jnp.int32, (slots, tokens), 0).astype(F32)
    pick = jnp.where(slot_line == rank, row_valid, 0.0).astype(BF16)
    pick_ref[...] = pick
    line = lax.broadcasted_iota(jnp.int32, (8, tokens), 0)
    both = jnp.where(line == 0, row_source, jnp.where(line == 1, row_length, 0.0)).astype(BF16)
    slot_table = lax.dot_general(pick, both, (((1,), (1,)), ((), ())), preferred_element_type=F32)
    slot_source, slot_length = slot_table[:, 0:1], slot_table[:, 1:2]
    weight = jnp.where(slot_length > 0.0, 1.0 / jnp.maximum(slot_length, 1.0), 0.0)
    teacher_lane = lax.broadcasted_iota(jnp.int32, (slots, tokens), 1).astype(F32)
    pick_t = jnp.where((slot_source == teacher_lane) & (slot_length > 0.0), 1.0, 0.0).astype(BF16)

    gain = gain_ref[...]
    own_gain = jnp.where(c == 0, gain[:, :half_s], gain[:, half_s:])

    halves = (slice(0, slots // 2), slice(slots // 2, slots))

    def share(blk, ssem, rsem):
        for vm, half_id in ((1, 0), (2, 1), (1, 1), (2, 0)):
            piece = blk.at[k, halves[half_id]]
            send(piece, piece, ssem.at[vm * 4 + half_id], rsem.at[vm * 4 + half_id], plane(vm, 0))
        send(blk.at[k], blk.at[k], ssem.at[2], rsem.at[2], plane(0, 1))

    def landed(blk, ssem, rsem, vm, half_id):
        piece = blk.at[slot(vm, 0), halves[half_id]]
        arrived(piece, ssem.at[vm * 4 + half_id], rsem.at[vm * 4 + half_id], plane(vm, 0))
        return piece

    def relay(blk, ssem, rsem):
        for vm, half_id in ((1, 0), (2, 1)):
            piece = landed(blk, ssem, rsem, vm, half_id)
            send(piece, piece, ssem.at[12 + half_id], rsem.at[12 + half_id], plane(3 - vm, 0))

    def to_sibling(blk, ssem, rsem, vm):
        for half_id in {1: (1,), 2: (0,), 3: (0, 1)}[vm]:
            landed(blk, ssem, rsem, vm, half_id)
        at = slot(vm, 0)
        send(blk.at[at], blk.at[at], ssem.at[vm * 4 + 2], rsem.at[vm * 4 + 2], plane(0, 1))

    def sibling(blk, ssem, rsem, vm):
        arrived(blk.at[slot(vm, 1)], ssem.at[vm * 4 + 2], rsem.at[vm * 4 + 2], plane(0, 1))

    hand_on(in_s, s1s, s1r)
    rows_in(in_s, s1s, s1r)
    for copy in local_copies[3:]:
        copy.wait()
    block = jnp.concatenate([in_s[i].astype(F32) for i in range(8)], axis=0).astype(BF16)
    block = jnp.dot(pick, block, preferred_element_type=F32)
    raw[...] = block
    s_blk[k] = (block * own_gain).astype(BF16)
    share(s_blk, s2s, s2r)
    squares = block * block
    partial = squares[:, 0:128]
    for i in range(1, half_s // 128):
        partial = partial + squares[:, i * 128:(i + 1) * 128]
    sq[k] = jnp.broadcast_to(jnp.sum(jnp.transpose(partial), axis=0, keepdims=True), (8, slots))
    for m in range(1, 8):
        send(sq.at[k], sq.at[k], us.at[m], ur.at[m], plane(m // 2, m % 2))
    s_acc[...] = jnp.zeros_like(s_acc)
    t_acc[...] = jnp.zeros_like(t_acc)

    def student_block(at):
        s_acc[...] += jnp.dot(s_blk[at], wv[at], preferred_element_type=F32)

    def teacher_block(at):
        t_acc[...] += jnp.dot(t_blk[at], tv[at], preferred_element_type=F32)

    w_copy.wait()
    student_block(k)
    hand_on(in_t, t1s, t1r)
    sibling(s_blk, s2s, s2r, 0)
    student_block(slot(0, 1))
    relay(s_blk, s2s, s2r)
    rows_in(in_t, t1s, t1r)
    block = jnp.concatenate([in_t[i].astype(F32) for i in range(8)], axis=0).astype(BF16)
    t_blk[k] = jnp.dot(pick_t, block, preferred_element_type=F32).astype(BF16)
    share(t_blk, t2s, t2r)

    to_sibling(s_blk, s2s, s2r, 1)
    to_sibling(s_blk, s2s, s2r, 2)
    t_copy.wait()
    teacher_block(k)
    student_block(slot(1, 0))
    student_block(slot(2, 0))
    relay(t_blk, t2s, t2r)
    sibling(s_blk, s2s, s2r, 1)
    student_block(slot(1, 1))
    sibling(s_blk, s2s, s2r, 2)
    student_block(slot(2, 1))
    to_sibling(s_blk, s2s, s2r, 3)
    student_block(slot(3, 0))
    sibling(t_blk, t2s, t2r, 0)
    teacher_block(slot(0, 1))
    to_sibling(t_blk, t2s, t2r, 1)
    to_sibling(t_blk, t2s, t2r, 2)
    sibling(s_blk, s2s, s2r, 3)
    student_block(slot(3, 1))
    for m in range(1, 8):
        arrived(sq.at[slot(m // 2, m % 2)], us.at[m], ur.at[m], plane(m // 2, m % 2))
    sums = sq[0, 0:1]
    for i in range(1, 8):
        sums = sums + sq[i, 0:1]
    sums = lax.rsqrt(sums / DS + EPSILON)
    inv = jnp.transpose(jnp.broadcast_to(sums, (slots, slots)))[:, 0:1]
    live = weight > 0.0
    teacher_block(slot(1, 0))
    teacher_block(slot(2, 0))
    for vm in (1, 2):
        sibling(t_blk, t2s, t2r, vm)
        teacher_block(slot(vm, 1))
    to_sibling(t_blk, t2s, t2r, 3)
    teacher_block(slot(3, 0))
    sibling(t_blk, t2s, t2r, 3)
    teacher_block(slot(3, 1))

    s_log = s_acc[...] * inv
    t_log = t_acc[...]
    top = jnp.max(s_log, axis=1, keepdims=True)
    top_t = jnp.max(t_log, axis=1, keepdims=True)
    a = s_log - top
    b = t_log - top_t
    e = jnp.exp(a)
    ea = e * a
    d = a - b
    figures = [
        top, jnp.sum(e, axis=1, keepdims=True), top_t, jnp.sum(jnp.exp(b), axis=1, keepdims=True),
        jnp.sum(e * d, axis=1, keepdims=True), jnp.sum(ea, axis=1, keepdims=True),
        jnp.sum(ea * d, axis=1, keepdims=True),
    ]
    lane = lax.broadcasted_iota(jnp.int32, (slots, 128), 1)
    packed = jnp.zeros((slots, 128), F32)
    for i, figure in enumerate(figures):
        packed = jnp.where(lane == i, figure, packed)
    st_a[k] = jnp.transpose(packed)[0:8, :]
    for m in range(1, 8):
        send(st_a.at[k], st_a.at[k], as_.at[m], ar.at[m], plane(m // 2, m % 2))
    for i in range(4):
        hg[i] = jnp.transpose(s_blk[i].astype(F32)).astype(BF16)
    for m in range(1, 8):
        arrived(st_a.at[slot(m // 2, m % 2)], as_.at[m], ar.at[m], plane(m // 2, m % 2))
    st_b[z] = merge([st_a[i] for i in range(8)])
    for m in range(1, 4):
        send(st_b.at[z], st_b.at[z], bs.at[m], br.at[m], column(m, 0))
    for i in range(4, 8):
        hg[i] = jnp.transpose(s_blk[i].astype(F32)).astype(BF16)
    for m in range(1, 4):
        arrived(st_b.at[flip(z, m)], bs.at[m], br.at[m], column(m, 0))
    full = merge([st_b[i] for i in range(4)])
    total = full[1:2]
    lse = full[0:1] + jnp.log(total)
    lse_t = full[2:3] + jnp.log(full[3:4])
    mean_ratio, mean_logit = full[4:5] / total, full[5:6] / total
    divergence = mean_ratio - jnp.log(total) + jnp.log(full[3:4])
    offset = lse - lse_t + divergence
    cov = full[6:7] / total - mean_ratio * mean_logit
    back = jnp.concatenate([lse, offset, divergence, cov, jnp.zeros((slots - 4, slots), F32)], axis=0)
    back = jnp.transpose(back)
    prob = jnp.exp(s_log - back[:, 0:1])
    grad = (weight * inv) * prob * (s_log - t_log - back[:, 1:2])
    g2[...] = jnp.where(live, grad, 0.0).astype(BF16)

    def block_grad(at):
        return lax.dot_general(g2[...], wv[at], (((1,), (1,)), ((), ())), preferred_element_type=F32)

    order = (1, 2, 3, 0)
    part = half_s // 2
    for vm in order:
        p_sib[vm] = block_grad(slot(vm, 1)).astype(BF16)
        send(p_sib.at[vm], r_sib.at[vm], qs.at[vm], qr.at[vm], plane(0, 1))
    for vm in order:
        mine = block_grad(slot(vm, 0))
        arrived(r_sib.at[vm], qs.at[vm], qr.at[vm], plane(0, 1))
        mine = mine + r_sib[vm].astype(F32)
        if vm:
            p_x[vm] = mine.astype(BF16)
            send(p_x.at[vm, :, 0:part], r_x.at[vm, :, 0:part], xs.at[vm], xr.at[vm], plane(vm, 0))
        else:
            own[...] = mine
    for vm in (1, 2, 3):
        send(p_x.at[vm, :, part:], r_x.at[vm, :, part:], xs.at[vm + 4], xr.at[vm + 4], plane(vm, 0))

    loss_ref[...] = jnp.sum(jnp.where(live, weight * back[:, 2:3], 0.0), axis=0, keepdims=True)
    lane = lax.broadcasted_iota(jnp.int32, (slots, 128), 1)
    figure = jnp.where(live, weight * inv * inv * back[:, 3:4] / DS, 0.0)
    hi = figure.astype(BF16).astype(F32)
    mid = (figure - hi).astype(BF16).astype(F32)
    lo = figure - hi - mid
    packed = jnp.where(lane == 0, hi, jnp.where(lane == 1, mid, jnp.where(lane == 2, lo, 0.0))).astype(BF16)
    packed = lax.dot_general(pick_ref[...], packed, (((0,), (0,)), ((), ())), preferred_element_type=F32)
    cols[...] = jnp.broadcast_to(jnp.sum(packed, axis=1, keepdims=True), cols.shape)

    def head_block(i):
        head[i] = jnp.dot(hg[i], g2[...], preferred_element_type=F32).astype(BF16)
        copy = pltpu.make_async_copy(head.at[i], head_hbm.at[i], h_sem.at[i])
        copy.start()
        head_copies.append(copy)

    head_copies = []
    for i in range(4):
        head_block(i)
    for h in range(2):
        at = slice(h * part, (h + 1) * part)
        for vm in (1, 2, 3):
            arrived(r_x.at[vm, :, at], xs.at[vm + 4 * h], xr.at[vm + 4 * h], plane(vm, 0))
        total = own[:, at]
        for vm in (1, 2, 3):
            total = total + r_x[vm, :, at].astype(F32)
        spread_out = lax.dot_general(
            pick_ref[...], total.astype(BF16), (((0,), (0,)), ((), ())), preferred_element_type=F32
        )
        for i in range(8):
            rb[i, :, at] = spread_out[i * rows:(i + 1) * rows].astype(BF16)
        for m in range(1, 8):
            send(
                rb.at[source(m), :, at], rz.at[g, :, at], zs.at[m + 8 * h], zr.at[m + 8 * h],
                column(m // 2, m % 2),
            )
        gp[:, at] = jnp.sum(
            total * raw[:, at], axis=0, keepdims=True
        )
        if h:
            for m in range(1, 8):
                send(gp, gz.at[g], ys.at[m], yr.at[m], column(m // 2, m % 2))
        for i in range(4 + 2 * h, 6 + 2 * h):
            head_block(i)
    rz[g] = rb[g]
    gz[g] = gp[...]
    for h in range(2):
        at = slice(h * part, (h + 1) * part)
        for m in range(1, 8):
            arrived(rz.at[source(m), :, at], zs.at[m + 8 * h], zr.at[m + 8 * h], column(m // 2, m % 2))
    own_cols = cols[pl.ds(pl.multiple_of(g * rows, 8), rows), :][:, 0:1]
    for h in range(2):
        at = slice(h * half_s, (h + 1) * half_s)
        ng = rz[h].astype(F32)
        for i in range(1, 4):
            ng = ng + rz[2 * i + h].astype(F32)
        hid = sh_ref[:, at].astype(F32)
        gh_ref[:, at] = (gain_ref[:, at] * ng - hid * own_cols).astype(BF16)
    for m in range(1, 8):
        arrived(gz.at[source(m)], ys.at[m], yr.at[m], column(m // 2, m % 2))
    for h in range(2):
        at = slice(h * half_s, (h + 1) * half_s)
        ng = gz[h]
        for i in range(1, 4):
            ng = ng + gz[2 * i + h]
        gg_ref[:, at] = ng
    for copy in head_copies:
        copy.wait()
    for copy in sends:
        copy.wait_send()
    for copy in middle_sends:
        pl.when(middle)(copy.wait_send)


def finish(
    head_in, loss_in, hidden_in, gain_in, head_out, loss_out, hidden_out, gain_out,
    head, hidden, gain, loss, in_sem, out_sem,
):
    moves = [(head_in.at[i], head.at[i], head_out.at[i]) for i in range(8)]
    moves += [(hidden_in, hidden, hidden_out), (gain_in, gain, gain_out), (loss_in, loss, loss_out)]
    inward = [pltpu.make_async_copy(a, b, in_sem.at[i]) for i, (a, b, _) in enumerate(moves)]
    outward = [pltpu.make_async_copy(b, c, out_sem.at[i]) for i, (_, b, c) in enumerate(moves)]
    for copy in inward:
        copy.start()
    for first, second in zip(inward, outward):
        first.wait()
        second.start()
    for copy in outward:
        copy.wait()


def fused(
    student_hidden, norm_gain, teacher_hidden, student_head, teacher_head, episode_source, lengths
):
    rows, wide_s = student_hidden.shape
    wide_t = teacher_hidden.shape[1]
    tokens = rows * lax.axis_size("grp")
    voc = student_head.shape[1]
    half_s, half_t = wide_s // 2, wide_t // 2
    slots = -(-(tokens * 5 // 8) // 128) * 128
    vmem = pl.BlockSpec(memory_space=pltpu.VMEM)
    hbm = pl.BlockSpec(memory_space=pltpu.HBM)
    dma = pltpu.SemaphoreType.DMA
    loss, grad_hidden, grad_gain, grad_head = pl.pallas_call(
        kernel,
        out_shape=(
            jax.ShapeDtypeStruct((1, 1), F32),
            jax.ShapeDtypeStruct((rows, wide_s), BF16),
            jax.ShapeDtypeStruct((1, wide_s), F32),
            jax.ShapeDtypeStruct((8, half_s, voc), BF16),
        ),
        in_specs=[hbm] * 7,
        out_specs=(vmem, vmem, vmem, hbm),
        scratch_shapes=[
            pltpu.VMEM((8, half_s, voc), BF16),
            pltpu.VMEM((8, half_t, voc), BF16),
            pltpu.VMEM((rows, wide_s), BF16),
            pltpu.VMEM((1, wide_s), F32),
            pltpu.VMEM((1, episode_source.shape[0]), jnp.int32),
            pltpu.VMEM((1, episode_source.shape[0]), jnp.int32),
            pltpu.VMEM((slots, tokens), BF16),
            pltpu.VMEM((8, rows, half_s), BF16),
            pltpu.VMEM((8, rows, half_t), BF16),
            pltpu.VMEM((8, slots, half_s), BF16),
            pltpu.VMEM((8, slots, half_t), BF16),
            pltpu.VMEM((8, half_s, slots), BF16),
            pltpu.VMEM((slots, voc), F32),
            pltpu.VMEM((slots, voc), F32),
            pltpu.VMEM((slots, half_s), F32),
            pltpu.VMEM((8, 8, slots), F32),
            pltpu.VMEM((tokens, 128), F32),
            pltpu.VMEM((8, 8, slots), F32),
            pltpu.VMEM((4, 8, slots), F32),
            pltpu.VMEM((slots, voc), BF16),
            pltpu.VMEM((slots, half_s), F32),
            pltpu.VMEM((4, slots, half_s), BF16),
            pltpu.VMEM((4, slots, half_s), BF16),
            pltpu.VMEM((4, slots, half_s), BF16),
            pltpu.VMEM((4, slots, half_s), BF16),
            pltpu.VMEM((8, rows, half_s), BF16),
            pltpu.VMEM((8, rows, half_s), BF16),
            pltpu.VMEM((1, half_s), F32),
            pltpu.VMEM((8, 1, half_s), F32),
            pltpu.VMEM((8, half_s, voc), BF16),
            dma(()), dma(()), dma((8,)), dma((8,)),
        ] + [dma((16,))] * 8 + [dma((8,))] * 8 + [dma((16,))] * 2 + [dma((8,))] * 4,
        compiler_params=pltpu.CompilerParams(
            collective_id=0, has_side_effects=True, vmem_limit_bytes=LIMIT * 1024
        ),
        cost_estimate=pl.CostEstimate(flops=2600000000, bytes_accessed=11000000, transcendentals=400000),
    )(
        student_hidden, teacher_hidden, norm_gain.reshape(1, -1),
        episode_source.reshape(1, -1), lengths.reshape(1, -1),
        student_head.reshape(8, half_s, voc), teacher_head.reshape(8, half_t, voc),
    )
    results = (grad_head, loss, grad_hidden, grad_gain)
    grad_head, loss, grad_hidden, grad_gain = pl.pallas_call(
        finish,
        out_shape=tuple(jax.ShapeDtypeStruct(r.shape, r.dtype) for r in results),
        in_specs=[hbm] * 4,
        out_specs=(hbm,) * 4,
        scratch_shapes=[
            pltpu.VMEM((8, half_s, voc), BF16),
            pltpu.VMEM((rows, wide_s), BF16),
            pltpu.VMEM((1, wide_s), F32),
            pltpu.VMEM((1, 1), F32),
            dma((11,)), dma((11,)),
        ],
        compiler_params=pltpu.CompilerParams(vmem_limit_bytes=LIMIT * 1024),
        cost_estimate=pl.CostEstimate(flops=0, bytes_accessed=6400000, transcendentals=0),
    )(*results)
    return (loss[0, 0], grad_hidden, grad_gain.reshape(-1), grad_head.reshape(student_head.shape))


def realign(teacher_hidden, table, group_index, per_group):
    groups = table.shape[0]
    source_group = table // per_group
    source_local = table % per_group
    mine = (source_group == group_index).astype(jnp.int32)
    earlier = jnp.cumsum(mine, axis=1) - mine
    slot_ids = jnp.arange(MOST, dtype=jnp.int32)
    matches = mine[:, :, None] * (earlier[:, :, None] == slot_ids[None, None, :]).astype(jnp.int32)
    send_index = jnp.sum(matches * source_local[:, :, None], axis=1)
    features = teacher_hidden.shape[1]
    episodes = teacher_hidden.reshape(per_group, SEQ, features)
    outgoing = jnp.take(episodes, send_index, axis=0)
    incoming = lax.all_to_all(outgoing, "grp", split_axis=0, concat_axis=0, tiled=True)
    own_groups = lax.dynamic_index_in_dim(source_group, group_index, 0, keepdims=False)
    matching = (own_groups[:, None] == own_groups[None, :]).astype(jnp.int32)
    position = jnp.sum(jnp.tril(matching, -1), axis=1)
    flat_index = own_groups * MOST + position
    received = incoming.reshape(groups * MOST, SEQ, features)
    return jnp.take(received, flat_index, axis=0).reshape(per_group * SEQ, features)


def local(
    student_hidden, norm_gain, teacher_hidden, student_head, teacher_head, episode_source, lengths
):
    groups = lax.axis_size("grp")
    group_index = lax.axis_index("grp")
    rows_group = student_hidden.shape[0]
    per_group = rows_group // SEQ
    hidden_f32 = student_hidden.astype(jnp.float32)
    squares = lax.psum(jnp.sum(hidden_f32 * hidden_f32, axis=1), "voc")
    inverse_rms = lax.rsqrt(squares / DS + EPSILON)
    normed = (hidden_f32 * inverse_rms[:, None] * norm_gain[None, :]).astype(jnp.bfloat16)
    table = episode_source.reshape(groups, per_group)
    aligned = realign(teacher_hidden, table, group_index, per_group)
    teacher_rows, student_rows = (
        lax.all_gather(aligned, "voc", axis=1, tiled=True),
        lax.all_gather(normed, "voc", axis=1, tiled=True),
    )
    teacher_logits = jnp.dot(
        lax.all_gather(teacher_rows, "grp", axis=0, tiled=True),
        teacher_head,
        preferred_element_type=jnp.float32,
    )
    positions = jnp.arange(SEQ, dtype=jnp.int32)
    all_rows = lax.all_gather(student_rows, "grp", axis=0, tiled=True)
    student_logits = jnp.dot(all_rows, student_head, preferred_element_type=jnp.float32)
    lengths_f32 = lengths.astype(jnp.float32)
    valid = positions[None, :] < lengths[:, None]
    token_weight = jnp.where(
        valid, 1.0 / lengths_f32[:, None], jnp.zeros_like(lengths_f32)[:, None]
    ).reshape(-1)
    top_student, top_teacher = lax.pmax(
        (jnp.max(student_logits, axis=1), jnp.max(teacher_logits, axis=1)), ("grp", "voc")
    )
    exp_student = jnp.exp(student_logits - top_student[:, None])
    exp_teacher = jnp.exp(teacher_logits - top_teacher[:, None])
    total_student, total_teacher = lax.psum(
        (jnp.sum(exp_student, axis=1), jnp.sum(exp_teacher, axis=1)), ("grp", "voc")
    )
    log_student = student_logits - (top_student + jnp.log(total_student))[:, None]
    log_teacher = teacher_logits - (top_teacher + jnp.log(total_teacher))[:, None]
    prob_student = jnp.exp(log_student)
    log_ratio = log_student - log_teacher
    divergence = lax.psum(jnp.sum(prob_student * log_ratio, axis=1), ("grp", "voc"))
    loss = jnp.sum(token_weight * divergence)
    logit_grad = (token_weight[:, None] * prob_student * (log_ratio - divergence[:, None])).astype(
        jnp.bfloat16
    )
    grad_head = lax.dot_general(
        all_rows, logit_grad, (((0,), (0,)), ((), ())), preferred_element_type=jnp.float32
    ).astype(jnp.bfloat16)
    full_term = lax.dot_general(
        logit_grad, student_head, (((1,), (1,)), ((), ())), preferred_element_type=jnp.float32
    )
    feature_part = lax.psum_scatter(
        full_term.astype(jnp.bfloat16), "voc", scatter_dimension=1, tiled=True
    )
    normed_grad = lax.psum_scatter(feature_part, "grp", scatter_dimension=0, tiled=True).astype(
        jnp.float32
    )
    scaled = normed_grad * norm_gain[None, :]
    inner = lax.psum(jnp.sum(scaled * hidden_f32, axis=1), "voc")
    grad_hidden = (
        inverse_rms[:, None] * scaled - hidden_f32 * (inverse_rms**3)[:, None] * inner[:, None] / DS
    )
    grad_gain = lax.psum(jnp.sum(normed_grad * hidden_f32 * inverse_rms[:, None], axis=0), "grp")
    return (loss, grad_hidden.astype(jnp.bfloat16), grad_gain, grad_head)


def solution(mesh):
    placed = (
        P("grp", "voc"),
        P("voc"),
        P("grp", "voc"),
        P(None, ("grp", "voc")),
        P(None, ("grp", "voc")),
        P(),
        P(),
    )
    body = fused if tuple(mesh.shape.values()) == (8, 4) else local
    return jax.shard_map(
        body,
        mesh=mesh,
        in_specs=placed,
        out_specs=(P(), P("grp", "voc"), P("voc"), P(None, ("grp", "voc"))),
        check_vma=False,
    )
```

```python
import functools

import jax
import jax.numpy as jnp
from jax import lax
from jax.experimental import pallas as pl
from jax.experimental.pallas import tpu as pltpu
from jax.sharding import PartitionSpec as P

DS = 4096
SEQ = 2
MOST = 2


EPSILON = 1e-06

F32 = jnp.float32
BF16 = jnp.bfloat16
LIMIT = 65472
MESH = pl.DeviceIdType.MESH


def flip(number, mask):
    low, high = number % 2, number // 2
    if mask & 1:
        low = 1 - low
    if mask & 2:
        high = 1 - high
    return high * 2 + low


def merge(parts):
    top = functools.reduce(jnp.maximum, [p[0:1] for p in parts])
    top_t = functools.reduce(jnp.maximum, [p[2:3] for p in parts])
    total = total_t = ratio = logit = both = 0.0
    for p in parts:
        shift, shift_t = p[0:1] - top, p[2:3] - top_t
        factor, factor_t = jnp.exp(shift), jnp.exp(shift_t)
        live = factor > 0.0
        shift = jnp.where(live, shift, 0.0)
        gap = shift - jnp.where(live, shift_t, 0.0)
        total = total + factor * p[1:2]
        total_t = total_t + factor_t * p[3:4]
        ratio = ratio + factor * (p[4:5] + p[1:2] * gap)
        logit = logit + factor * (p[5:6] + p[1:2] * shift)
        both = both + factor * (p[6:7] + gap * p[5:6] + shift * p[4:5] + shift * gap * p[1:2])
    return jnp.concatenate([top, total, top_t, total_t, ratio, logit, both, jnp.zeros_like(top)], axis=0)


def kernel(
    sh_hbm, th_hbm, gain_hbm, source_hbm, lengths_hbm, w_hbm, t_hbm,
    loss_ref, gh_ref, gg_ref, head_hbm,
    wv, tv, sh_ref, gain_ref, source_ref, lengths_ref, pick_ref, in_s, in_t, s_blk, t_blk, hg, s_acc, t_acc, raw, sq, cols,
    st_a, st_b, g2, own, p_sib, r_sib, p_x, r_x, rb, rz, gp, gz, head,
    w_sem, t_sem, h_sem, l_sem, s1s, s1r, t1s, t1r, s2s, s2r, t2s, t2r, as_, ar, bs, br,
    qs, qr, xs, xr, zs, zr, ys, yr, us, ur,
):
    g = lax.axis_index("grp")
    v = lax.axis_index("voc")
    z, c = g // 2, g % 2
    k = v * 2 + c
    rows, half_s = in_s.shape[1], in_s.shape[2]
    half_t = in_t.shape[2]
    tokens = in_s.shape[0] * rows
    slots = s_acc.shape[0]

    def plane(vm, cm):
        return {"grp": z * 2 + (1 - c if cm else c), "voc": flip(v, vm)}

    def column(zm, cm):
        return {"grp": flip(z, zm) * 2 + (1 - c if cm else c), "voc": v}

    def slot(vm, cm):
        return flip(v, vm) * 2 + (1 - c if cm else c)

    sends = []

    def send(src, dst, ssem, rsem, to):
        copy = pltpu.make_async_remote_copy(
            src_ref=src, dst_ref=dst, send_sem=ssem, recv_sem=rsem, device_id=to, device_id_type=MESH
        )
        copy.start()
        sends.append(copy)

    def arrived(dst, ssem, rsem, to):
        pltpu.make_async_remote_copy(
            src_ref=dst, dst_ref=dst, send_sem=ssem, recv_sem=rsem, device_id=to, device_id_type=MESH
        ).wait_recv()

    def half(ref, number, width):
        return ref.at[:, pl.ds(pl.multiple_of(number * width, 128), width)]

    local_copies = [
        pltpu.make_async_copy(src, dst, l_sem.at[i])
        for i, (src, dst) in enumerate((
            (source_hbm, source_ref), (lengths_hbm, lengths_ref), (gain_hbm, gain_ref),
            (half(sh_hbm, c, half_s), in_s.at[g]), (half(th_hbm, c, half_t), in_t.at[g]), (sh_hbm, sh_ref),
        ))
    ]
    for copy in local_copies:
        copy.start()
    w_copy = pltpu.make_async_copy(w_hbm, wv, w_sem)
    t_copy = pltpu.make_async_copy(t_hbm, tv, t_sem)
    w_copy.start()
    t_copy.start()

    barrier = pltpu.get_barrier_semaphore()
    peers = [plane(m // 2, m % 2) for m in range(1, 8)] + [column(m // 2, m % 2) for m in range(2, 8)]
    for peer in peers:
        pl.semaphore_signal(barrier, inc=1, device_id=peer, device_id_type=MESH)
    pl.semaphore_wait(barrier, len(peers))

    def source(m):
        return flip(z, m // 2) * 2 + (1 - c if m % 2 else c)

    def spread_rows(ref, width, dst, ssem, rsem):
        for m in (6, 7, 4, 5, 2, 3, 1):
            other = 1 - c if m % 2 else c
            send(half(ref, other, width), dst.at[g], ssem.at[m], rsem.at[m], column(m // 2, m % 2))

    def rows_in(dst, ssem, rsem):
        for m in range(1, 8):
            arrived(dst.at[source(m)], ssem.at[m], rsem.at[m], column(m // 2, m % 2))

    spread_rows(sh_hbm, half_s, in_s, s1s, s1r)
    spread_rows(th_hbm, half_t, in_t, t1s, t1r)

    for copy in local_copies[:3]:
        copy.wait()
    episodes = source_ref.shape[1]
    line = lax.broadcasted_iota(jnp.int32, (8, episodes), 0)
    table = jnp.where(line == 0, source_ref[...], jnp.where(line == 1, lengths_ref[...], 0)).astype(F32).astype(BF16)
    spread = lax.broadcasted_iota(jnp.int32, (episodes, tokens), 1) // SEQ == lax.broadcasted_iota(
        jnp.int32, (episodes, tokens), 0
    )
    table = jnp.dot(table, spread.astype(F32).astype(BF16), preferred_element_type=F32)
    position = (lax.broadcasted_iota(jnp.int32, (1, tokens), 1) % SEQ).astype(F32)
    row_source = table[0:1] * SEQ + position
    row_length = table[1:2]
    row_valid = (position < row_length).astype(F32)
    before = lax.broadcasted_iota(jnp.int32, (tokens, tokens), 0) < lax.broadcasted_iota(jnp.int32, (tokens, tokens), 1)
    rank = jnp.dot(
        jnp.broadcast_to(row_valid, (8, tokens)).astype(BF16), before.astype(F32).astype(BF16),
        preferred_element_type=F32,
    )[0:1]
    slot_line = lax.broadcasted_iota(jnp.int32, (slots, tokens), 0).astype(F32)
    pick = jnp.where(slot_line == rank, row_valid, 0.0).astype(BF16)
    pick_ref[...] = pick
    line = lax.broadcasted_iota(jnp.int32, (8, tokens), 0)
    both = jnp.where(line == 0, row_source, jnp.where(line == 1, row_length, 0.0)).astype(BF16)
    slot_table = lax.dot_general(pick, both, (((1,), (1,)), ((), ())), preferred_element_type=F32)
    slot_source, slot_length = slot_table[:, 0:1], slot_table[:, 1:2]
    weight = jnp.where(slot_length > 0.0, 1.0 / jnp.maximum(slot_length, 1.0), 0.0)
    teacher_lane = lax.broadcasted_iota(jnp.int32, (slots, tokens), 1).astype(F32)
    pick_t = jnp.where((slot_source == teacher_lane) & (slot_length > 0.0), 1.0, 0.0).astype(BF16)

    gain = gain_ref[...]
    own_gain = jnp.where(c == 0, gain[:, :half_s], gain[:, half_s:])

    halves = (slice(0, slots // 2), slice(slots // 2, slots))

    def share(blk, ssem, rsem):
        for vm, half_id in ((1, 0), (2, 1), (1, 1), (2, 0)):
            piece = blk.at[k, halves[half_id]]
            send(piece, piece, ssem.at[vm * 4 + half_id], rsem.at[vm * 4 + half_id], plane(vm, 0))
        send(blk.at[k], blk.at[k], ssem.at[2], rsem.at[2], plane(0, 1))

    def landed(blk, ssem, rsem, vm, half_id):
        piece = blk.at[slot(vm, 0), halves[half_id]]
        arrived(piece, ssem.at[vm * 4 + half_id], rsem.at[vm * 4 + half_id], plane(vm, 0))
        return piece

    def relay(blk, ssem, rsem):
        for vm, half_id in ((1, 0), (2, 1)):
            piece = landed(blk, ssem, rsem, vm, half_id)
            send(piece, piece, ssem.at[12 + half_id], rsem.at[12 + half_id], plane(3 - vm, 0))

    def to_sibling(blk, ssem, rsem, vm):
        for half_id in {1: (1,), 2: (0,), 3: (0, 1)}[vm]:
            landed(blk, ssem, rsem, vm, half_id)
        at = slot(vm, 0)
        send(blk.at[at], blk.at[at], ssem.at[vm * 4 + 2], rsem.at[vm * 4 + 2], plane(0, 1))

    def sibling(blk, ssem, rsem, vm):
        arrived(blk.at[slot(vm, 1)], ssem.at[vm * 4 + 2], rsem.at[vm * 4 + 2], plane(0, 1))

    rows_in(in_s, s1s, s1r)
    for copy in local_copies[3:]:
        copy.wait()
    block = jnp.concatenate([in_s[i].astype(F32) for i in range(8)], axis=0).astype(BF16)
    block = jnp.dot(pick, block, preferred_element_type=F32)
    raw[...] = block
    s_blk[k] = (block * own_gain).astype(BF16)
    share(s_blk, s2s, s2r)
    squares = block * block
    partial = squares[:, 0:128]
    for i in range(1, half_s // 128):
        partial = partial + squares[:, i * 128:(i + 1) * 128]
    sq[k] = jnp.broadcast_to(jnp.sum(jnp.transpose(partial), axis=0, keepdims=True), (8, slots))
    for m in range(1, 8):
        send(sq.at[k], sq.at[k], us.at[m], ur.at[m], plane(m // 2, m % 2))
    s_acc[...] = jnp.zeros_like(s_acc)
    t_acc[...] = jnp.zeros_like(t_acc)

    def student_block(at):
        s_acc[...] += jnp.dot(s_blk[at], wv[at], preferred_element_type=F32)

    def teacher_block(at):
        t_acc[...] += jnp.dot(t_blk[at], tv[at], preferred_element_type=F32)

    w_copy.wait()
    student_block(k)
    sibling(s_blk, s2s, s2r, 0)
    student_block(slot(0, 1))
    relay(s_blk, s2s, s2r)
    rows_in(in_t, t1s, t1r)
    block = jnp.concatenate([in_t[i].astype(F32) for i in range(8)], axis=0).astype(BF16)
    t_blk[k] = jnp.dot(pick_t, block, preferred_element_type=F32).astype(BF16)
    share(t_blk, t2s, t2r)

    to_sibling(s_blk, s2s, s2r, 1)
    to_sibling(s_blk, s2s, s2r, 2)
    t_copy.wait()
    teacher_block(k)
    student_block(slot(1, 0))
    student_block(slot(2, 0))
    relay(t_blk, t2s, t2r)
    sibling(s_blk, s2s, s2r, 1)
    student_block(slot(1, 1))
    sibling(s_blk, s2s, s2r, 2)
    student_block(slot(2, 1))
    to_sibling(s_blk, s2s, s2r, 3)
    student_block(slot(3, 0))
    sibling(t_blk, t2s, t2r, 0)
    teacher_block(slot(0, 1))
    to_sibling(t_blk, t2s, t2r, 1)
    to_sibling(t_blk, t2s, t2r, 2)
    sibling(s_blk, s2s, s2r, 3)
    student_block(slot(3, 1))
    for m in range(1, 8):
        arrived(sq.at[slot(m // 2, m % 2)], us.at[m], ur.at[m], plane(m // 2, m % 2))
    sums = sq[0, 0:1]
    for i in range(1, 8):
        sums = sums + sq[i, 0:1]
    sums = lax.rsqrt(sums / DS + EPSILON)
    inv = jnp.transpose(jnp.broadcast_to(sums, (slots, slots)))[:, 0:1]
    live = weight > 0.0
    teacher_block(slot(1, 0))
    teacher_block(slot(2, 0))
    for vm in (1, 2):
        sibling(t_blk, t2s, t2r, vm)
        teacher_block(slot(vm, 1))
    to_sibling(t_blk, t2s, t2r, 3)
    teacher_block(slot(3, 0))
    sibling(t_blk, t2s, t2r, 3)
    teacher_block(slot(3, 1))

    s_log = s_acc[...] * inv
    t_log = t_acc[...]
    top = jnp.max(s_log, axis=1, keepdims=True)
    top_t = jnp.max(t_log, axis=1, keepdims=True)
    a = s_log - top
    b = t_log - top_t
    e = jnp.exp(a)
    ea = e * a
    d = a - b
    figures = [
        top, jnp.sum(e, axis=1, keepdims=True), top_t, jnp.sum(jnp.exp(b), axis=1, keepdims=True),
        jnp.sum(e * d, axis=1, keepdims=True), jnp.sum(ea, axis=1, keepdims=True),
        jnp.sum(ea * d, axis=1, keepdims=True),
    ]
    lane = lax.broadcasted_iota(jnp.int32, (slots, 128), 1)
    packed = jnp.zeros((slots, 128), F32)
    for i, figure in enumerate(figures):
        packed = jnp.where(lane == i, figure, packed)
    st_a[k] = jnp.transpose(packed)[0:8, :]
    for m in range(1, 8):
        send(st_a.at[k], st_a.at[k], as_.at[m], ar.at[m], plane(m // 2, m % 2))
    for i in range(4):
        hg[i] = jnp.transpose(s_blk[i].astype(F32)).astype(BF16)
    for m in range(1, 8):
        arrived(st_a.at[slot(m // 2, m % 2)], as_.at[m], ar.at[m], plane(m // 2, m % 2))
    st_b[z] = merge([st_a[i] for i in range(8)])
    for m in range(1, 4):
        send(st_b.at[z], st_b.at[z], bs.at[m], br.at[m], column(m, 0))
    for i in range(4, 8):
        hg[i] = jnp.transpose(s_blk[i].astype(F32)).astype(BF16)
    for m in range(1, 4):
        arrived(st_b.at[flip(z, m)], bs.at[m], br.at[m], column(m, 0))
    full = merge([st_b[i] for i in range(4)])
    total = full[1:2]
    lse = full[0:1] + jnp.log(total)
    lse_t = full[2:3] + jnp.log(full[3:4])
    mean_ratio, mean_logit = full[4:5] / total, full[5:6] / total
    divergence = mean_ratio - jnp.log(total) + jnp.log(full[3:4])
    offset = lse - lse_t + divergence
    cov = full[6:7] / total - mean_ratio * mean_logit
    back = jnp.concatenate([lse, offset, divergence, cov, jnp.zeros((slots - 4, slots), F32)], axis=0)
    back = jnp.transpose(back)
    prob = jnp.exp(s_log - back[:, 0:1])
    grad = (weight * inv) * prob * (s_log - t_log - back[:, 1:2])
    g2[...] = jnp.where(live, grad, 0.0).astype(BF16)

    def block_grad(at):
        return lax.dot_general(g2[...], wv[at], (((1,), (1,)), ((), ())), preferred_element_type=F32)

    order = (3, 1, 2, 0)
    part = half_s // 2
    for vm in order:
        p_sib[vm] = block_grad(slot(vm, 1)).astype(BF16)
        send(p_sib.at[vm], r_sib.at[vm], qs.at[vm], qr.at[vm], plane(0, 1))
    for vm in order:
        mine = block_grad(slot(vm, 0))
        arrived(r_sib.at[vm], qs.at[vm], qr.at[vm], plane(0, 1))
        mine = mine + r_sib[vm].astype(F32)
        if vm:
            p_x[vm] = mine.astype(BF16)
            send(p_x.at[vm, :, 0:part], r_x.at[vm, :, 0:part], xs.at[vm], xr.at[vm], plane(vm, 0))
        else:
            own[...] = mine
    for vm in (3, 1, 2):
        send(p_x.at[vm, :, part:], r_x.at[vm, :, part:], xs.at[vm + 4], xr.at[vm + 4], plane(vm, 0))

    loss_ref[...] = jnp.sum(jnp.where(live, weight * back[:, 2:3], 0.0), axis=0, keepdims=True)
    lane = lax.broadcasted_iota(jnp.int32, (slots, 128), 1)
    figure = jnp.where(live, weight * inv * inv * back[:, 3:4] / DS, 0.0)
    hi = figure.astype(BF16).astype(F32)
    mid = (figure - hi).astype(BF16).astype(F32)
    lo = figure - hi - mid
    packed = jnp.where(lane == 0, hi, jnp.where(lane == 1, mid, jnp.where(lane == 2, lo, 0.0))).astype(BF16)
    packed = lax.dot_general(pick_ref[...], packed, (((0,), (0,)), ((), ())), preferred_element_type=F32)
    cols[...] = jnp.broadcast_to(jnp.sum(packed, axis=1, keepdims=True), cols.shape)

    def head_block(i):
        head[i] = jnp.dot(hg[i], g2[...], preferred_element_type=F32).astype(BF16)
        copy = pltpu.make_async_copy(head.at[i], head_hbm.at[i], h_sem.at[i])
        copy.start()
        head_copies.append(copy)

    head_copies = []
    for i in range(4):
        head_block(i)
    for h in range(2):
        at = slice(h * part, (h + 1) * part)
        for vm in (1, 2, 3):
            arrived(r_x.at[vm, :, at], xs.at[vm + 4 * h], xr.at[vm + 4 * h], plane(vm, 0))
        total = own[:, at]
        for vm in (1, 2, 3):
            total = total + r_x[vm, :, at].astype(F32)
        spread_out = lax.dot_general(
            pick_ref[...], total.astype(BF16), (((0,), (0,)), ((), ())), preferred_element_type=F32
        )
        for i in range(8):
            rb[i, :, at] = spread_out[i * rows:(i + 1) * rows].astype(BF16)
        for m in range(1, 8):
            send(
                rb.at[source(m), :, at], rz.at[g, :, at], zs.at[m + 8 * h], zr.at[m + 8 * h],
                column(m // 2, m % 2),
            )
        gp[:, at] = jnp.sum(
            total * raw[:, at], axis=0, keepdims=True
        )
        if h:
            for m in range(1, 8):
                send(gp, gz.at[g], ys.at[m], yr.at[m], column(m // 2, m % 2))
        for i in range(4 + 2 * h, 6 + 2 * h):
            head_block(i)
    rz[g] = rb[g]
    gz[g] = gp[...]
    for h in range(2):
        at = slice(h * part, (h + 1) * part)
        for m in range(1, 8):
            arrived(rz.at[source(m), :, at], zs.at[m + 8 * h], zr.at[m + 8 * h], column(m // 2, m % 2))
    own_cols = cols[pl.ds(pl.multiple_of(g * rows, 8), rows), :][:, 0:1]
    for h in range(2):
        at = slice(h * half_s, (h + 1) * half_s)
        ng = rz[h].astype(F32)
        for i in range(1, 4):
            ng = ng + rz[2 * i + h].astype(F32)
        hid = sh_ref[:, at].astype(F32)
        gh_ref[:, at] = (gain_ref[:, at] * ng - hid * own_cols).astype(BF16)
    for m in range(1, 8):
        arrived(gz.at[source(m)], ys.at[m], yr.at[m], column(m // 2, m % 2))
    for h in range(2):
        at = slice(h * half_s, (h + 1) * half_s)
        ng = gz[h]
        for i in range(1, 4):
            ng = ng + gz[2 * i + h]
        gg_ref[:, at] = ng
    for copy in head_copies:
        copy.wait()
    for copy in sends:
        copy.wait_send()


def finish(
    head_in, loss_in, hidden_in, gain_in, head_out, loss_out, hidden_out, gain_out,
    head, hidden, gain, loss, in_sem, out_sem,
):
    moves = [(head_in.at[i], head.at[i], head_out.at[i]) for i in range(8)]
    moves += [(hidden_in, hidden, hidden_out), (gain_in, gain, gain_out), (loss_in, loss, loss_out)]
    inward = [pltpu.make_async_copy(a, b, in_sem.at[i]) for i, (a, b, _) in enumerate(moves)]
    outward = [pltpu.make_async_copy(b, c, out_sem.at[i]) for i, (_, b, c) in enumerate(moves)]
    for copy in inward:
        copy.start()
    for first, second in zip(inward, outward):
        first.wait()
        second.start()
    for copy in outward:
        copy.wait()


def fused(
    student_hidden, norm_gain, teacher_hidden, student_head, teacher_head, episode_source, lengths
):
    rows, wide_s = student_hidden.shape
    wide_t = teacher_hidden.shape[1]
    tokens = rows * lax.axis_size("grp")
    voc = student_head.shape[1]
    half_s, half_t = wide_s // 2, wide_t // 2
    slots = -(-(tokens * 5 // 8) // 128) * 128
    vmem = pl.BlockSpec(memory_space=pltpu.VMEM)
    hbm = pl.BlockSpec(memory_space=pltpu.HBM)
    dma = pltpu.SemaphoreType.DMA
    loss, grad_hidden, grad_gain, grad_head = pl.pallas_call(
        kernel,
        out_shape=(
            jax.ShapeDtypeStruct((1, 1), F32),
            jax.ShapeDtypeStruct((rows, wide_s), BF16),
            jax.ShapeDtypeStruct((1, wide_s), F32),
            jax.ShapeDtypeStruct((8, half_s, voc), BF16),
        ),
        in_specs=[hbm] * 7,
        out_specs=(vmem, vmem, vmem, hbm),
        scratch_shapes=[
            pltpu.VMEM((8, half_s, voc), BF16),
            pltpu.VMEM((8, half_t, voc), BF16),
            pltpu.VMEM((rows, wide_s), BF16),
            pltpu.VMEM((1, wide_s), F32),
            pltpu.VMEM((1, episode_source.shape[0]), jnp.int32),
            pltpu.VMEM((1, episode_source.shape[0]), jnp.int32),
            pltpu.VMEM((slots, tokens), BF16),
            pltpu.VMEM((8, rows, half_s), BF16),
            pltpu.VMEM((8, rows, half_t), BF16),
            pltpu.VMEM((8, slots, half_s), BF16),
            pltpu.VMEM((8, slots, half_t), BF16),
            pltpu.VMEM((8, half_s, slots), BF16),
            pltpu.VMEM((slots, voc), F32),
            pltpu.VMEM((slots, voc), F32),
            pltpu.VMEM((slots, half_s), F32),
            pltpu.VMEM((8, 8, slots), F32),
            pltpu.VMEM((tokens, 128), F32),
            pltpu.VMEM((8, 8, slots), F32),
            pltpu.VMEM((4, 8, slots), F32),
            pltpu.VMEM((slots, voc), BF16),
            pltpu.VMEM((slots, half_s), F32),
            pltpu.VMEM((4, slots, half_s), BF16),
            pltpu.VMEM((4, slots, half_s), BF16),
            pltpu.VMEM((4, slots, half_s), BF16),
            pltpu.VMEM((4, slots, half_s), BF16),
            pltpu.VMEM((8, rows, half_s), BF16),
            pltpu.VMEM((8, rows, half_s), BF16),
            pltpu.VMEM((1, half_s), F32),
            pltpu.VMEM((8, 1, half_s), F32),
            pltpu.VMEM((8, half_s, voc), BF16),
            dma(()), dma(()), dma((8,)), dma((8,)),
        ] + [dma((16,))] * 8 + [dma((8,))] * 8 + [dma((16,))] * 2 + [dma((8,))] * 4,
        compiler_params=pltpu.CompilerParams(
            collective_id=0, has_side_effects=True, vmem_limit_bytes=LIMIT * 1024
        ),
        cost_estimate=pl.CostEstimate(flops=2600000000, bytes_accessed=11000000, transcendentals=400000),
    )(
        student_hidden, teacher_hidden, norm_gain.reshape(1, -1),
        episode_source.reshape(1, -1), lengths.reshape(1, -1),
        student_head.reshape(8, half_s, voc), teacher_head.reshape(8, half_t, voc),
    )
    results = (grad_head, loss, grad_hidden, grad_gain)
    grad_head, loss, grad_hidden, grad_gain = pl.pallas_call(
        finish,
        out_shape=tuple(jax.ShapeDtypeStruct(r.shape, r.dtype) for r in results),
        in_specs=[hbm] * 4,
        out_specs=(hbm,) * 4,
        scratch_shapes=[
            pltpu.VMEM((8, half_s, voc), BF16),
            pltpu.VMEM((rows, wide_s), BF16),
            pltpu.VMEM((1, wide_s), F32),
            pltpu.VMEM((1, 1), F32),
            dma((11,)), dma((11,)),
        ],
        compiler_params=pltpu.CompilerParams(vmem_limit_bytes=LIMIT * 1024),
        cost_estimate=pl.CostEstimate(flops=0, bytes_accessed=6400000, transcendentals=0),
    )(*results)
    return (loss[0, 0], grad_hidden, grad_gain.reshape(-1), grad_head.reshape(student_head.shape))


def realign(teacher_hidden, table, group_index, per_group):
    groups = table.shape[0]
    source_group = table // per_group
    source_local = table % per_group
    mine = (source_group == group_index).astype(jnp.int32)
    earlier = jnp.cumsum(mine, axis=1) - mine
    slot_ids = jnp.arange(MOST, dtype=jnp.int32)
    matches = mine[:, :, None] * (earlier[:, :, None] == slot_ids[None, None, :]).astype(jnp.int32)
    send_index = jnp.sum(matches * source_local[:, :, None], axis=1)
    features = teacher_hidden.shape[1]
    episodes = teacher_hidden.reshape(per_group, SEQ, features)
    outgoing = jnp.take(episodes, send_index, axis=0)
    incoming = lax.all_to_all(outgoing, "grp", split_axis=0, concat_axis=0, tiled=True)
    own_groups = lax.dynamic_index_in_dim(source_group, group_index, 0, keepdims=False)
    matching = (own_groups[:, None] == own_groups[None, :]).astype(jnp.int32)
    position = jnp.sum(jnp.tril(matching, -1), axis=1)
    flat_index = own_groups * MOST + position
    received = incoming.reshape(groups * MOST, SEQ, features)
    return jnp.take(received, flat_index, axis=0).reshape(per_group * SEQ, features)


def local(
    student_hidden, norm_gain, teacher_hidden, student_head, teacher_head, episode_source, lengths
):
    groups = lax.axis_size("grp")
    group_index = lax.axis_index("grp")
    rows_group = student_hidden.shape[0]
    per_group = rows_group // SEQ
    hidden_f32 = student_hidden.astype(jnp.float32)
    squares = lax.psum(jnp.sum(hidden_f32 * hidden_f32, axis=1), "voc")
    inverse_rms = lax.rsqrt(squares / DS + EPSILON)
    normed = (hidden_f32 * inverse_rms[:, None] * norm_gain[None, :]).astype(jnp.bfloat16)
    table = episode_source.reshape(groups, per_group)
    aligned = realign(teacher_hidden, table, group_index, per_group)
    teacher_rows, student_rows = (
        lax.all_gather(aligned, "voc", axis=1, tiled=True),
        lax.all_gather(normed, "voc", axis=1, tiled=True),
    )
    teacher_logits = jnp.dot(
        lax.all_gather(teacher_rows, "grp", axis=0, tiled=True),
        teacher_head,
        preferred_element_type=jnp.float32,
    )
    positions = jnp.arange(SEQ, dtype=jnp.int32)
    all_rows = lax.all_gather(student_rows, "grp", axis=0, tiled=True)
    student_logits = jnp.dot(all_rows, student_head, preferred_element_type=jnp.float32)
    lengths_f32 = lengths.astype(jnp.float32)
    valid = positions[None, :] < lengths[:, None]
    token_weight = jnp.where(
        valid, 1.0 / lengths_f32[:, None], jnp.zeros_like(lengths_f32)[:, None]
    ).reshape(-1)
    top_student, top_teacher = lax.pmax(
        (jnp.max(student_logits, axis=1), jnp.max(teacher_logits, axis=1)), ("grp", "voc")
    )
    exp_student = jnp.exp(student_logits - top_student[:, None])
    exp_teacher = jnp.exp(teacher_logits - top_teacher[:, None])
    total_student, total_teacher = lax.psum(
        (jnp.sum(exp_student, axis=1), jnp.sum(exp_teacher, axis=1)), ("grp", "voc")
    )
    log_student = student_logits - (top_student + jnp.log(total_student))[:, None]
    log_teacher = teacher_logits - (top_teacher + jnp.log(total_teacher))[:, None]
    prob_student = jnp.exp(log_student)
    log_ratio = log_student - log_teacher
    divergence = lax.psum(jnp.sum(prob_student * log_ratio, axis=1), ("grp", "voc"))
    loss = jnp.sum(token_weight * divergence)
    logit_grad = (token_weight[:, None] * prob_student * (log_ratio - divergence[:, None])).astype(
        jnp.bfloat16
    )
    grad_head = lax.dot_general(
        all_rows, logit_grad, (((0,), (0,)), ((), ())), preferred_element_type=jnp.float32
    ).astype(jnp.bfloat16)
    full_term = lax.dot_general(
        logit_grad, student_head, (((1,), (1,)), ((), ())), preferred_element_type=jnp.float32
    )
    feature_part = lax.psum_scatter(
        full_term.astype(jnp.bfloat16), "voc", scatter_dimension=1, tiled=True
    )
    normed_grad = lax.psum_scatter(feature_part, "grp", scatter_dimension=0, tiled=True).astype(
        jnp.float32
    )
    scaled = normed_grad * norm_gain[None, :]
    inner = lax.psum(jnp.sum(scaled * hidden_f32, axis=1), "voc")
    grad_hidden = (
        inverse_rms[:, None] * scaled - hidden_f32 * (inverse_rms**3)[:, None] * inner[:, None] / DS
    )
    grad_gain = lax.psum(jnp.sum(normed_grad * hidden_f32 * inverse_rms[:, None], axis=0), "grp")
    return (loss, grad_hidden.astype(jnp.bfloat16), grad_gain, grad_head)


def solution(mesh):
    placed = (
        P("grp", "voc"),
        P("voc"),
        P("grp", "voc"),
        P(None, ("grp", "voc")),
        P(None, ("grp", "voc")),
        P(),
        P(),
    )
    body = fused if tuple(mesh.shape.values()) == (8, 4) else local
    return jax.shard_map(
        body,
        mesh=mesh,
        in_specs=placed,
        out_specs=(P(), P("grp", "voc"), P("voc"), P(None, ("grp", "voc"))),
        check_vma=False,
    )
```

```python
import functools

import jax
import jax.numpy as jnp
from jax import lax
from jax.experimental import pallas as pl
from jax.experimental.pallas import tpu as pltpu
from jax.sharding import PartitionSpec as P

DS = 4096
SEQ = 2
MOST = 2


EPSILON = 1e-06

F32 = jnp.float32
BF16 = jnp.bfloat16
LIMIT = 65472
MESH = pl.DeviceIdType.MESH


def flip(number, mask):
    low, high = number % 2, number // 2
    if mask & 1:
        low = 1 - low
    if mask & 2:
        high = 1 - high
    return high * 2 + low


def merge(parts):
    top = functools.reduce(jnp.maximum, [p[0:1] for p in parts])
    top_t = functools.reduce(jnp.maximum, [p[2:3] for p in parts])
    total = total_t = ratio = logit = both = 0.0
    for p in parts:
        shift, shift_t = p[0:1] - top, p[2:3] - top_t
        factor, factor_t = jnp.exp(shift), jnp.exp(shift_t)
        live = factor > 0.0
        shift = jnp.where(live, shift, 0.0)
        gap = shift - jnp.where(live, shift_t, 0.0)
        total = total + factor * p[1:2]
        total_t = total_t + factor_t * p[3:4]
        ratio = ratio + factor * (p[4:5] + p[1:2] * gap)
        logit = logit + factor * (p[5:6] + p[1:2] * shift)
        both = both + factor * (p[6:7] + gap * p[5:6] + shift * p[4:5] + shift * gap * p[1:2])
    return jnp.concatenate([top, total, top_t, total_t, ratio, logit, both, jnp.zeros_like(top)], axis=0)


def kernel(
    sh_hbm, th_hbm, gain_hbm, source_hbm, lengths_hbm, w_hbm, t_hbm,
    loss_ref, gh_ref, gg_ref, head_hbm,
    wv, tv, sh_ref, gain_ref, source_ref, lengths_ref, pick_ref, in_s, in_t, s_blk, t_blk, hg, s_acc, t_acc, raw, sq, cols,
    st_a, st_b, g2, own, p_sib, r_sib, p_x, r_x, rb, rz, gp, gz, head,
    w_sem, t_sem, h_sem, l_sem, s1s, s1r, t1s, t1r, s2s, s2r, t2s, t2r, as_, ar, bs, br,
    qs, qr, xs, xr, zs, zr, ys, yr, us, ur,
):
    g = lax.axis_index("grp")
    v = lax.axis_index("voc")
    z, c = g // 2, g % 2
    k = v * 2 + c
    rows, half_s = in_s.shape[1], in_s.shape[2]
    half_t = in_t.shape[2]
    tokens = in_s.shape[0] * rows
    slots = s_acc.shape[0]

    def plane(vm, cm):
        return {"grp": z * 2 + (1 - c if cm else c), "voc": flip(v, vm)}

    def column(zm, cm):
        return {"grp": flip(z, zm) * 2 + (1 - c if cm else c), "voc": v}

    def slot(vm, cm):
        return flip(v, vm) * 2 + (1 - c if cm else c)

    sends = []

    def send(src, dst, ssem, rsem, to):
        copy = pltpu.make_async_remote_copy(
            src_ref=src, dst_ref=dst, send_sem=ssem, recv_sem=rsem, device_id=to, device_id_type=MESH
        )
        copy.start()
        sends.append(copy)

    def arrived(dst, ssem, rsem, to):
        pltpu.make_async_remote_copy(
            src_ref=dst, dst_ref=dst, send_sem=ssem, recv_sem=rsem, device_id=to, device_id_type=MESH
        ).wait_recv()

    def half(ref, number, width):
        return ref.at[:, pl.ds(pl.multiple_of(number * width, 128), width)]

    local_copies = [
        pltpu.make_async_copy(src, dst, l_sem.at[i])
        for i, (src, dst) in enumerate((
            (source_hbm, source_ref), (lengths_hbm, lengths_ref), (gain_hbm, gain_ref),
            (half(sh_hbm, c, half_s), in_s.at[g]), (half(th_hbm, c, half_t), in_t.at[g]), (sh_hbm, sh_ref),
        ))
    ]
    for copy in local_copies:
        copy.start()
    w_copy = pltpu.make_async_copy(w_hbm, wv, w_sem)
    t_copy = pltpu.make_async_copy(t_hbm, tv, t_sem)
    w_copy.start()
    t_copy.start()

    barrier = pltpu.get_barrier_semaphore()
    peers = [plane(m // 2, m % 2) for m in range(1, 8)] + [column(m // 2, m % 2) for m in range(2, 8)]
    for peer in peers:
        pl.semaphore_signal(barrier, inc=1, device_id=peer, device_id_type=MESH)
    pl.semaphore_wait(barrier, len(peers))

    def source(m):
        return flip(z, m // 2) * 2 + (1 - c if m % 2 else c)

    middle = (z == 1) | (z == 2)
    middle_sends = []

    def spread_rows(ref, width, dst, ssem, rsem):
        for m in range(1, 8):
            other = 1 - c if m % 2 else c
            if m < 6:
                send(half(ref, other, width), dst.at[g], ssem.at[m], rsem.at[m], column(m // 2, m % 2))
            else:
                middle_sends.append(pltpu.make_async_remote_copy(
                    src_ref=half(ref, other, width), dst_ref=dst.at[g], send_sem=ssem.at[m], recv_sem=rsem.at[m],
                    device_id=column(m // 2, m % 2), device_id_type=MESH,
                ))
                pl.when(middle)(middle_sends[-1].start)

    def hand_on(dst, ssem, rsem):
        for m in (4, 5):
            piece = dst.at[source(m)]
            arrived(piece, ssem.at[m], rsem.at[m], column(2, m % 2))
            middle_sends.append(pltpu.make_async_remote_copy(
                src_ref=piece, dst_ref=piece, send_sem=ssem.at[m + 4], recv_sem=rsem.at[m + 2],
                device_id=column(1, 0), device_id_type=MESH,
            ))
            pl.when(middle)(middle_sends[-1].start)

    def rows_in(dst, ssem, rsem):
        for m in (1, 2, 3, 6, 7):
            arrived(dst.at[source(m)], ssem.at[m], rsem.at[m], column(m // 2, m % 2))

    spread_rows(sh_hbm, half_s, in_s, s1s, s1r)
    spread_rows(th_hbm, half_t, in_t, t1s, t1r)

    for copy in local_copies[:3]:
        copy.wait()
    episodes = source_ref.shape[1]
    line = lax.broadcasted_iota(jnp.int32, (8, episodes), 0)
    table = jnp.where(line == 0, source_ref[...], jnp.where(line == 1, lengths_ref[...], 0)).astype(F32).astype(BF16)
    spread = lax.broadcasted_iota(jnp.int32, (episodes, tokens), 1) // SEQ == lax.broadcasted_iota(
        jnp.int32, (episodes, tokens), 0
    )
    table = jnp.dot(table, spread.astype(F32).astype(BF16), preferred_element_type=F32)
    position = (lax.broadcasted_iota(jnp.int32, (1, tokens), 1) % SEQ).astype(F32)
    row_source = table[0:1] * SEQ + position
    row_length = table[1:2]
    row_valid = (position < row_length).astype(F32)
    before = lax.broadcasted_iota(jnp.int32, (tokens, tokens), 0) < lax.broadcasted_iota(jnp.int32, (tokens, tokens), 1)
    rank = jnp.dot(
        jnp.broadcast_to(row_valid, (8, tokens)).astype(BF16), before.astype(F32).astype(BF16),
        preferred_element_type=F32,
    )[0:1]
    slot_line = lax.broadcasted_iota(jnp.int32, (slots, tokens), 0).astype(F32)
    pick = jnp.where(slot_line == rank, row_valid, 0.0).astype(BF16)
    pick_ref[...] = pick
    line = lax.broadcasted_iota(jnp.int32, (8, tokens), 0)
    both = jnp.where(line == 0, row_source, jnp.where(line == 1, row_length, 0.0)).astype(BF16)
    slot_table = lax.dot_general(pick, both, (((1,), (1,)), ((), ())), preferred_element_type=F32)
    slot_source, slot_length = slot_table[:, 0:1], slot_table[:, 1:2]
    weight = jnp.where(slot_length > 0.0, 1.0 / jnp.maximum(slot_length, 1.0), 0.0)
    teacher_lane = lax.broadcasted_iota(jnp.int32, (slots, tokens), 1).astype(F32)
    pick_t = jnp.where((slot_source == teacher_lane) & (slot_length > 0.0), 1.0, 0.0).astype(BF16)

    gain = gain_ref[...]
    own_gain = jnp.where(c == 0, gain[:, :half_s], gain[:, half_s:])

    halves = (slice(0, slots // 2), slice(slots // 2, slots))

    def share(blk, ssem, rsem):
        for vm, half_id in ((1, 0), (2, 1), (1, 1), (2, 0)):
            piece = blk.at[k, halves[half_id]]
            send(piece, piece, ssem.at[vm * 4 + half_id], rsem.at[vm * 4 + half_id], plane(vm, 0))
        send(blk.at[k], blk.at[k], ssem.at[2], rsem.at[2], plane(0, 1))

    def landed(blk, ssem, rsem, vm, half_id):
        piece = blk.at[slot(vm, 0), halves[half_id]]
        arrived(piece, ssem.at[vm * 4 + half_id], rsem.at[vm * 4 + half_id], plane(vm, 0))
        return piece

    def relay(blk, ssem, rsem):
        for vm, half_id in ((1, 0), (2, 1)):
            piece = landed(blk, ssem, rsem, vm, half_id)
            send(piece, piece, ssem.at[12 + half_id], rsem.at[12 + half_id], plane(3 - vm, 0))

    def to_sibling(blk, ssem, rsem, vm):
        for half_id in {1: (1,), 2: (0,), 3: (0, 1)}[vm]:
            landed(blk, ssem, rsem, vm, half_id)
        at = slot(vm, 0)
        send(blk.at[at], blk.at[at], ssem.at[vm * 4 + 2], rsem.at[vm * 4 + 2], plane(0, 1))

    def sibling(blk, ssem, rsem, vm):
        arrived(blk.at[slot(vm, 1)], ssem.at[vm * 4 + 2], rsem.at[vm * 4 + 2], plane(0, 1))

    hand_on(in_s, s1s, s1r)
    rows_in(in_s, s1s, s1r)
    for copy in local_copies[3:]:
        copy.wait()
    block = jnp.concatenate([in_s[i].astype(F32) for i in range(8)], axis=0).astype(BF16)
    block = jnp.dot(pick, block, preferred_element_type=F32)
    raw[...] = block
    s_blk[k] = (block * own_gain).astype(BF16)
    share(s_blk, s2s, s2r)
    squares = block * block
    partial = squares[:, 0:128]
    for i in range(1, half_s // 128):
        partial = partial + squares[:, i * 128:(i + 1) * 128]
    sq[k] = jnp.broadcast_to(jnp.sum(jnp.transpose(partial), axis=0, keepdims=True), (8, slots))
    for m in range(1, 8):
        send(sq.at[k], sq.at[k], us.at[m], ur.at[m], plane(m // 2, m % 2))
    s_acc[...] = jnp.zeros_like(s_acc)
    t_acc[...] = jnp.zeros_like(t_acc)

    def student_block(at):
        s_acc[...] += jnp.dot(s_blk[at], wv[at], preferred_element_type=F32)

    def teacher_block(at):
        t_acc[...] += jnp.dot(t_blk[at], tv[at], preferred_element_type=F32)

    w_copy.wait()
    student_block(k)
    hand_on(in_t, t1s, t1r)
    sibling(s_blk, s2s, s2r, 0)
    student_block(slot(0, 1))
    relay(s_blk, s2s, s2r)
    rows_in(in_t, t1s, t1r)
    block = jnp.concatenate([in_t[i].astype(F32) for i in range(8)], axis=0).astype(BF16)
    t_blk[k] = jnp.dot(pick_t, block, preferred_element_type=F32).astype(BF16)
    share(t_blk, t2s, t2r)

    to_sibling(s_blk, s2s, s2r, 1)
    to_sibling(s_blk, s2s, s2r, 2)
    t_copy.wait()
    teacher_block(k)
    student_block(slot(1, 0))
    student_block(slot(2, 0))
    relay(t_blk, t2s, t2r)
    sibling(s_blk, s2s, s2r, 1)
    student_block(slot(1, 1))
    sibling(s_blk, s2s, s2r, 2)
    student_block(slot(2, 1))
    to_sibling(s_blk, s2s, s2r, 3)
    student_block(slot(3, 0))
    sibling(t_blk, t2s, t2r, 0)
    teacher_block(slot(0, 1))
    to_sibling(t_blk, t2s, t2r, 1)
    to_sibling(t_blk, t2s, t2r, 2)
    sibling(s_blk, s2s, s2r, 3)
    student_block(slot(3, 1))
    for m in range(1, 8):
        arrived(sq.at[slot(m // 2, m % 2)], us.at[m], ur.at[m], plane(m // 2, m % 2))
    sums = sq[0, 0:1]
    for i in range(1, 8):
        sums = sums + sq[i, 0:1]
    sums = lax.rsqrt(sums / DS + EPSILON)
    inv = jnp.transpose(jnp.broadcast_to(sums, (slots, slots)))[:, 0:1]
    live = weight > 0.0
    teacher_block(slot(1, 0))
    teacher_block(slot(2, 0))
    for vm in (1, 2):
        sibling(t_blk, t2s, t2r, vm)
        teacher_block(slot(vm, 1))
    to_sibling(t_blk, t2s, t2r, 3)
    teacher_block(slot(3, 0))
    sibling(t_blk, t2s, t2r, 3)
    teacher_block(slot(3, 1))

    s_log = s_acc[...] * inv
    t_log = t_acc[...]
    top = jnp.max(s_log, axis=1, keepdims=True)
    top_t = jnp.max(t_log, axis=1, keepdims=True)
    a = s_log - top
    b = t_log - top_t
    e = jnp.exp(a)
    ea = e * a
    d = a - b
    figures = [
        top, jnp.sum(e, axis=1, keepdims=True), top_t, jnp.sum(jnp.exp(b), axis=1, keepdims=True),
        jnp.sum(e * d, axis=1, keepdims=True), jnp.sum(ea, axis=1, keepdims=True),
        jnp.sum(ea * d, axis=1, keepdims=True),
    ]
    lane = lax.broadcasted_iota(jnp.int32, (slots, 128), 1)
    packed = jnp.zeros((slots, 128), F32)
    for i, figure in enumerate(figures):
        packed = jnp.where(lane == i, figure, packed)
    st_a[k] = jnp.transpose(packed)[0:8, :]
    for m in range(1, 8):
        send(st_a.at[k], st_a.at[k], as_.at[m], ar.at[m], plane(m // 2, m % 2))
    for i in range(4):
        hg[i] = jnp.transpose(s_blk[i].astype(F32)).astype(BF16)
    for m in range(1, 8):
        arrived(st_a.at[slot(m // 2, m % 2)], as_.at[m], ar.at[m], plane(m // 2, m % 2))
    st_b[z] = merge([st_a[i] for i in range(8)])
    for m in range(1, 4):
        send(st_b.at[z], st_b.at[z], bs.at[m], br.at[m], column(m, 0))
    for i in range(4, 8):
        hg[i] = jnp.transpose(s_blk[i].astype(F32)).astype(BF16)
    for m in range(1, 4):
        arrived(st_b.at[flip(z, m)], bs.at[m], br.at[m], column(m, 0))
    full = merge([st_b[i] for i in range(4)])
    total = full[1:2]
    lse = full[0:1] + jnp.log(total)
    lse_t = full[2:3] + jnp.log(full[3:4])
    mean_ratio, mean_logit = full[4:5] / total, full[5:6] / total
    divergence = mean_ratio - jnp.log(total) + jnp.log(full[3:4])
    offset = lse - lse_t + divergence
    cov = full[6:7] / total - mean_ratio * mean_logit
    back = jnp.concatenate([lse, offset, divergence, cov, jnp.zeros((slots - 4, slots), F32)], axis=0)
    back = jnp.transpose(back)
    prob = jnp.exp(s_log - back[:, 0:1])
    grad = (weight * inv) * prob * (s_log - t_log - back[:, 1:2])
    g2[...] = jnp.where(live, grad, 0.0).astype(BF16)

    def block_grad(at):
        return lax.dot_general(g2[...], wv[at], (((1,), (1,)), ((), ())), preferred_element_type=F32)

    order = (1, 2, 3, 0)
    part = half_s // 2
    for vm in order:
        p_sib[vm] = block_grad(slot(vm, 1)).astype(BF16)
        send(p_sib.at[vm], r_sib.at[vm], qs.at[vm], qr.at[vm], plane(0, 1))
    for vm in order:
        mine = block_grad(slot(vm, 0))
        arrived(r_sib.at[vm], qs.at[vm], qr.at[vm], plane(0, 1))
        mine = mine + r_sib[vm].astype(F32)
        if vm:
            p_x[vm] = mine.astype(BF16)
            send(p_x.at[vm, :, 0:part], r_x.at[vm, :, 0:part], xs.at[vm], xr.at[vm], plane(vm, 0))
        else:
            own[...] = mine
    for vm in (1, 2, 3):
        send(p_x.at[vm, :, part:], r_x.at[vm, :, part:], xs.at[vm + 4], xr.at[vm + 4], plane(vm, 0))

    loss_ref[...] = jnp.sum(jnp.where(live, weight * back[:, 2:3], 0.0), axis=0, keepdims=True)
    lane = lax.broadcasted_iota(jnp.int32, (slots, 128), 1)
    figure = jnp.where(live, weight * inv * inv * back[:, 3:4] / DS, 0.0)
    hi = figure.astype(BF16).astype(F32)
    mid = (figure - hi).astype(BF16).astype(F32)
    lo = figure - hi - mid
    packed = jnp.where(lane == 0, hi, jnp.where(lane == 1, mid, jnp.where(lane == 2, lo, 0.0))).astype(BF16)
    packed = lax.dot_general(pick_ref[...], packed, (((0,), (0,)), ((), ())), preferred_element_type=F32)
    cols[...] = jnp.broadcast_to(jnp.sum(packed, axis=1, keepdims=True), cols.shape)

    def head_block(i):
        head[i] = jnp.dot(hg[i], g2[...], preferred_element_type=F32).astype(BF16)
        copy = pltpu.make_async_copy(head.at[i], head_hbm.at[i], h_sem.at[i])
        copy.start()
        head_copies.append(copy)

    head_copies = []
    for i in range(4):
        head_block(i)
    for h in range(2):
        at = slice(h * part, (h + 1) * part)
        for vm in (1, 2, 3):
            arrived(r_x.at[vm, :, at], xs.at[vm + 4 * h], xr.at[vm + 4 * h], plane(vm, 0))
        total = own[:, at]
        for vm in (1, 2, 3):
            total = total + r_x[vm, :, at].astype(F32)
        spread_out = lax.dot_general(
            pick_ref[...], total.astype(BF16), (((0,), (0,)), ((), ())), preferred_element_type=F32
        )
        for i in range(8):
            rb[i, :, at] = spread_out[i * rows:(i + 1) * rows].astype(BF16)
        for m in range(1, 8):
            send(
                rb.at[source(m), :, at], rz.at[g, :, at], zs.at[m + 8 * h], zr.at[m + 8 * h],
                column(m // 2, m % 2),
            )
        gp[:, at] = jnp.sum(
            total * raw[:, at], axis=0, keepdims=True
        )
        if h:
            for m in range(1, 8):
                send(gp, gz.at[g], ys.at[m], yr.at[m], column(m // 2, m % 2))
        for i in range(4 + 2 * h, 6 + 2 * h):
            head_block(i)
    rz[g] = rb[g]
    gz[g] = gp[...]
    for h in range(2):
        at = slice(h * part, (h + 1) * part)
        for m in range(1, 8):
            arrived(rz.at[source(m), :, at], zs.at[m + 8 * h], zr.at[m + 8 * h], column(m // 2, m % 2))
    own_cols = cols[pl.ds(pl.multiple_of(g * rows, 8), rows), :][:, 0:1]
    for h in range(2):
        at = slice(h * half_s, (h + 1) * half_s)
        ng = rz[h].astype(F32)
        for i in range(1, 4):
            ng = ng + rz[2 * i + h].astype(F32)
        hid = sh_ref[:, at].astype(F32)
        gh_ref[:, at] = (gain_ref[:, at] * ng - hid * own_cols).astype(BF16)
    for m in range(1, 8):
        arrived(gz.at[source(m)], ys.at[m], yr.at[m], column(m // 2, m % 2))
    for h in range(2):
        at = slice(h * half_s, (h + 1) * half_s)
        ng = gz[h]
        for i in range(1, 4):
            ng = ng + gz[2 * i + h]
        gg_ref[:, at] = ng
    for copy in head_copies:
        copy.wait()
    for copy in sends:
        copy.wait_send()
    for copy in middle_sends:
        pl.when(middle)(copy.wait_send)


def finish(
    head_in, loss_in, hidden_in, gain_in, head_out, loss_out, hidden_out, gain_out,
    head, hidden, gain, loss, in_sem, out_sem,
):
    moves = [(head_in.at[i], head.at[i], head_out.at[i]) for i in range(8)]
    moves += [(hidden_in, hidden, hidden_out), (gain_in, gain, gain_out), (loss_in, loss, loss_out)]
    inward = [pltpu.make_async_copy(a, b, in_sem.at[i]) for i, (a, b, _) in enumerate(moves)]
    outward = [pltpu.make_async_copy(b, c, out_sem.at[i]) for i, (_, b, c) in enumerate(moves)]
    for copy in inward:
        copy.start()
    for first, second in zip(inward, outward):
        first.wait()
        second.start()
    for copy in outward:
        copy.wait()


def fused(
    student_hidden, norm_gain, teacher_hidden, student_head, teacher_head, episode_source, lengths
):
    rows, wide_s = student_hidden.shape
    wide_t = teacher_hidden.shape[1]
    tokens = rows * lax.axis_size("grp")
    voc = student_head.shape[1]
    half_s, half_t = wide_s // 2, wide_t // 2
    slots = -(-(tokens * 5 // 8) // 128) * 128
    vmem = pl.BlockSpec(memory_space=pltpu.VMEM)
    hbm = pl.BlockSpec(memory_space=pltpu.HBM)
    dma = pltpu.SemaphoreType.DMA
    loss, grad_hidden, grad_gain, grad_head = pl.pallas_call(
        kernel,
        out_shape=(
            jax.ShapeDtypeStruct((1, 1), F32),
            jax.ShapeDtypeStruct((rows, wide_s), BF16),
            jax.ShapeDtypeStruct((1, wide_s), F32),
            jax.ShapeDtypeStruct((8, half_s, voc), BF16),
        ),
        in_specs=[hbm] * 7,
        out_specs=(vmem, vmem, vmem, hbm),
        scratch_shapes=[
            pltpu.VMEM((8, half_s, voc), BF16),
            pltpu.VMEM((8, half_t, voc), BF16),
            pltpu.VMEM((rows, wide_s), BF16),
            pltpu.VMEM((1, wide_s), F32),
            pltpu.VMEM((1, episode_source.shape[0]), jnp.int32),
            pltpu.VMEM((1, episode_source.shape[0]), jnp.int32),
            pltpu.VMEM((slots, tokens), BF16),
            pltpu.VMEM((8, rows, half_s), BF16),
            pltpu.VMEM((8, rows, half_t), BF16),
            pltpu.VMEM((8, slots, half_s), BF16),
            pltpu.VMEM((8, slots, half_t), BF16),
            pltpu.VMEM((8, half_s, slots), BF16),
            pltpu.VMEM((slots, voc), F32),
            pltpu.VMEM((slots, voc), F32),
            pltpu.VMEM((slots, half_s), F32),
            pltpu.VMEM((8, 8, slots), F32),
            pltpu.VMEM((tokens, 128), F32),
            pltpu.VMEM((8, 8, slots), F32),
            pltpu.VMEM((4, 8, slots), F32),
            pltpu.VMEM((slots, voc), BF16),
            pltpu.VMEM((slots, half_s), F32),
            pltpu.VMEM((4, slots, half_s), BF16),
            pltpu.VMEM((4, slots, half_s), BF16),
            pltpu.VMEM((4, slots, half_s), BF16),
            pltpu.VMEM((4, slots, half_s), BF16),
            pltpu.VMEM((8, rows, half_s), BF16),
            pltpu.VMEM((8, rows, half_s), BF16),
            pltpu.VMEM((1, half_s), F32),
            pltpu.VMEM((8, 1, half_s), F32),
            pltpu.VMEM((8, half_s, voc), BF16),
            dma(()), dma(()), dma((8,)), dma((8,)),
        ] + [dma((16,))] * 8 + [dma((8,))] * 8 + [dma((16,))] * 2 + [dma((8,))] * 4,
        compiler_params=pltpu.CompilerParams(
            collective_id=0, has_side_effects=True, vmem_limit_bytes=LIMIT * 1024
        ),
        cost_estimate=pl.CostEstimate(flops=2600000000, bytes_accessed=11000000, transcendentals=400000),
    )(
        student_hidden, teacher_hidden, norm_gain.reshape(1, -1),
        episode_source.reshape(1, -1), lengths.reshape(1, -1),
        student_head.reshape(8, half_s, voc), teacher_head.reshape(8, half_t, voc),
    )
    results = (grad_head, loss, grad_hidden, grad_gain)
    grad_head, loss, grad_hidden, grad_gain = pl.pallas_call(
        finish,
        out_shape=tuple(jax.ShapeDtypeStruct(r.shape, r.dtype) for r in results),
        in_specs=[hbm] * 4,
        out_specs=(hbm,) * 4,
        scratch_shapes=[
            pltpu.VMEM((8, half_s, voc), BF16),
            pltpu.VMEM((rows, wide_s), BF16),
            pltpu.VMEM((1, wide_s), F32),
            pltpu.VMEM((1, 1), F32),
            dma((11,)), dma((11,)),
        ],
        compiler_params=pltpu.CompilerParams(vmem_limit_bytes=LIMIT * 1024),
        cost_estimate=pl.CostEstimate(flops=0, bytes_accessed=6400000, transcendentals=0),
    )(*results)
    return (loss[0, 0], grad_hidden, grad_gain.reshape(-1), grad_head.reshape(student_head.shape))


def realign(teacher_hidden, table, group_index, per_group):
    groups = table.shape[0]
    source_group = table // per_group
    source_local = table % per_group
    mine = (source_group == group_index).astype(jnp.int32)
    earlier = jnp.cumsum(mine, axis=1) - mine
    slot_ids = jnp.arange(MOST, dtype=jnp.int32)
    matches = mine[:, :, None] * (earlier[:, :, None] == slot_ids[None, None, :]).astype(jnp.int32)
    send_index = jnp.sum(matches * source_local[:, :, None], axis=1)
    features = teacher_hidden.shape[1]
    episodes = teacher_hidden.reshape(per_group, SEQ, features)
    outgoing = jnp.take(episodes, send_index, axis=0)
    incoming = lax.all_to_all(outgoing, "grp", split_axis=0, concat_axis=0, tiled=True)
    own_groups = lax.dynamic_index_in_dim(source_group, group_index, 0, keepdims=False)
    matching = (own_groups[:, None] == own_groups[None, :]).astype(jnp.int32)
    position = jnp.sum(jnp.tril(matching, -1), axis=1)
    flat_index = own_groups * MOST + position
    received = incoming.reshape(groups * MOST, SEQ, features)
    return jnp.take(received, flat_index, axis=0).reshape(per_group * SEQ, features)


def local(
    student_hidden, norm_gain, teacher_hidden, student_head, teacher_head, episode_source, lengths
):
    groups = lax.axis_size("grp")
    group_index = lax.axis_index("grp")
    rows_group = student_hidden.shape[0]
    per_group = rows_group // SEQ
    hidden_f32 = student_hidden.astype(jnp.float32)
    squares = lax.psum(jnp.sum(hidden_f32 * hidden_f32, axis=1), "voc")
    inverse_rms = lax.rsqrt(squares / DS + EPSILON)
    normed = (hidden_f32 * inverse_rms[:, None] * norm_gain[None, :]).astype(jnp.bfloat16)
    table = episode_source.reshape(groups, per_group)
    aligned = realign(teacher_hidden, table, group_index, per_group)
    teacher_rows, student_rows = (
        lax.all_gather(aligned, "voc", axis=1, tiled=True),
        lax.all_gather(normed, "voc", axis=1, tiled=True),
    )
    teacher_logits = jnp.dot(
        lax.all_gather(teacher_rows, "grp", axis=0, tiled=True),
        teacher_head,
        preferred_element_type=jnp.float32,
    )
    positions = jnp.arange(SEQ, dtype=jnp.int32)
    all_rows = lax.all_gather(student_rows, "grp", axis=0, tiled=True)
    student_logits = jnp.dot(all_rows, student_head, preferred_element_type=jnp.float32)
    lengths_f32 = lengths.astype(jnp.float32)
    valid = positions[None, :] < lengths[:, None]
    token_weight = jnp.where(
        valid, 1.0 / lengths_f32[:, None], jnp.zeros_like(lengths_f32)[:, None]
    ).reshape(-1)
    top_student, top_teacher = lax.pmax(
        (jnp.max(student_logits, axis=1), jnp.max(teacher_logits, axis=1)), ("grp", "voc")
    )
    exp_student = jnp.exp(student_logits - top_student[:, None])
    exp_teacher = jnp.exp(teacher_logits - top_teacher[:, None])
    total_student, total_teacher = lax.psum(
        (jnp.sum(exp_student, axis=1), jnp.sum(exp_teacher, axis=1)), ("grp", "voc")
    )
    log_student = student_logits - (top_student + jnp.log(total_student))[:, None]
    log_teacher = teacher_logits - (top_teacher + jnp.log(total_teacher))[:, None]
    prob_student = jnp.exp(log_student)
    log_ratio = log_student - log_teacher
    divergence = lax.psum(jnp.sum(prob_student * log_ratio, axis=1), ("grp", "voc"))
    loss = jnp.sum(token_weight * divergence)
    logit_grad = (token_weight[:, None] * prob_student * (log_ratio - divergence[:, None])).astype(
        jnp.bfloat16
    )
    grad_head = lax.dot_general(
        all_rows, logit_grad, (((0,), (0,)), ((), ())), preferred_element_type=jnp.float32
    ).astype(jnp.bfloat16)
    full_term = lax.dot_general(
        logit_grad, student_head, (((1,), (1,)), ((), ())), preferred_element_type=jnp.float32
    )
    feature_part = lax.psum_scatter(
        full_term.astype(jnp.bfloat16), "voc", scatter_dimension=1, tiled=True
    )
    normed_grad = lax.psum_scatter(feature_part, "grp", scatter_dimension=0, tiled=True).astype(
        jnp.float32
    )
    scaled = normed_grad * norm_gain[None, :]
    inner = lax.psum(jnp.sum(scaled * hidden_f32, axis=1), "voc")
    grad_hidden = (
        inverse_rms[:, None] * scaled - hidden_f32 * (inverse_rms**3)[:, None] * inner[:, None] / DS
    )
    grad_gain = lax.psum(jnp.sum(normed_grad * hidden_f32 * inverse_rms[:, None], axis=0), "grp")
    return (loss, grad_hidden.astype(jnp.bfloat16), grad_gain, grad_head)


def solution(mesh):
    placed = (
        P("grp", "voc"),
        P("voc"),
        P("grp", "voc"),
        P(None, ("grp", "voc")),
        P(None, ("grp", "voc")),
        P(),
        P(),
    )
    body = fused if tuple(mesh.shape.values()) == (8, 4) else local
    return jax.shard_map(
        body,
        mesh=mesh,
        in_specs=placed,
        out_specs=(P(), P("grp", "voc"), P("voc"), P(None, ("grp", "voc"))),
        check_vma=False,
    )
```
